32 devices in a mesh: seq: 4 (over y, core), rows: 8 (over z, x).
Axes of the slice: x: 2, y: 2, z: 4, core: 2. Of those that a mesh axis runs over, the one named last changes fastest.
Arguments:
- tokens: bfloat16 [64, 512, 768], P('rows', 'seq'), may hold values from -6 to 6
- query_weight: bfloat16 [768, 768], replicated, may hold values from -0.21875 to 0.21875
- query_bias: bfloat16 [768], replicated, may hold values from -1.5 to 1.5
- key_weight: bfloat16 [768, 768], replicated, may hold values from -0.21875 to 0.21875
- value_weight: bfloat16 [768, 768], replicated, may hold values from -0.21875 to 0.21875
- value_bias: bfloat16 [768], replicated, may hold values from -1.5 to 1.5
- output_weight: bfloat16 [768, 768], replicated, may hold values from -1.75 to 1.75
- output_bias: bfloat16 [768], replicated, may hold values from -1.5 to 1.5
- attn_gain: bfloat16 [768], replicated, may hold values from 0.5 to 1.5
- attn_shift: bfloat16 [768], replicated, may hold values from -0.5 to 0.5
- inner_weight: bfloat16 [768, 3072], replicated, may hold values from -0.21875 to 0.21875
- inner_bias: bfloat16 [3072], replicated, may hold values from -1.5 to 1.5
- outer_weight: bfloat16 [3072, 768], replicated, may hold values from -0.109375 to 0.109375
- outer_bias: bfloat16 [768], replicated, may hold values from -1.5 to 1.5
- ffn_gain: bfloat16 [768], replicated, may hold values from 0.5 to 1.5
- ffn_shift: bfloat16 [768], replicated, may hold values from -0.5 to 0.5
- segment_ids: int32 [64, 512], P('rows'), may hold values from 0 to 7, as said below
- positives: int32 [512], P('rows'), may hold values from 0 to 511, as said below
Outputs:
- loss_mean: float32 [], replicated
- grad_tokens: float32 [64, 512, 768], P('rows', 'seq')
- grad_query_weight: float32 [768, 768], replicated
- grad_query_bias: float32 [768], replicated
- grad_key_weight: float32 [768, 768], replicated
- grad_value_weight: float32 [768, 768], replicated
- grad_value_bias: float32 [768], replicated
- grad_output_weight: float32 [768, 768], replicated
- grad_output_bias: float32 [768], replicated
- grad_attn_gain: float32 [768], replicated
- grad_attn_shift: float32 [768], replicated
- grad_inner_weight: float32 [768, 3072], replicated
- grad_inner_bias: float32 [3072], replicated
- grad_outer_weight: float32 [3072, 768], replicated
- outer_bias_gradient: float32 [768], replicated
- grad_ffn_gain: float32 [768], replicated
- grad_ffn_shift: float32 [768], replicated
The draws below stay inside these ranges and needn't reach their ends.
Inputs may be any that keep to these rules, and one draw needn't show every extreme that they name: `segment_ids`: in each row the ids never fall, every id of 0 to 7 occurs, and one segment covers 512 - 127 positions or more. positives[i] differs from i.
All inputs are finite; a program needn't handle non-finite values.
Results may differ from the reference program's by a relative error of at most 0.012.
Values may be sent and summed in bfloat16 or wider, within the bound.
A program may use at most 256 MiB of HBM per device.

```python
import jax
import jax.numpy as jnp
from jax import lax

D = 768
HEADS = 12
HEAD_DIM = 64
FF = 3072
LENGTH = 512
SEG_ROW = 8
ROWS_GRP = 8
POS_DEV = 128
ROWS = 64
SEGS = 512
N_ROWS = 8


def draw_segment_ids(key, part):
    key = jax.random.fold_in(key, 11)
    pick_key, length_key = jax.random.split(key)
    short_most = (POS_DEV - 1) // (SEG_ROW - 1)
    long_pick = jax.random.randint(pick_key, (ROWS, 1), 0, SEG_ROW)
    shorts = jax.random.randint(length_key, (ROWS, SEG_ROW), 1, short_most + 1)
    is_long = jnp.arange(SEG_ROW)[None, :] == long_pick
    shorts = jnp.where(is_long, 0, shorts)
    long_len = LENGTH - jnp.sum(shorts, axis=1, keepdims=True)
    lengths = jnp.where(is_long, long_len, shorts)
    bounds = jnp.cumsum(lengths, axis=1)[:, :-1]
    places = jnp.arange(LENGTH)
    return jnp.sum(places[None, :, None] >= bounds[:, None, :], axis=2).astype(jnp.int32)


def draw_positives(key, part):
    key = jax.random.fold_in(key, 12)
    offsets_drawn = jax.random.randint(key, (SEGS,), 1, SEGS)
    indices = jnp.arange(SEGS)
    offsets_drawn = jnp.where(indices < 2, SEGS - 1, offsets_drawn)
    return ((indices + offsets_drawn) % SEGS).astype(jnp.int32)


def level_of(own_key, dims, cuts, smallest, largest):
    loudness = 1.0
    for dim, blocks in cuts:
        draws = jax.random.uniform(jax.random.fold_in(jax.random.fold_in(own_key, 6), dim), (blocks,), jnp.float32, smallest / len(cuts), largest / len(cuts))
        loudness = loudness * jnp.repeat(jnp.exp(draws), dims[dim] // blocks).reshape((-1,) + (1,) * (len(dims) - 1 - dim))
    return loudness


def noise(own_key, dims, scale, most, cuts=(), held_as=jnp.bfloat16):
    loudness = level_of(own_key, dims, cuts, -0.22, 0.18) if cuts else 1.0
    drawn = jax.random.normal(own_key, dims, jnp.float32) * scale * loudness
    return jnp.minimum(jnp.maximum(drawn, -most), most).astype(held_as)


def setup_inputs(seed: int = 0) -> dict:
    seeds = jax.random.split(jax.random.key(seed), 19)
    return {
        "tokens": noise(seeds[0], (ROWS, LENGTH, D), 1.0, 6.0, ((0, 8), (1, 4))),
        "query_weight": noise(seeds[1], (D, D), D ** -0.5, 0.21875),
        "query_bias": noise(seeds[2], (D,), 0.3, 1.5),
        "key_weight": noise(seeds[3], (D, D), D ** -0.5, 0.21875),
        "value_weight": noise(seeds[4], (D, D), D ** -0.5, 0.21875),
        "value_bias": noise(seeds[5], (D,), 0.3, 1.5),
        "output_weight": noise(seeds[6], (D, D), (D // 64) ** -0.5, 1.75),
        "output_bias": noise(seeds[7], (D,), 0.3, 1.5),
        "attn_gain": jnp.clip(1.0 + 0.1 * jax.random.normal(seeds[8], (D,), jnp.float32), 0.5, 1.5).astype(jnp.bfloat16),
        "attn_shift": noise(seeds[9], (D,), 0.1, 0.5),
        "inner_weight": noise(seeds[10], (D, FF), D ** -0.5, 0.21875),
        "inner_bias": noise(seeds[11], (FF,), 0.3, 1.5),
        "outer_weight": noise(seeds[12], (FF, D), FF ** -0.5, 0.109375),
        "outer_bias": noise(seeds[13], (D,), 0.3, 1.5),
        "ffn_gain": jnp.clip(1.0 + 0.1 * jax.random.normal(seeds[14], (D,), jnp.float32), 0.5, 1.5).astype(jnp.bfloat16),
        "ffn_shift": noise(seeds[15], (D,), 0.1, 0.5),
        "segment_ids": draw_segment_ids(jax.random.fold_in(seeds[18], 71), 0),
        "positives": draw_positives(jax.random.fold_in(seeds[18], 71), 0),
    }


@jax.custom_vjp
def low(v):
    return lax.optimization_barrier(v.astype(jnp.bfloat16)).astype(jnp.float32)

@jax.custom_vjp
def low_back(v):
    return v

def low_keep(v):
    return (low(v), None)

def low_pass(kept, grad):
    return (grad,)

def back_keep(v):
    return (v, None)

def back_low(kept, grad):
    return (low(grad),)
low.defvjp(low_keep, low_pass)
low_back.defvjp(back_keep, back_low)
maximal_accuracy_mode = lax.Precision.HIGHEST
norm_eps = 1e-12
pool_eps = 1e-06
softmax_temper = 0.01
masked_score = -1000000000.0

def layer_norm(resid, gain, shift):
    center = resid - lax.optimization_barrier(jnp.mean(resid, axis=-1, keepdims=True))
    spread = lax.optimization_barrier(jnp.mean(center * center, axis=-1, keepdims=True))
    return center * lax.rsqrt(spread + norm_eps) * gain + shift

def softmax_rows(similarity_logits):
    top = lax.optimization_barrier(jnp.max(similarity_logits, axis=-1, keepdims=True))
    expo = jnp.exp(similarity_logits - top)
    return expo / lax.optimization_barrier(jnp.sum(expo, axis=-1, keepdims=True))

def contrast_terms(pooled, query_rows, query_start, positives_part):
    normalized_rows = pooled * lax.rsqrt(lax.optimization_barrier(jnp.sum(pooled * pooled, axis=1, keepdims=True)) + pool_eps)
    start = jnp.asarray(query_start).astype(jnp.int32)
    selected_entries = lax.dynamic_slice_in_dim(normalized_rows, start, query_rows, 0)
    similarity_logits = jnp.dot(selected_entries, normalized_rows.T, precision=maximal_accuracy_mode) / softmax_temper
    row_index = jnp.arange(query_rows, dtype=jnp.int32) + start
    column_index = jnp.arange(pooled.shape[0], dtype=jnp.int32)
    similarity_logits = jnp.where(column_index[None, :] == row_index[:, None], masked_score, similarity_logits)
    top = lax.optimization_barrier(jnp.max(similarity_logits, axis=1, keepdims=True))
    spread_log = jnp.log(lax.optimization_barrier(jnp.sum(jnp.exp(similarity_logits - top), axis=1))) + top[:, 0]
    picked = lax.optimization_barrier(jnp.sum(jnp.where(column_index[None, :] == positives_part[:, None], similarity_logits, 0.0), axis=1))
    return jnp.sum(spread_log - picked)

def matmul_high(left, right):
    return jnp.dot(left, right, precision=maximal_accuracy_mode)

def attend_block(operands):
    queries, key_rows, value_rows, block_ids = operands
    raw = jnp.einsum('bqhd,bkhd->bhqk', queries, key_rows, precision=maximal_accuracy_mode) * HEAD_DIM ** (-0.5)
    same = block_ids[:, None, :, None] == block_ids[:, None, None, :]
    similarity_logits = low_back(jnp.where(same, raw, masked_score))
    probs = softmax_rows(similarity_logits)
    return jnp.einsum('bhqk,bkhd->bqhd', low(probs), value_rows, precision=maximal_accuracy_mode)

def forward(params, tokens_float, segment_ids, positives):
    query_weight, query_bias, key_weight, value_weight, value_bias, output_weight, output_bias, attn_gain, attn_shift, inner_weight, inner_bias, outer_weight, outer_bias, ffn_gain, ffn_shift = params
    flat = tokens_float.reshape(ROWS * LENGTH, D)
    queries = low_back(low(matmul_high(flat, query_weight) + query_bias))
    key_rows = low_back(low(matmul_high(flat, key_weight)))
    value_rows = low_back(low(matmul_high(flat, value_weight) + value_bias))
    block_shape = (N_ROWS, ROWS_GRP, LENGTH, HEADS, HEAD_DIM)
    mixed = lax.map(jax.checkpoint(attend_block), (queries.reshape(block_shape), key_rows.reshape(block_shape), value_rows.reshape(block_shape), segment_ids.reshape(N_ROWS, ROWS_GRP, LENGTH)))
    heads_out = low_back(low(mixed.reshape(ROWS * LENGTH, D)))
    attn_out = low_back(matmul_high(heads_out, output_weight) + output_bias)
    hidden = layer_norm(flat + attn_out, attn_gain, attn_shift)
    inner = low_back(matmul_high(low(hidden), inner_weight) + inner_bias)
    active = low(jax.nn.gelu(inner, approximate=False))
    outer = low_back(matmul_high(active, outer_weight) + outer_bias)
    output = layer_norm(hidden + outer, ffn_gain, ffn_shift).reshape(ROWS, LENGTH, D)
    onehot = (segment_ids[:, :, None] == jnp.arange(SEG_ROW, dtype=jnp.int32)[None, None, :]).astype(jnp.float32)
    seg_sums = jnp.einsum('rls,rld->rsd', onehot, output, precision=maximal_accuracy_mode)
    counts = lax.optimization_barrier(jnp.sum(onehot, axis=1))[:, :, None]
    pooled = (seg_sums / counts).reshape(SEGS, D)
    return contrast_terms(pooled, SEGS, 0, positives)

def reference(tokens, query_weight, query_bias, key_weight, value_weight, value_bias, output_weight, output_bias, attn_gain, attn_shift, inner_weight, inner_bias, outer_weight, outer_bias, ffn_gain, ffn_shift, segment_ids, positives):
    weights = (query_weight, query_bias, key_weight, value_weight, value_bias, output_weight, output_bias, attn_gain, attn_shift, inner_weight, inner_bias, outer_weight, outer_bias, ffn_gain, ffn_shift)
    params = tuple((item.astype(jnp.float32) for item in weights))
    tokens_float = tokens.astype(jnp.float32)

    def objective(params_in, tokens_in):
        return forward(params_in, tokens_in, segment_ids, positives)
    total, pull = jax.vjp(objective, params, tokens_float)
    grad_params, grad_tokens = pull(jnp.ones_like(total))
    g_query_w, g_query_b, g_key_w, g_value_w, g_value_b, g_output_w, g_output_b, g_attn_gain, g_attn_shift, g_inner_w, g_inner_b, g_outer_w, g_outer_b, g_ffn_gain, g_ffn_shift = grad_params
    return (total / SEGS, grad_tokens, g_query_w, g_query_b, g_key_w, g_value_w, g_value_b, g_output_w, g_output_b, g_attn_gain, g_attn_shift, g_inner_w, g_inner_b, g_outer_w, g_outer_b, g_ffn_gain, g_ffn_shift)
```

```python
import jax
import jax.numpy as jnp
from jax import lax
from jax.sharding import PartitionSpec as P

HEADS = 12
SEG_ROW = 8
HIGHEST = lax.Precision.HIGHEST
NORM_EPS = 1e-12
POOL_EPS = 1e-06
INV_TEMPER = 100.0
MASKED = -1000000000.0
INV_ROOT_TWO_PI = 0.3989422804014327
INV_ROOT_TWO = 0.7071067811865476
BF = jnp.bfloat16
F32 = jnp.float32


def exchange(array, partner):
    seqs, rows = lax.axis_size("seq"), lax.axis_size("rows")
    pairs = []
    for s in range(seqs):
        for r in range(rows):
            to_s, to_r = partner(s, r)
            pairs.append((s * rows + r, to_s * rows + to_r))
    return lax.ppermute(array, ("seq", "rows"), pairs)


def halving_steps():
    seq, row = lax.axis_index("seq"), lax.axis_index("rows")
    core = seq % 2
    seq_bit, row_bit = seq // 2 % 2, row % 2

    def first(s, r):
        return (s, r ^ 1) if s % 2 == 0 else (s ^ 2, r)

    def second(s, r):
        return (s ^ 2, r) if s % 2 == 0 else (s, r ^ 1)

    steps = [
        (lambda s, r: (s ^ 1, r), core),
        (first, jnp.where(core == 0, row_bit, seq_bit)),
        (second, jnp.where(core == 0, seq_bit, row_bit)),
    ]
    step = 2
    while step < lax.axis_size("rows"):
        steps.append((lambda s, r, step=step: (s, r ^ step), row // step % 2))
        step *= 2
    return steps


def half(array, bit):
    size = array.shape[0] // 2
    return lax.dynamic_slice_in_dim(array, bit * size, size, 0)


def reduce_scatter(array):
    for partner, bit in halving_steps():
        sent = half(array, 1 - bit)
        came = exchange(sent, partner)
        array = (half(array, bit).astype(F32) + came.astype(F32)).astype(BF)
    return array


def all_gather(array):
    for partner, bit in reversed(halving_steps()):
        came = exchange(array, partner)
        array = jnp.where(
            bit == 0,
            jnp.concatenate([array, came], axis=0),
            jnp.concatenate([came, array], axis=0),
        )
    return array


def all_sum_small(array):
    for partner, _ in halving_steps():
        array = array + exchange(array, partner)
    return array


def gather_embeddings(own):
    return lax.all_gather(own, ("rows", "seq"), axis=0, tiled=True)


def layer_norm(resid, gain, shift):
    center = resid - jnp.mean(resid, axis=-1, keepdims=True)
    spread = jnp.mean(center * center, axis=-1, keepdims=True)
    scale = lax.rsqrt(spread + NORM_EPS)
    xhat = center * scale
    return xhat * gain + shift, xhat, scale


def norm_back(grad, gain, xhat, scale):
    q = grad * gain
    return scale * (
        q - jnp.mean(q, axis=-1, keepdims=True) - xhat * jnp.mean(q * xhat, axis=-1, keepdims=True)
    )


def dot(a, b):
    return jnp.dot(a, b, preferred_element_type=F32)


def dot_t(a, b):
    return lax.dot_general(a, b, (((1,), (1,)), ((), ())), preferred_element_type=F32)


def t_dot(a, b):
    return lax.dot_general(a, b, (((0,), (0,)), ((), ())), preferred_element_type=F32)


def contrast(pooled, own_pooled, own_start, positives_all, own_positives):
    def normalized(e):
        rho = lax.rsqrt(jnp.sum(e * e, axis=1, keepdims=True) + POOL_EPS)
        return e * rho, rho

    n_all, _ = normalized(pooled)
    n_own, rho = normalized(own_pooled)
    total, own = pooled.shape[0], own_pooled.shape[0]
    col = jnp.arange(total, dtype=jnp.int32)
    row_own = jnp.arange(own, dtype=jnp.int32) + own_start
    c_all = jnp.dot(n_all, n_all.T, precision=HIGHEST) * INV_TEMPER
    c_all = jnp.where(col[None, :] == col[:, None], MASKED, c_all)
    top = jnp.max(c_all, axis=1)
    lse = jnp.log(jnp.sum(jnp.exp(c_all - top[:, None]), axis=1)) + top
    c_own = lax.dynamic_slice_in_dim(c_all, own_start, own, 0)
    lse_own = lax.dynamic_slice_in_dim(lse, own_start, own, 0)
    chosen = col[None, :] == own_positives[:, None]
    loss = jnp.sum(lse_own - jnp.sum(jnp.where(chosen, c_own, 0.0), axis=1))
    weight = (
        jnp.exp(c_own - lse_own[:, None])
        + jnp.exp(c_own - lse[None, :])
        - chosen.astype(F32)
        - (positives_all[None, :] == row_own[:, None]).astype(F32)
    )
    d_n = INV_TEMPER * jnp.dot(weight, n_all, precision=HIGHEST)
    d_e = rho * d_n - rho**3 * own_pooled * jnp.sum(own_pooled * d_n, axis=1, keepdims=True)
    return loss, d_e


def local(
    tokens,
    query_weight,
    query_bias,
    key_weight,
    value_weight,
    value_bias,
    output_weight,
    output_bias,
    attn_gain,
    attn_shift,
    inner_weight,
    inner_bias,
    outer_weight,
    outer_bias,
    ffn_gain,
    ffn_shift,
    segment_ids,
    positives,
):
    group_rows, local_len, width = tokens.shape
    ff = inner_weight.shape[1]
    seqs = lax.axis_size("seq")
    seq, row_place = lax.axis_index("seq"), lax.axis_index("rows")
    head_dim = width // HEADS
    scale = head_dim ** (-0.5)
    batch, length = group_rows // seqs, local_len * seqs
    count = batch * length
    ids = lax.dynamic_slice_in_dim(segment_ids, seq * batch, batch, 0)
    own_segs = batch * SEG_ROW
    own_positives = lax.dynamic_slice_in_dim(positives, seq * own_segs, own_segs, 0)
    positives_all = lax.all_gather(positives, "rows", axis=0, tiled=True)
    own_start = row_place * positives.shape[0] + seq * own_segs

    flat = lax.all_to_all(tokens, "seq", split_axis=0, concat_axis=1, tiled=True)
    flat = flat.reshape(count, width)
    f = lambda v: v.astype(F32)
    q = (dot(flat, query_weight) + f(query_bias)).astype(BF)
    k = dot(flat, key_weight).astype(BF)
    v = (dot(flat, value_weight) + f(value_bias)).astype(BF)
    heads = lambda a: a.reshape(batch, length, HEADS, head_dim)
    q4, k4, v4 = heads(q), heads(k), heads(v)
    raw = jnp.einsum("bqhd,bkhd->bhqk", q4, k4, preferred_element_type=F32) * scale
    same = ids[:, None, :, None] == ids[:, None, None, :]
    raw = jnp.where(same, raw, MASKED)
    expo = jnp.exp(raw - jnp.max(raw, axis=-1, keepdims=True))
    probs = expo / jnp.sum(expo, axis=-1, keepdims=True)
    probs_low = probs.astype(BF)
    o = jnp.einsum("bhqk,bkhd->bqhd", probs_low, v4, preferred_element_type=F32)
    o = o.astype(BF).reshape(count, width)
    resid_one = f(flat) + dot(o, output_weight) + f(output_bias)
    hidden, xhat_one, scale_one = layer_norm(resid_one, f(attn_gain), f(attn_shift))
    hidden_low = hidden.astype(BF)
    inner = dot(hidden_low, inner_weight) + f(inner_bias)
    cdf = 0.5 * (1.0 + lax.erf(inner * INV_ROOT_TWO))
    active = (inner * cdf).astype(BF)
    slope = (cdf + inner * jnp.exp(-0.5 * inner * inner) * INV_ROOT_TWO_PI).astype(BF)
    resid_two = hidden + dot(active, outer_weight) + f(outer_bias)
    _, xhat_two, scale_two = layer_norm(resid_two, f(ffn_gain), f(ffn_shift))
    onehot = (ids[:, :, None] == jnp.arange(SEG_ROW, dtype=jnp.int32)).astype(F32)
    counts = jnp.sum(onehot, axis=1).reshape(own_segs, 1)
    pooled_xhat = (
        jnp.einsum("bls,bld->bsd", onehot, xhat_two.reshape(batch, length, width), precision=HIGHEST)
        .reshape(own_segs, width) / counts
    )
    own_pooled = pooled_xhat * f(ffn_gain) + f(ffn_shift)
    pooled = gather_embeddings(own_pooled)
    loss, d_e = contrast(pooled, own_pooled, own_start, positives_all, own_positives)

    g_ffn_gain = jnp.sum(d_e * pooled_xhat, axis=0)
    g_ffn_shift = jnp.sum(d_e, axis=0)
    d_y = jnp.einsum(
        "bls,bsd->bld", onehot, (d_e / counts).reshape(batch, SEG_ROW, width), precision=HIGHEST
    ).reshape(count, width)
    d_two = norm_back(d_y, f(ffn_gain), xhat_two, scale_two)
    d_outer = d_two.astype(BF)
    g_outer = t_dot(active, d_outer).astype(BF)
    part_outer = reduce_scatter(g_outer)
    d_inner = (dot_t(d_outer, outer_weight) * f(slope)).astype(BF)
    g_inner = jnp.concatenate(
        [t_dot(hidden_low, d_inner[:, i * width : (i + 1) * width]) for i in range(ff // width)], axis=0
    ).astype(BF)
    part_inner = reduce_scatter(g_inner)
    d_hidden = d_two + dot_t(d_inner, inner_weight)
    d_one = norm_back(d_hidden, f(attn_gain), xhat_one, scale_one)
    d_attn = d_one.astype(BF)
    g_output = t_dot(o, d_attn)
    d_o = dot_t(d_attn, output_weight).astype(BF)
    d_o4 = heads(d_o)
    d_probs = jnp.einsum("bqhd,bkhd->bhqk", d_o4, v4, preferred_element_type=F32)
    d_v = jnp.einsum("bhqk,bqhd->bkhd", probs_low, d_o4, preferred_element_type=F32)
    d_s = (probs * (d_probs - jnp.sum(d_probs * probs, axis=-1, keepdims=True))).astype(BF)
    d_q = jnp.einsum("bhqk,bkhd->bqhd", d_s, k4, preferred_element_type=F32) * scale
    d_k = jnp.einsum("bhqk,bqhd->bkhd", d_s, q4, preferred_element_type=F32) * scale
    d_q, d_k, d_v = (a.astype(BF).reshape(count, width) for a in (d_q, d_k, d_v))
    g_attn = jnp.concatenate(
        [t_dot(flat, d_q), t_dot(flat, d_k), t_dot(flat, d_v), g_output], axis=0
    ).astype(BF)
    part_attn = reduce_scatter(g_attn)
    column = lambda a: jnp.sum(f(a), axis=0)
    small = jnp.concatenate(
        [
            column(d_q), column(d_v), column(d_attn),
            jnp.sum(d_hidden * xhat_one, axis=0), jnp.sum(d_hidden, axis=0),
            column(d_inner), column(d_outer), g_ffn_gain, g_ffn_shift,
            jnp.broadcast_to(loss, (width,)),
        ]
    ).reshape(-1, 128)
    small = all_sum_small(small).reshape(-1)
    token_grad = (
        d_one + dot_t(d_q, query_weight) + dot_t(d_k, key_weight) + dot_t(d_v, value_weight)
    ).astype(BF)
    grad_tokens = lax.all_to_all(
        token_grad.reshape(batch, length, width), "seq", split_axis=1, concat_axis=0, tiled=True
    ).astype(F32)
    sum_outer = all_gather(part_outer).astype(F32)
    sum_inner = all_gather(part_inner).astype(F32)
    sum_inner = jnp.concatenate(
        [sum_inner[i * width : (i + 1) * width] for i in range(ff // width)], axis=1
    )
    sum_attn = all_gather(part_attn).astype(F32)
    sizes = [width] * 5 + [ff] + [width] * 4
    pieces, at = [], 0
    for size in sizes:
        pieces.append(small[at : at + size])
        at += size
    qb, vb, ob, ag, ash, ib, wb, fg, fs, ls = pieces
    return (
        ls[0] / pooled.shape[0],
        grad_tokens,
        sum_attn[:width],
        qb,
        sum_attn[width : 2 * width],
        sum_attn[2 * width : 3 * width],
        vb,
        sum_attn[3 * width :],
        ob,
        ag,
        ash,
        sum_inner,
        ib,
        sum_outer,
        wb,
        fg,
        fs,
    )


def solution(mesh):
    placed = (
        (P("rows", "seq", None),) + (P(),) * 15 + (P("rows", None), P("rows"))
    )
    return jax.shard_map(
        local,
        mesh=mesh,
        in_specs=placed,
        out_specs=(P(), P("rows", "seq", None)) + (P(),) * 15,
        check_vma=False,
    )
```

```python
import functools

import jax
import jax.numpy as jnp
from jax import lax
from jax.experimental import pallas as pl
from jax.experimental.pallas import tpu as pltpu
from jax.sharding import PartitionSpec as P

HEADS = 12
SEG_ROW = 8
HIGHEST = lax.Precision.HIGHEST
NORM_EPS = 1e-12
POOL_EPS = 1e-06
INV_TEMPER = 100.0
MASKED = -1000000000.0
INV_ROOT_TWO_PI = 0.3989422804014327
INV_ROOT_TWO = 0.7071067811865476
BF = jnp.bfloat16
F32 = jnp.float32
MESH = pl.DeviceIdType.MESH


def dot(a, b):
    return jnp.dot(a, b, preferred_element_type=F32)


def dot_t(a, b, precision=None):
    return lax.dot_general(
        a, b, (((1,), (1,)), ((), ())), preferred_element_type=F32, precision=precision
    )


def t_dot(a, b):
    return lax.dot_general(a, b, (((0,), (0,)), ((), ())), preferred_element_type=F32)


def normalize(resid):
    center = resid - jnp.mean(resid, axis=-1, keepdims=True)
    spread = jnp.mean(center * center, axis=-1, keepdims=True)
    scale = lax.rsqrt(spread + NORM_EPS)
    return center * scale, scale


def norm_back(grad, gain, xhat, scale):
    q = grad * gain
    return scale * (
        q - jnp.mean(q, axis=-1, keepdims=True) - xhat * jnp.mean(q * xhat, axis=-1, keepdims=True)
    )


def split3(a):
    hi = a.astype(BF)
    rest = a - hi.astype(F32)
    mid = rest.astype(BF)
    return hi, mid, (rest - mid.astype(F32)).astype(BF)


def call(kernel, grid, in_specs, out_specs, out_shape, scratch, flops, moved, vmem=48):
    return pl.pallas_call(
        kernel,
        grid=grid,
        in_specs=in_specs,
        out_specs=out_specs,
        out_shape=out_shape,
        scratch_shapes=scratch,
        cost_estimate=pl.CostEstimate(flops=flops, bytes_accessed=moved, transcendentals=0),
        compiler_params=pltpu.CompilerParams(vmem_limit_bytes=vmem << 20),
    )


def shape_of(dims, dtype):
    return jax.ShapeDtypeStruct(dims, dtype)


PAIR = 128
QUAD = 256


def attend_kernel(
    x_ref, wq_ref, bq_ref, wk_ref, wv_ref, bv_ref, wo_ref, bo_ref, qa_ref, kb_ref,
    q_ref, k_ref, v_ref, o_ref, pt_ref, r_ref,
):
    x = x_ref[0]
    hd = PAIR // 2
    q = (dot(x, wq_ref[...]) + bq_ref[...]).astype(BF) * jnp.asarray(hd ** (-0.5), BF)
    k = dot(x, wk_ref[...]).astype(BF)
    v = (dot(x, wv_ref[...]) + bv_ref[...]).astype(BF)
    q_ref[0], k_ref[0], v_ref[0] = q, k, v
    lane = lax.broadcasted_iota(jnp.int32, (x.shape[0], PAIR), 1)
    outs = []
    for pair in range(QUAD // PAIR):
        at = slice(pair * PAIR, (pair + 1) * PAIR)
        keys = jnp.concatenate([k[:, at], kb_ref[0]], axis=1)
        vt = v[:, at].T
        parts = []
        for h in range(2):
            mine = (lane >= hd) if h else (lane < hd)
            queries = jnp.concatenate([jnp.where(mine, q[:, at], 0), qa_ref[0]], axis=1)
            st = dot_t(keys, queries)
            expo = jnp.exp(st - jnp.max(st, axis=0, keepdims=True))
            pt = (expo * (1.0 / jnp.sum(expo, axis=0, keepdims=True))).astype(BF)
            pt_ref[0, 2 * pair + h] = pt
            parts.append(dot(vt[h * hd : (h + 1) * hd], pt))
        outs.append(jnp.concatenate(parts, axis=0).T)
    o = jnp.concatenate(outs, axis=1).astype(BF)
    o_ref[0] = o
    part = dot(o, wo_ref[...])

    @pl.when(pl.program_id(1) == 0)
    def _():
        r_ref[0] = x.astype(F32) + bo_ref[...] + part

    @pl.when(pl.program_id(1) > 0)
    def _():
        r_ref[0] += part


def attend(x, wq, bq, wk, wv, bv, wo, bo, qa, kb):
    batch, length, width = x.shape
    row = pl.BlockSpec((1, length, width), lambda b, j: (b, 0, 0))
    cols = pl.BlockSpec((width, QUAD), lambda b, j: (0, j))
    bias = pl.BlockSpec((1, QUAD), lambda b, j: (0, j))
    quad = pl.BlockSpec((1, length, QUAD), lambda b, j: (b, 0, j))
    aug = pl.BlockSpec((1, length, PAIR), lambda b, j: (b, 0, 0))
    heads = QUAD // (width // HEADS)
    act = shape_of(x.shape, BF)
    return call(
        attend_kernel,
        (batch, width // QUAD),
        [row, cols, bias, cols, cols, bias,
         pl.BlockSpec((QUAD, width), lambda b, j: (j, 0)),
         pl.BlockSpec((1, width), lambda b, j: (0, 0)), aug, aug],
        [quad, quad, quad, quad,
         pl.BlockSpec((1, heads, length, length), lambda b, j: (b, j, 0, 0)), row],
        [act, act, act, act, shape_of((batch, HEADS, length, length), BF), shape_of(x.shape, F32)],
        [],
        batch * length * width * (8 * width + 8 * length),
        batch * length * (14 * width + 2 * HEADS * length) + 8 * width * width,
    )(x, wq, bq, wk, wv, bv, wo, bo, qa, kb)


def attend_back_kernel(
    q_ref, k_ref, v_ref, o_ref, do_ref, pt_ref, dq_ref, dk_ref, dv_ref, sum_ref,
):
    hd = PAIR // 2
    length = q_ref.shape[1]
    lane = lax.broadcasted_iota(jnp.int32, (length, PAIR), 1)
    lane8 = lax.broadcasted_iota(jnp.int32, (8, PAIR), 1)
    dqs, dvs = [], []
    for pair in range(QUAD // PAIR):
        at = slice(pair * PAIR, (pair + 1) * PAIR)
        q, k, v, o, do = (ref[0, :, at] for ref in (q_ref, k_ref, v_ref, o_ref, do_ref))
        kt = k.T
        prod = o.astype(F32) * do.astype(F32)
        high = prod.astype(BF)
        low = (prod - high.astype(F32)).astype(BF)
        dk = dv = None
        dqt = []
        for h in range(2):
            mine = (lane >= hd) if h else (lane < hd)
            ones = jnp.where((lane8 >= hd) if h else (lane8 < hd), 1.0, 0.0).astype(BF)
            do_h = jnp.where(mine, do, 0)
            q_h = jnp.where(mine, q, 0)
            mixed = (dot_t(ones, high) + dot_t(ones, low))[0:1]
            pt = pt_ref[0, 2 * pair + h]
            ds = (pt.astype(F32) * (dot_t(v, do_h) - mixed)).astype(BF)
            dv_h, dk_h = dot(pt, do_h), dot(ds, q_h)
            dv = dv_h if dv is None else dv + dv_h
            dk = dk_h if dk is None else dk + dk_h
            dqt.append(dot(kt[h * hd : (h + 1) * hd], ds))
        dq = (jnp.concatenate(dqt, axis=0).T * (hd ** (-0.5))).astype(BF)
        dv = dv.astype(BF)
        dq_ref[0, :, at], dk_ref[0, :, at], dv_ref[0, :, at] = dq, dk.astype(BF), dv
        sum_ref[0, 0:1, at] = jnp.sum(dq.astype(F32), axis=0, keepdims=True)
        sum_ref[0, 1:2, at] = jnp.sum(dv.astype(F32), axis=0, keepdims=True)


def attend_back(q, k, v, o, do, pt):
    batch, length, width = q.shape
    quad = pl.BlockSpec((1, length, QUAD), lambda b, j: (b, 0, j))
    heads = QUAD // (width // HEADS)
    act = shape_of(q.shape, BF)
    return call(
        attend_back_kernel,
        (batch, width // QUAD),
        [quad] * 5 + [pl.BlockSpec((1, heads, length, length), lambda b, j: (b, j, 0, 0))],
        [quad, quad, quad, pl.BlockSpec((1, 8, QUAD), lambda b, j: (b, 0, j))],
        [act, act, act, shape_of((batch, 8, width), F32)],
        [],
        batch * length * length * width * 16,
        batch * length * (16 * width + 2 * HEADS * length),
    )(q, k, v, o, do, pt)


def gelu_both(u):
    t = 1.0 / (1.0 + (0.3275911 * INV_ROOT_TWO) * jnp.abs(u))
    poly = t * (
        0.127414796 + t * (-0.142248368 + t * (0.7107068705 + t * (-0.7265760135 + t * 0.5307027145)))
    )
    bell = jnp.exp(-0.5 * u * u)
    tail = poly * bell
    cdf = jnp.where(u < 0.0, tail, 1.0 - tail)
    return u * cdf, cdf + (INV_ROOT_TWO_PI * u) * bell


def feed_kernel(
    r_ref, g_ref, b_ref, wi_ref, bi_ref, wo_ref, bo_ref, ids_ref,
    h_ref, act_ref, slope_ref, r2_ref, pool_ref, hidden,
):
    step = pl.program_id(1)

    @pl.when(step == 0)
    def _():
        xhat, _ = normalize(r_ref[0])
        h = xhat * g_ref[...] + b_ref[...]
        hidden[...] = h
        h_ref[0] = h.astype(BF)

    u = dot(h_ref[0], wi_ref[...]) + bi_ref[...]
    act, slope = gelu_both(u)
    act = act.astype(BF)
    act_ref[0] = act
    slope_ref[0] = slope.astype(BF)
    hidden[...] += dot(act, wo_ref[...])

    @pl.when(step == pl.num_programs(1) - 1)
    def _():
        r2 = hidden[...] + bo_ref[...]
        r2_ref[0] = r2
        xhat, _ = normalize(r2)
        hot = lax.broadcasted_iota(jnp.int32, (SEG_ROW, r2.shape[0]), 0) == ids_ref[0]
        counts = jnp.sum(hot.astype(F32), axis=1, keepdims=True)
        hot = hot.astype(F32).astype(BF)
        total = sum(dot(hot, piece) for piece in split3(xhat))
        pool_ref[0] = total / counts


def feed(r, gain, shift, wi, bi, wo, bo, ids):
    batch, length, width = r.shape
    ff = wi.shape[1]
    row = pl.BlockSpec((1, length, width), lambda b, c: (b, 0, 0))
    vec = pl.BlockSpec((1, width), lambda b, c: (0, 0))
    chunk = pl.BlockSpec((1, length, width), lambda b, c: (b, 0, c))
    wide = shape_of((batch, length, ff), BF)
    return call(
        feed_kernel,
        (batch, ff // width),
        [row, vec, vec, pl.BlockSpec((width, width), lambda b, c: (0, c)),
         pl.BlockSpec((1, width), lambda b, c: (0, c)),
         pl.BlockSpec((width, width), lambda b, c: (c, 0)), vec,
         pl.BlockSpec((1, 1, length), lambda b, c: (b, 0, 0))],
        [row, chunk, chunk, row, pl.BlockSpec((1, SEG_ROW, width), lambda b, c: (b, 0, 0))],
        [shape_of(r.shape, BF), wide, wide, shape_of(r.shape, F32), shape_of((batch, SEG_ROW, width), F32)],
        [pltpu.VMEM((length, width), F32)],
        4 * batch * length * width * ff,
        batch * length * (10 * width + 4 * ff) + 4 * batch * width * ff,
    )(r, gain, shift, wi, bi, wo, bo, ids)


def flip(v, step):
    return v + step * (1 - 2 * (v // step % 2))


def links(rows):
    seq, row = lax.axis_index("seq"), lax.axis_index("rows")
    core, y, x = seq % 2, seq // 2 % 2, row % 2
    other = 1 - core
    found = [
        ((flip(seq, 1), row), core),
        ((seq + core * 2 * (1 - 2 * y), row + other * (1 - 2 * x)), core * y + other * x),
        ((seq + other * 2 * (1 - 2 * y), row + core * (1 - 2 * x)), other * y + core * x),
    ]
    step = 2
    while step < rows:
        found.append(((seq, flip(row, step)), row // step % 2))
        step *= 2
    return found


def greet(devices):
    barrier = pltpu.get_barrier_semaphore()
    for device in devices:
        pl.semaphore_signal(barrier, inc=1, device_id=device, device_id_type=MESH)
    pl.semaphore_wait(barrier, len(devices))


def remote(source, target, send, receive, device):
    return pltpu.make_async_remote_copy(
        src_ref=source, dst_ref=target, send_sem=send, recv_sem=receive,
        device_id=device, device_id_type=MESH,
    )


def contrast_kernel(
    rows, xpool_ref, gain_ref, shift_ref, tag_ref, counts_ref,
    de_ref, vec_ref, all_ref, lse_ref, send, receive,
):
    own, width = xpool_ref.shape
    total = all_ref.shape[0]
    near = links(rows)
    hops = near[3:][::-1] + near[1:3] + near[:1]
    greet([device for device, _ in hops])
    e_own = xpool_ref[...] * gain_ref[...] + shift_ref[...]
    all_ref[0:own, 0:width] = e_own
    all_ref[0:own, width:] = tag_ref[...]
    have = own
    for i, (device, _) in enumerate(hops):
        copy = remote(
            all_ref.at[0:have], all_ref.at[have : 2 * have], send.at[i], receive.at[i], device
        )
        copy.start()
        copy.wait()
        have *= 2

    def unit(e):
        rho = lax.rsqrt(jnp.sum(e * e, axis=1, keepdims=True) + POOL_EPS)
        return e * rho, rho

    n_all, _ = unit(all_ref[:, 0:width])
    pick = lax.broadcasted_iota(jnp.int32, (8, PAIR), 0) == lax.broadcasted_iota(jnp.int32, (8, PAIR), 1)
    tags = dot_t(pick.astype(F32), all_ref[:, width:], HIGHEST)
    pos_all, id_all = tags[0:1], tags[1:2]
    block = min(total, 512)
    for b in range(total // block):
        n_b, _ = unit(all_ref[b * block : (b + 1) * block, 0:width])
        c = dot_t(n_all, n_b, HIGHEST) * INV_TEMPER
        i = lax.broadcasted_iota(jnp.int32, c.shape, 0)
        j = lax.broadcasted_iota(jnp.int32, c.shape, 1) + b * block
        c = jnp.where(i == j, MASKED, c)
        top = jnp.max(c, axis=0, keepdims=True)
        lse_ref[:, b * block : (b + 1) * block] = (
            jnp.log(jnp.sum(jnp.exp(c - top), axis=0, keepdims=True)) + top
        )
    n_own, rho = unit(e_own)
    pos_own, id_own = tag_ref[:, 0:1], tag_ref[:, 1:2]
    c = dot_t(n_own, n_all, HIGHEST) * INV_TEMPER
    c = jnp.where(id_own == id_all, MASKED, c)
    top = jnp.max(c, axis=1, keepdims=True)
    lse_own = jnp.log(jnp.sum(jnp.exp(c - top), axis=1, keepdims=True)) + top
    chosen = id_all == pos_own
    picked = jnp.sum(jnp.where(chosen, c, 0.0), axis=1, keepdims=True)
    weight = (
        jnp.exp(c - lse_own)
        + jnp.exp(c - lse_ref[...])
        - jnp.where(chosen, 1.0, 0.0)
        - jnp.where(id_own == pos_all, 1.0, 0.0)
    )
    d_n = INV_TEMPER * jnp.dot(weight, n_all, precision=HIGHEST, preferred_element_type=F32)
    along = jnp.sum(e_own * d_n, axis=1, keepdims=True)
    d_e = rho * d_n - (rho * rho * rho) * e_own * along
    de_ref[...] = d_e / counts_ref[...]
    vec_ref[0:1] = jnp.sum(d_e * xpool_ref[...], axis=0, keepdims=True)
    vec_ref[1:2] = jnp.sum(d_e, axis=0, keepdims=True)
    vec_ref[2:3] = jnp.broadcast_to(jnp.sum(lse_own - picked), (1, vec_ref.shape[1]))
    vec_ref[3:8] = jnp.zeros((5, vec_ref.shape[1]), F32)


def contrast(xpool, gain, shift, tags, counts, devices, rows):
    own, width = xpool.shape
    total = own * devices
    vmem = pl.BlockSpec(memory_space=pltpu.VMEM)
    stages = len(bin(devices)) - 3
    return pl.pallas_call(
        functools.partial(contrast_kernel, rows),
        in_specs=[vmem] * 5,
        out_specs=[vmem, vmem],
        out_shape=[shape_of((own, width), F32), shape_of((8, width), F32)],
        scratch_shapes=[
            pltpu.VMEM((total, width + PAIR), F32),
            pltpu.VMEM((1, total), F32),
            pltpu.SemaphoreType.DMA((stages,)),
            pltpu.SemaphoreType.DMA((stages,)),
        ],
        cost_estimate=pl.CostEstimate(
            flops=12 * total * total * width, bytes_accessed=4 * total * width, transcendentals=0
        ),
        compiler_params=pltpu.CompilerParams(
            vmem_limit_bytes=48 << 20, collective_id=0, has_side_effects=True
        ),
    )(xpool, gain, shift, tags, counts)


class Chain:
    def __init__(self, order, first, number, rows_chunk, start, period, grads, sums, send, receive, came):
        self.order, self.first, self.number = order, first, number
        self.start, self.period = start, period
        self.grads, self.sums, self.send, self.receive, self.came = grads, sums, send, receive, came
        sizes, height, wide = [], rows_chunk, grads.shape[1]
        for _ in order:
            if height % 32 == 0:
                height //= 2
            else:
                wide //= 2
            sizes.append((height, wide))
        self.sizes, self.rows_chunk = sizes, rows_chunk
        self.last = start + (number - 1) * period + 2 * len(order)

    def places(self, chunk):
        row, column = chunk * self.rows_chunk, 0
        before = self.rows_chunk
        found = []
        for (height, wide), (_, bit) in zip(self.sizes, self.order):
            if height < before:
                kept = (row + bit * height, column)
                sent = (row + (1 - bit) * height, column)
            else:
                kept = (row, column + bit * wide)
                sent = (row, column + (1 - bit) * wide)
            found.append((kept, sent))
            (row, column), before = kept, height
        return found

    def at(self, ref, place, size):
        row, column = place
        if size[1] == ref.shape[1]:
            return ref.at[pl.ds(pl.multiple_of(row, 16), size[0])]
        return ref.at[
            pl.ds(pl.multiple_of(row, 16), size[0]), pl.ds(pl.multiple_of(column, PAIR), size[1])
        ]

    def copy(self, chunk, places, stage):
        n = len(self.order)
        i = stage if stage < n else 2 * n - 1 - stage
        kept, sent = places[i]
        size, device = self.sizes[i], self.order[i][0]
        sems = self.send.at[stage, chunk], self.receive.at[stage, chunk]
        if stage < n:
            slot = self.came[i].at[chunk - self.first]
            return remote(self.at(self.grads, sent, size), slot, *sems, device)
        part = self.at(self.sums, kept, size)
        return remote(part, part, *sems, device)

    def step(self, t):
        for stage in range(2 * len(self.order), -1, -1):
            since = t - stage - self.start
            index = since // self.period
            pl.when((since >= 0) & (since % self.period == 0) & (index < self.number))(
                functools.partial(self.advance, stage, index + self.first)
            )

    def advance(self, stage, chunk):
        n = len(self.order)
        places = self.places(chunk)
        if stage > 0:
            self.copy(chunk, places, stage - 1).wait()
        if 0 < stage <= n:
            i = stage - 1
            height, wide = self.sizes[i]
            tile = min(height, 32)
            (row, column), _ = places[i]
            target = self.grads if stage < n else self.sums

            def add(k, carry):
                place, size = (row + k * tile, column), (tile, wide)
                mine = self.at(self.grads, place, size)
                theirs = self.came[i].at[chunk - self.first, pl.ds(pl.multiple_of(k * tile, 16), tile)]
                total = mine[...].astype(F32) + theirs[...].astype(F32)
                self.at(target, place, size)[...] = total.astype(BF)
                return carry

            lax.fori_loop(0, height // tile, add, 0)
        if stage < 2 * n:
            self.copy(chunk, places, stage).start()


def sum_kernel(plan, rows, *refs):
    (grads, tokens, small), (sums, token_out, small_out) = refs[:3], refs[3:6]
    send, receive, s_send, s_receive, t_send, t_receive, own_sem, small_came = refs[6:14]
    came = refs[14:]
    near = links(rows)
    n = len(near)
    seq, row = lax.axis_index("seq"), lax.axis_index("rows")
    seqs = tokens.shape[1] // token_out.shape[1]
    greet([device for device, _ in near] + [(flip(flip(seq, 1), 2), row)])

    batch, part = tokens.shape[0], token_out.shape[1]
    def piece(i):
        to = lax.rem(seq + i, seqs)
        return remote(
            tokens.at[:, pl.ds(pl.multiple_of(to * part, 16), part)],
            token_out.at[pl.ds(seq * batch, batch)],
            t_send.at[i], t_receive.at[i], (to, row),
        )
    for i in range(1, seqs):
        piece(i).start()
    own = pltpu.make_async_copy(
        tokens.at[:, pl.ds(pl.multiple_of(seq * part, 16), part)],
        token_out.at[pl.ds(seq * batch, batch)], own_sem,
    )
    own.start()

    small_out[...] = small[...]
    orders = {"ab": near, "z": near[:1] + near[3:] + near[1:3]}
    chains, at = [], 0
    for name, first, number, rows_chunk, start, period in plan:
        chains.append(
            Chain(orders[name], first, number, rows_chunk, start, period,
                  grads, sums, send, receive, came[at : at + n])
        )
        at += n

    def small_copy(i):
        source = small_out if i == 0 else small_came.at[n + i - 1]
        return remote(source, small_came.at[i], s_send.at[i], s_receive.at[i], near[i][0])

    def step(t, carry):
        for chain in chains:
            chain.step(t)
        for i in range(n + 1):
            @pl.when(t == i)
            def _(i=i):
                if i > 0:
                    small_copy(i - 1).wait()
                    before = small_out if i == 1 else small_came.at[n + i - 2]
                    after = small_out if i == n else small_came.at[n + i - 1]
                    after[...] = before[...] + small_came[i - 1]
                if i < n:
                    small_copy(i).start()
        return carry

    lax.fori_loop(0, max(max(chain.last for chain in chains), n) + 1, step, 0)
    own.wait()
    for i in range(1, seqs):
        piece(i).wait()


def sum_all(grads, tokens, small, devices, rows, seqs):
    n = len(bin(devices)) - 3
    chunk = 1024
    plan = [("ab", 0, 9, chunk, 0, 1)]
    batch, length, width = tokens.shape
    total = grads.shape[0]
    vmem = pl.BlockSpec(memory_space=pltpu.VMEM)
    came = []
    for _, _, number, height, _, _ in plan:
        wide = width
        for _ in range(n):
            if height % 32 == 0:
                height //= 2
            else:
                wide //= 2
            came.append(pltpu.VMEM((number, height, wide), BF))
    chunks = sum(p[2] for p in plan)
    return pl.pallas_call(
        functools.partial(sum_kernel, plan, rows),
        in_specs=[vmem] * 3,
        out_specs=[vmem] * 3,
        out_shape=[
            shape_of(grads.shape, BF),
            shape_of((batch * seqs, length // seqs, width), BF),
            shape_of(small.shape, F32),
        ],
        scratch_shapes=[
            pltpu.SemaphoreType.DMA((2 * n, chunks)),
            pltpu.SemaphoreType.DMA((2 * n, chunks)),
            pltpu.SemaphoreType.DMA((n,)),
            pltpu.SemaphoreType.DMA((n,)),
            pltpu.SemaphoreType.DMA((seqs,)),
            pltpu.SemaphoreType.DMA((seqs,)),
            pltpu.SemaphoreType.DMA,
            pltpu.VMEM((2 * n,) + small.shape, F32),
        ] + came,
        cost_estimate=pl.CostEstimate(flops=total * width * 4, bytes_accessed=total * width * 8, transcendentals=0),
        compiler_params=pltpu.CompilerParams(
            vmem_limit_bytes=60 << 20, collective_id=1, has_side_effects=True
        ),
    )(grads, tokens, small)


def pool_back_kernel(r2_ref, gain_ref, ids_ref, de_ref, dr_ref, df_ref, sum_ref):
    length, width = r2_ref.shape[1:]
    xhat, scale = normalize(r2_ref[0])
    lane = lax.broadcasted_iota(jnp.int32, (length, PAIR), 1)
    hot = (lane % SEG_ROW == ids_ref[0]) & (lane < 3 * SEG_ROW)
    hot = jnp.where(hot, 1.0, 0.0).astype(BF)
    pieces = list(split3(de_ref[0])) + [jnp.zeros((PAIR - 3 * SEG_ROW, width), BF)]
    d_y = dot(hot, jnp.concatenate(pieces, axis=0))
    d_r = norm_back(d_y, gain_ref[...], xhat, scale)
    dr_ref[0] = d_r
    d_f = d_r.astype(BF)
    df_ref[0] = d_f
    sum_ref[0, 0:1] = jnp.sum(d_f.astype(F32), axis=0, keepdims=True)


def pool_back(r2, gain, ids_col, de):
    batch, length, width = r2.shape
    row = pl.BlockSpec((1, length, width), lambda b: (b, 0, 0))
    eight = pl.BlockSpec((1, 8, width), lambda b: (b, 0, 0))
    return call(
        pool_back_kernel,
        (batch,),
        [row, pl.BlockSpec((1, width), lambda b: (0, 0)),
         pl.BlockSpec((1, length, 1), lambda b: (b, 0, 0)),
         pl.BlockSpec((1, SEG_ROW, width), lambda b: (b, 0, 0))],
        [row, row, eight],
        [shape_of(r2.shape, F32), shape_of(r2.shape, BF), shape_of((batch, 8, width), F32)],
        [],
        batch * length * width * 300,
        batch * length * width * 10,
    )(r2, gain, ids_col, de)


def feed_back_kernel(
    df_ref, dr2_ref, slope_ref, wo_ref, wi_ref, r_ref, gain_ref, wa_ref,
    du_ref, dr_ref, da_ref, do_ref, sum_ref, usum_ref, total,
):
    step = pl.program_id(1)
    d_u = (dot_t(df_ref[0], wo_ref[...]) * slope_ref[0].astype(F32)).astype(BF)
    du_ref[0] = d_u
    usum_ref[0, 0:1] = jnp.sum(d_u.astype(F32), axis=0, keepdims=True)
    part = dot_t(d_u, wi_ref[...])

    @pl.when(step == 0)
    def _():
        total[...] = dr2_ref[0] + part

    @pl.when(step > 0)
    def _():
        total[...] += part

    @pl.when(step == pl.num_programs(1) - 1)
    def _():
        d_h = total[...]
        xhat, scale = normalize(r_ref[0])
        d_r = norm_back(d_h, gain_ref[...], xhat, scale)
        dr_ref[0] = d_r
        d_a = d_r.astype(BF)
        da_ref[0] = d_a
        do_ref[0] = dot_t(d_a, wa_ref[...]).astype(BF)
        sum_ref[0, 0:1] = jnp.sum(d_a.astype(F32), axis=0, keepdims=True)
        sum_ref[0, 1:2] = jnp.sum(d_h * xhat, axis=0, keepdims=True)
        sum_ref[0, 2:3] = jnp.sum(d_h, axis=0, keepdims=True)


def feed_back(df, dr2, slope, wo, wi, r, gain, wa):
    batch, length, width = r.shape
    ff = wi.shape[1]
    row = pl.BlockSpec((1, length, width), lambda b, c: (b, 0, 0))
    chunk = pl.BlockSpec((1, length, width), lambda b, c: (b, 0, c))
    return call(
        feed_back_kernel,
        (batch, ff // width),
        [row, row, chunk, pl.BlockSpec((width, width), lambda b, c: (c, 0)),
         pl.BlockSpec((width, width), lambda b, c: (0, c)), row,
         pl.BlockSpec((1, width), lambda b, c: (0, 0)),
         pl.BlockSpec((width, width), lambda b, c: (0, 0))],
        [chunk, row, row, row, pl.BlockSpec((1, 8, width), lambda b, c: (b, 0, 0)),
         pl.BlockSpec((1, 8, width), lambda b, c: (b, 0, c))],
        [shape_of((batch, length, ff), BF), shape_of(r.shape, F32), shape_of(r.shape, BF),
         shape_of(r.shape, BF), shape_of((batch, 8, width), F32), shape_of((batch, 8, ff), F32)],
        [pltpu.VMEM((length, width), F32)],
        batch * length * width * (4 * ff + 2 * width),
        batch * length * (20 * width + 4 * ff) + 4 * batch * width * ff,
    )(df, dr2, slope, wo, wi, r, gain, wa)


def local(
    tokens,
    query_weight,
    query_bias,
    key_weight,
    value_weight,
    value_bias,
    output_weight,
    output_bias,
    attn_gain,
    attn_shift,
    inner_weight,
    inner_bias,
    outer_weight,
    outer_bias,
    ffn_gain,
    ffn_shift,
    segment_ids,
    positives,
):
    group_rows, local_len, width = tokens.shape
    ff = inner_weight.shape[1]
    seqs = lax.axis_size("seq")
    seq, row_place = lax.axis_index("seq"), lax.axis_index("rows")
    batch, length = group_rows // seqs, local_len * seqs
    count = batch * length
    ids = lax.dynamic_slice_in_dim(segment_ids, seq * batch, batch, 0)
    own_segs = batch * SEG_ROW
    own_positives = lax.dynamic_slice_in_dim(positives, seq * own_segs, own_segs, 0)
    own_ids = row_place * positives.shape[0] + seq * own_segs + jnp.arange(own_segs, dtype=jnp.int32)
    tags = jnp.stack([own_positives, own_ids] + [jnp.zeros_like(own_ids)] * (PAIR - 2), axis=1).astype(F32)
    hot = ids[:, :, None] == jnp.arange(PAIR, dtype=jnp.int32)
    real = jnp.arange(PAIR, dtype=jnp.int32) < SEG_ROW
    apart_q = jnp.where(hot, -(2.0**30), 0.0).astype(BF)
    apart_k = jnp.where(hot | ~real, 0.0, 1.0).astype(BF)
    counts = jnp.sum(hot.astype(F32), axis=1)[:, :SEG_ROW].reshape(own_segs, 1)
    vec = lambda v: v.astype(F32).reshape(1, -1)
    flat2 = lambda a: a.reshape(count, a.shape[-1])

    x = lax.all_to_all(tokens, "seq", split_axis=0, concat_axis=1, tiled=True)
    q, k, v, o, pt, r_one = attend(
        x, query_weight, vec(query_bias), key_weight, value_weight, vec(value_bias),
        output_weight, vec(output_bias), apart_q, apart_k,
    )
    hidden, active, slope, r_two, xpool = feed(
        r_one, vec(attn_gain), vec(attn_shift), inner_weight, vec(inner_bias), outer_weight,
        vec(outer_bias), ids.reshape(batch, 1, length),
    )
    xpool = xpool.reshape(own_segs, width)
    rows = lax.axis_size("rows")
    devices = rows * seqs
    d_e, loss_vec = contrast(xpool, vec(ffn_gain), vec(ffn_shift), tags, counts, devices, rows)
    d_two, d_outer, outer_sum = pool_back(
        r_two, vec(ffn_gain), ids.reshape(batch, length, 1), d_e.reshape(batch, SEG_ROW, width)
    )
    g_outer = t_dot(flat2(active), flat2(d_outer)).astype(BF)
    d_inner, d_one, d_attn, d_o, row_sums, inner_sum = feed_back(
        d_outer, d_two, slope, outer_weight, inner_weight, r_one, vec(attn_gain), output_weight
    )
    d_inner2 = flat2(d_inner)
    g_inner = jnp.concatenate(
        [t_dot(flat2(hidden), d_inner2[:, i * width : (i + 1) * width]).astype(BF) for i in range(ff // width)],
        axis=0,
    )
    d_q, d_k, d_v, head_sums = attend_back(q, k, v, o, d_o, pt)
    d_q, d_k, d_v = flat2(d_q), flat2(d_k), flat2(d_v)
    flat = flat2(x)
    g_attn = jnp.concatenate(
        [t_dot(flat, d_q).astype(BF), t_dot(flat, d_k).astype(BF), t_dot(flat, d_v).astype(BF),
         t_dot(flat2(o), flat2(d_attn)).astype(BF)], axis=0
    )
    row_sums, head_sums = jnp.sum(row_sums, axis=0), jnp.sum(head_sums, axis=0)
    small = jnp.concatenate(
        [
            head_sums[0], head_sums[1], row_sums[0], row_sums[1], row_sums[2],
            jnp.sum(inner_sum[:, 0], axis=0), jnp.sum(outer_sum[:, 0], axis=0),
            loss_vec[0], loss_vec[1], loss_vec[2],
        ]
    ).reshape(-1, 128)
    small = jnp.pad(small, ((0, -small.shape[0] % 8), (0, 0)))
    token_grad = (
        flat2(d_one) + dot_t(d_q, query_weight) + dot_t(d_k, key_weight) + dot_t(d_v, value_weight)
    ).astype(BF)
    sums, grad_tokens, small = sum_all(
        jnp.concatenate([g_outer, g_inner, g_attn], axis=0),
        token_grad.reshape(batch, length, width), small, devices, rows, seqs,
    )
    grad_tokens = grad_tokens.astype(F32)
    small = small.reshape(-1)
    sum_outer = sums[:ff].astype(F32)
    sum_inner = jnp.concatenate(
        [sums[ff + i * width : ff + (i + 1) * width] for i in range(ff // width)], axis=1
    ).astype(F32)
    sum_attn = sums[2 * ff :].astype(F32)
    sizes = [width] * 5 + [ff] + [width] * 4
    pieces, at = [], 0
    for size in sizes:
        pieces.append(small[at : at + size])
        at += size
    qb, vb, ob, ag, ash, ib, wb, fg, fs, ls = pieces
    return (
        ls[0] / (own_segs * devices),
        grad_tokens,
        sum_attn[:width],
        qb,
        sum_attn[width : 2 * width],
        sum_attn[2 * width : 3 * width],
        vb,
        sum_attn[3 * width :],
        ob,
        ag,
        ash,
        sum_inner,
        ib,
        sum_outer,
        wb,
        fg,
        fs,
    )


def solution(mesh):
    placed = (
        (P("rows", "seq", None),) + (P(),) * 15 + (P("rows", None), P("rows"))
    )
    return jax.shard_map(
        local,
        mesh=mesh,
        in_specs=placed,
        out_specs=(P(), P("rows", "seq", None)) + (P(),) * 15,
        check_vma=False,
    )
```

```python
import functools

import jax
import jax.numpy as jnp
from jax import lax
from jax.experimental import pallas as pl
from jax.experimental.pallas import tpu as pltpu
from jax.sharding import PartitionSpec as P

HEADS = 12
SEG_ROW = 8
HIGHEST = lax.Precision.HIGHEST
NORM_EPS = 1e-12
POOL_EPS = 1e-06
INV_TEMPER = 100.0
MASKED = -1000000000.0
INV_ROOT_TWO_PI = 0.3989422804014327
INV_ROOT_TWO = 0.7071067811865476
BF = jnp.bfloat16
F32 = jnp.float32
MESH = pl.DeviceIdType.MESH


def dot(a, b):
    return jnp.dot(a, b, preferred_element_type=F32)


def dot_t(a, b, precision=None):
    return lax.dot_general(
        a, b, (((1,), (1,)), ((), ())), preferred_element_type=F32, precision=precision
    )


def t_dot(a, b):
    return lax.dot_general(a, b, (((0,), (0,)), ((), ())), preferred_element_type=F32)


def normalize(resid):
    center = resid - jnp.mean(resid, axis=-1, keepdims=True)
    spread = jnp.mean(center * center, axis=-1, keepdims=True)
    scale = lax.rsqrt(spread + NORM_EPS)
    return center * scale, scale


def norm_back(grad, gain, xhat, scale):
    q = grad * gain
    return scale * (
        q - jnp.mean(q, axis=-1, keepdims=True) - xhat * jnp.mean(q * xhat, axis=-1, keepdims=True)
    )


def split3(a):
    hi = a.astype(BF)
    rest = a - hi.astype(F32)
    mid = rest.astype(BF)
    return hi, mid, (rest - mid.astype(F32)).astype(BF)


def call(kernel, grid, in_specs, out_specs, out_shape, scratch, flops, moved, vmem=48):
    return pl.pallas_call(
        kernel,
        grid=grid,
        in_specs=in_specs,
        out_specs=out_specs,
        out_shape=out_shape,
        scratch_shapes=scratch,
        cost_estimate=pl.CostEstimate(flops=flops, bytes_accessed=moved, transcendentals=0),
        compiler_params=pltpu.CompilerParams(vmem_limit_bytes=vmem << 20),
    )


def shape_of(dims, dtype):
    return jax.ShapeDtypeStruct(dims, dtype)


PAIR = 128
QUAD = 256


def attend_kernel(
    x_ref, wq_ref, bq_ref, wk_ref, wv_ref, bv_ref, wo_ref, bo_ref, qa_ref, kb_ref,
    q_ref, k_ref, v_ref, o_ref, pt_ref, r_ref,
):
    x = x_ref[0]
    hd = PAIR // 2
    q = (dot(x, wq_ref[...]) + bq_ref[...]).astype(BF) * jnp.asarray(hd ** (-0.5), BF)
    k = dot(x, wk_ref[...]).astype(BF)
    v = (dot(x, wv_ref[...]) + bv_ref[...]).astype(BF)
    q_ref[0], k_ref[0], v_ref[0] = q, k, v
    lane = lax.broadcasted_iota(jnp.int32, (x.shape[0], PAIR), 1)
    outs = []
    for pair in range(QUAD // PAIR):
        at = slice(pair * PAIR, (pair + 1) * PAIR)
        keys = jnp.concatenate([k[:, at], kb_ref[0]], axis=1)
        vt = v[:, at].T
        parts = []
        for h in range(2):
            mine = (lane >= hd) if h else (lane < hd)
            queries = jnp.concatenate([jnp.where(mine, q[:, at], 0), qa_ref[0]], axis=1)
            st = dot_t(keys, queries)
            expo = jnp.exp(st - jnp.max(st, axis=0, keepdims=True))
            pt = (expo * (1.0 / jnp.sum(expo, axis=0, keepdims=True))).astype(BF)
            pt_ref[0, 2 * pair + h] = pt
            parts.append(dot(vt[h * hd : (h + 1) * hd], pt))
        outs.append(jnp.concatenate(parts, axis=0).T)
    o = jnp.concatenate(outs, axis=1).astype(BF)
    o_ref[0] = o
    part = dot(o, wo_ref[...])

    @pl.when(pl.program_id(1) == 0)
    def _():
        r_ref[0] = x.astype(F32) + bo_ref[...] + part

    @pl.when(pl.program_id(1) > 0)
    def _():
        r_ref[0] += part


def attend(x, wq, bq, wk, wv, bv, wo, bo, qa, kb):
    batch, length, width = x.shape
    row = pl.BlockSpec((1, length, width), lambda b, j: (b, 0, 0))
    cols = pl.BlockSpec((width, QUAD), lambda b, j: (0, j))
    bias = pl.BlockSpec((1, QUAD), lambda b, j: (0, j))
    quad = pl.BlockSpec((1, length, QUAD), lambda b, j: (b, 0, j))
    aug = pl.BlockSpec((1, length, PAIR), lambda b, j: (b, 0, 0))
    heads = QUAD // (width // HEADS)
    act = shape_of(x.shape, BF)
    return call(
        attend_kernel,
        (batch, width // QUAD),
        [row, cols, bias, cols, cols, bias,
         pl.BlockSpec((QUAD, width), lambda b, j: (j, 0)),
         pl.BlockSpec((1, width), lambda b, j: (0, 0)), aug, aug],
        [quad, quad, quad, quad,
         pl.BlockSpec((1, heads, length, length), lambda b, j: (b, j, 0, 0)), row],
        [act, act, act, act, shape_of((batch, HEADS, length, length), BF), shape_of(x.shape, F32)],
        [],
        batch * length * width * (8 * width + 8 * length),
        batch * length * (14 * width + 2 * HEADS * length) + 8 * width * width,
    )(x, wq, bq, wk, wv, bv, wo, bo, qa, kb)


def gelu_both(u):
    t = 1.0 / (1.0 + (0.3275911 * INV_ROOT_TWO) * jnp.abs(u))
    poly = t * (
        0.127414796 + t * (-0.142248368 + t * (0.7107068705 + t * (-0.7265760135 + t * 0.5307027145)))
    )
    bell = jnp.exp(-0.5 * u * u)
    tail = poly * bell
    cdf = jnp.where(u < 0.0, tail, 1.0 - tail)
    return u * cdf, cdf + (INV_ROOT_TWO_PI * u) * bell


def feed_kernel(
    r_ref, g_ref, b_ref, wi_ref, bi_ref, wo_ref, bo_ref, ids_ref,
    h_ref, act_ref, slope_ref, r2_ref, pool_ref, hidden,
):
    step = pl.program_id(1)

    @pl.when(step == 0)
    def _():
        xhat, _ = normalize(r_ref[0])
        h = xhat * g_ref[...] + b_ref[...]
        hidden[...] = h
        h_ref[0] = h.astype(BF)

    u = dot(h_ref[0], wi_ref[...]) + bi_ref[...]
    act, slope = gelu_both(u)
    act = act.astype(BF)
    act_ref[0] = act
    slope_ref[0] = slope.astype(BF)
    hidden[...] += dot(act, wo_ref[...])

    @pl.when(step == pl.num_programs(1) - 1)
    def _():
        r2 = hidden[...] + bo_ref[...]
        r2_ref[0] = r2
        xhat, _ = normalize(r2)
        hot = lax.broadcasted_iota(jnp.int32, (SEG_ROW, r2.shape[0]), 0) == ids_ref[0]
        counts = jnp.sum(hot.astype(F32), axis=1, keepdims=True)
        hot = hot.astype(F32).astype(BF)
        total = sum(dot(hot, piece) for piece in split3(xhat))
        pool_ref[0] = total / counts


def feed(r, gain, shift, wi, bi, wo, bo, ids):
    batch, length, width = r.shape
    ff = wi.shape[1]
    row = pl.BlockSpec((1, length, width), lambda b, c: (b, 0, 0))
    vec = pl.BlockSpec((1, width), lambda b, c: (0, 0))
    chunk = pl.BlockSpec((1, length, width), lambda b, c: (b, 0, c))
    wide = shape_of((batch, length, ff), BF)
    return call(
        feed_kernel,
        (batch, ff // width),
        [row, vec, vec, pl.BlockSpec((width, width), lambda b, c: (0, c)),
         pl.BlockSpec((1, width), lambda b, c: (0, c)),
         pl.BlockSpec((width, width), lambda b, c: (c, 0)), vec,
         pl.BlockSpec((1, 1, length), lambda b, c: (b, 0, 0))],
        [row, chunk, chunk, row, pl.BlockSpec((1, SEG_ROW, width), lambda b, c: (b, 0, 0))],
        [shape_of(r.shape, BF), wide, wide, shape_of(r.shape, F32), shape_of((batch, SEG_ROW, width), F32)],
        [pltpu.VMEM((length, width), F32)],
        4 * batch * length * width * ff,
        batch * length * (10 * width + 4 * ff) + 4 * batch * width * ff,
    )(r, gain, shift, wi, bi, wo, bo, ids)


def flip(v, step):
    return v + step * (1 - 2 * (v // step % 2))


def links(rows):
    seq, row = lax.axis_index("seq"), lax.axis_index("rows")
    core, y, x = seq % 2, seq // 2 % 2, row % 2
    other = 1 - core
    found = [
        ((flip(seq, 1), row), core),
        ((seq + core * 2 * (1 - 2 * y), row + other * (1 - 2 * x)), core * y + other * x),
        ((seq + other * 2 * (1 - 2 * y), row + core * (1 - 2 * x)), other * y + core * x),
    ]
    step = 2
    while step < rows:
        found.append(((seq, flip(row, step)), row // step % 2))
        step *= 2
    return found


def greet(devices):
    barrier = pltpu.get_barrier_semaphore()
    for device in devices:
        pl.semaphore_signal(barrier, inc=1, device_id=device, device_id_type=MESH)
    pl.semaphore_wait(barrier, len(devices))


def remote(source, target, send, receive, device):
    return pltpu.make_async_remote_copy(
        src_ref=source, dst_ref=target, send_sem=send, recv_sem=receive,
        device_id=device, device_id_type=MESH,
    )


def contrast_kernel(
    rows, xpool_ref, gain_ref, shift_ref, tag_ref, counts_ref,
    de_ref, vec_ref, all_ref, lse_ref, send, receive,
):
    own, width = xpool_ref.shape
    total = all_ref.shape[0]
    near = links(rows)
    hops = near[3:][::-1] + near[1:3] + near[:1]
    greet([device for device, _ in hops])
    e_own = xpool_ref[...] * gain_ref[...] + shift_ref[...]
    all_ref[0:own, 0:width] = e_own
    all_ref[0:own, width:] = tag_ref[...]
    have = own
    for i, (device, _) in enumerate(hops):
        copy = remote(
            all_ref.at[0:have], all_ref.at[have : 2 * have], send.at[i], receive.at[i], device
        )
        copy.start()
        copy.wait()
        have *= 2

    def unit(e):
        rho = lax.rsqrt(jnp.sum(e * e, axis=1, keepdims=True) + POOL_EPS)
        return e * rho, rho

    n_all, _ = unit(all_ref[:, 0:width])
    pick = lax.broadcasted_iota(jnp.int32, (8, PAIR), 0) == lax.broadcasted_iota(jnp.int32, (8, PAIR), 1)
    tags = dot_t(pick.astype(F32), all_ref[:, width:], HIGHEST)
    pos_all, id_all = tags[0:1], tags[1:2]
    block = min(total, 512)
    for b in range(total // block):
        n_b, _ = unit(all_ref[b * block : (b + 1) * block, 0:width])
        c = dot_t(n_all, n_b, HIGHEST) * INV_TEMPER
        i = lax.broadcasted_iota(jnp.int32, c.shape, 0)
        j = lax.broadcasted_iota(jnp.int32, c.shape, 1) + b * block
        c = jnp.where(i == j, MASKED, c)
        top = jnp.max(c, axis=0, keepdims=True)
        lse_ref[:, b * block : (b + 1) * block] = (
            jnp.log(jnp.sum(jnp.exp(c - top), axis=0, keepdims=True)) + top
        )
    n_own, rho = unit(e_own)
    pos_own, id_own = tag_ref[:, 0:1], tag_ref[:, 1:2]
    c = dot_t(n_own, n_all, HIGHEST) * INV_TEMPER
    c = jnp.where(id_own == id_all, MASKED, c)
    top = jnp.max(c, axis=1, keepdims=True)
    lse_own = jnp.log(jnp.sum(jnp.exp(c - top), axis=1, keepdims=True)) + top
    chosen = id_all == pos_own
    picked = jnp.sum(jnp.where(chosen, c, 0.0), axis=1, keepdims=True)
    weight = (
        jnp.exp(c - lse_own)
        + jnp.exp(c - lse_ref[...])
        - jnp.where(chosen, 1.0, 0.0)
        - jnp.where(id_own == pos_all, 1.0, 0.0)
    )
    d_n = INV_TEMPER * jnp.dot(weight, n_all, precision=HIGHEST, preferred_element_type=F32)
    along = jnp.sum(e_own * d_n, axis=1, keepdims=True)
    d_e = rho * d_n - (rho * rho * rho) * e_own * along
    de_ref[...] = d_e / counts_ref[...]
    vec_ref[0:1] = jnp.sum(d_e * xpool_ref[...], axis=0, keepdims=True)
    vec_ref[1:2] = jnp.sum(d_e, axis=0, keepdims=True)
    vec_ref[2:3] = jnp.broadcast_to(jnp.sum(lse_own - picked), (1, vec_ref.shape[1]))
    vec_ref[3:8] = jnp.zeros((5, vec_ref.shape[1]), F32)


def contrast(xpool, gain, shift, tags, counts, devices, rows):
    own, width = xpool.shape
    total = own * devices
    vmem = pl.BlockSpec(memory_space=pltpu.VMEM)
    stages = len(bin(devices)) - 3
    return pl.pallas_call(
        functools.partial(contrast_kernel, rows),
        in_specs=[vmem] * 5,
        out_specs=[vmem, vmem],
        out_shape=[shape_of((own, width), F32), shape_of((8, width), F32)],
        scratch_shapes=[
            pltpu.VMEM((total, width + PAIR), F32),
            pltpu.VMEM((1, total), F32),
            pltpu.SemaphoreType.DMA((stages,)),
            pltpu.SemaphoreType.DMA((stages,)),
        ],
        cost_estimate=pl.CostEstimate(
            flops=12 * total * total * width, bytes_accessed=4 * total * width, transcendentals=0
        ),
        compiler_params=pltpu.CompilerParams(
            vmem_limit_bytes=48 << 20, collective_id=0, has_side_effects=True
        ),
    )(xpool, gain, shift, tags, counts)


CHUNK = 1024


def halves(steps, dims):
    sizes, (height, wide) = [], dims
    for _ in range(steps):
        if height % 32 == 0:
            height //= 2
        else:
            wide //= 2
        sizes.append((height, wide))
    return sizes


def plan(outer, inner, quads, batch):
    ready = outer + inner + 2 * batch
    return [
        ("ab", 0, 0, outer, 1, 1, (1, 3, 2, 1)),
        ("ab", 1, 0, inner, outer + 1, 1, (1, 3, 2, 1)),
        ("ab", 2, 0, quads, ready, 2 * batch, (1, 2, 2, 1)),
    ]


def orders(rows):
    near = links(rows)
    seq, row = lax.axis_index("seq"), lax.axis_index("rows")
    along = [((seq, flip(row, 1)), row % 2), ((flip(seq, 2), row), seq // 2 % 2)]
    return {
        "ab": near,
        "xy": near[:1] + along + near[3:],
        "z": near[:1] + near[3:] + near[1:3],
    }


class Chain:
    def __init__(self, order, entry, dims, down, grads, sums, mark, came, piece, send, receive, keep):
        self.first, self.number, self.start, self.period, stretch = entry
        stretch = list(stretch) + [stretch[-1]] * (len(order) - len(stretch))
        self.after = [0]
        for wait in stretch + stretch[::-1]:
            self.after.append(self.after[-1] + wait)
        self.order, self.dims, self.down = order, dims, down
        self.grads, self.sums, self.mark = grads, sums, mark
        self.came, self.piece = came, piece
        self.send, self.receive, self.keep = send, receive, keep
        self.sizes = halves(len(order), dims)
        self.last = self.start + (self.number - 1) * self.period + self.after[-1]

    def places(self, chunk):
        row, column = (chunk * self.dims[0], 0) if self.down else (0, chunk * self.dims[1])
        before = self.dims[0]
        found = []
        for (height, wide), (_, bit) in zip(self.sizes, self.order):
            if height < before:
                kept = (row + bit * height, column)
                sent = (row + (1 - bit) * height, column)
            else:
                kept = (row, column + bit * wide)
                sent = (row, column + (1 - bit) * wide)
            found.append((kept, sent))
            (row, column), before = kept, height
        return found

    def at(self, ref, place, size):
        row, column = place
        return ref.at[
            pl.ds(pl.multiple_of(row, 16), size[0]), pl.ds(pl.multiple_of(column, PAIR), size[1])
        ]

    def copy(self, chunk, places, stage):
        n = len(self.order)
        i = stage if stage < n else 2 * n - 1 - stage
        kept, sent = places[i]
        size, device = self.sizes[i], self.order[i][0]
        mark = chunk + self.mark
        pair = self.send.at[stage, mark], self.receive.at[stage, mark]
        if stage < n:
            return remote(self.at(self.grads, sent, size), self.came[i].at[chunk], *pair, device)
        target = self.at(self.sums, kept, size)
        return remote(self.piece.at[chunk] if stage == n else target, target, *pair, device)

    def own(self, chunk, places):
        target = self.at(self.sums, places[-1][0], self.sizes[-1])
        return pltpu.make_async_copy(self.piece.at[chunk], target, self.keep.at[chunk + self.mark])

    def step(self, t):
        for stage in range(2 * len(self.order), -1, -1):
            since = t - self.after[stage] - self.start
            if self.number == 1:
                pl.when(since == 0)(functools.partial(self.advance, stage, self.first))
                continue
            index = since // self.period if self.period > 1 else since
            here = (since >= 0) & (index < self.number)
            if self.period > 1:
                here &= since % self.period == 0
            pl.when(here)(functools.partial(self.advance, stage, index + self.first))

    def advance(self, stage, chunk):
        n = len(self.order)
        places = self.places(chunk)
        if stage > 0:
            self.copy(chunk, places, stage - 1).wait()
        if 0 < stage <= n:
            height, wide = self.sizes[stage - 1]
            row, column = places[stage - 1][0]
            tile = 16 if height % 32 else 32

            def add(k, carry):
                at = pl.ds(pl.multiple_of(k * tile, 16), tile)
                mine = self.at(self.grads, (row + k * tile, column), (tile, wide))
                total = (mine[...].astype(F32) + self.came[stage - 1][chunk, at].astype(F32)).astype(BF)
                if stage < n:
                    mine[...] = total
                else:
                    self.piece[chunk, at] = total
                return carry

            lax.fori_loop(0, height // tile, add, 0)
        if stage == n:
            self.own(chunk, places).start()
        if stage == n + 1:
            self.own(chunk, places).wait()
        if stage < 2 * n:
            self.copy(chunk, places, stage).start()


def sems(*dims):
    return [pltpu.SemaphoreType.DMA(dims)] * 2


def feed_back_kernel(
    df_ref, dr2_ref, slope_ref, wo_ref, wi_ref, r_ref, gain_ref, wa_ref,
    du_ref, dr_ref, da_ref, do_ref, sum_ref, usum_ref, total,
):
    step = pl.program_id(1)
    d_u = (dot_t(df_ref[0], wo_ref[...]) * slope_ref[0].astype(F32)).astype(BF)
    du_ref[0] = d_u
    usum_ref[0, 0:1] = jnp.sum(d_u.astype(F32), axis=0, keepdims=True)
    part = dot_t(d_u, wi_ref[...])

    @pl.when(step == 0)
    def _():
        total[...] = dr2_ref[0] + part

    @pl.when(step > 0)
    def _():
        total[...] += part

    @pl.when(step == pl.num_programs(1) - 1)
    def _():
        d_h = total[...]
        xhat, scale = normalize(r_ref[0])
        d_r = norm_back(d_h, gain_ref[...], xhat, scale)
        dr_ref[0] = d_r
        d_a = d_r.astype(BF)
        da_ref[0] = d_a
        do_ref[0] = dot_t(d_a, wa_ref[...]).astype(BF)
        sum_ref[0, 0:1] = jnp.sum(d_a.astype(F32), axis=0, keepdims=True)
        sum_ref[0, 1:2] = jnp.sum(d_h * xhat, axis=0, keepdims=True)
        sum_ref[0, 2:3] = jnp.sum(d_h, axis=0, keepdims=True)


def feed_back(df, dr2, slope, wo, wi, r, gain, wa):
    batch, length, width = r.shape
    ff = wi.shape[1]
    row = pl.BlockSpec((1, length, width), lambda b, c: (b, 0, 0))
    chunk = pl.BlockSpec((1, length, width), lambda b, c: (b, 0, c))
    return call(
        feed_back_kernel,
        (batch, ff // width),
        [row, row, chunk, pl.BlockSpec((width, width), lambda b, c: (c, 0)),
         pl.BlockSpec((width, width), lambda b, c: (0, c)), row,
         pl.BlockSpec((1, width), lambda b, c: (0, 0)),
         pl.BlockSpec((width, width), lambda b, c: (0, 0))],
        [chunk, row, row, row, pl.BlockSpec((1, 8, width), lambda b, c: (b, 0, 0)),
         pl.BlockSpec((1, 8, width), lambda b, c: (b, 0, c))],
        [shape_of((batch, length, ff), BF), shape_of(r.shape, F32), shape_of(r.shape, BF),
         shape_of(r.shape, BF), shape_of((batch, 8, width), F32), shape_of((batch, 8, ff), F32)],
        [pltpu.VMEM((length, width), F32)],
        batch * length * width * (4 * ff + 2 * width),
        batch * length * (20 * width + 4 * ff) + 4 * batch * width * ff,
    )(df, dr2, slope, wo, wi, r, gain, wa)


def fixed(dims):
    return pl.BlockSpec(dims, lambda g: (0,) * len(dims), pipeline_mode=pl.Buffered(1))


def back_kernel(rows, *refs):
    (act_ref, df_ref, du_ref, h_ref, q_ref, k_ref, v_ref, o_ref, do_ref, pt_ref, x_ref, da_ref, dr_ref,
     wq_ref, wk_ref, wv_ref, small_ref) = refs[:17]
    sums, (token_out, small_out) = refs[17:20], refs[20:22]
    (g_outer, g_inner, g_attn, g_total, go_total, dx, tokens, small_came, send, receive, s_send,
     s_receive, t_send, t_receive, keep, other) = refs[22:38]
    landing = refs[38:]
    step = pl.program_id(0)
    length = q_ref.shape[1]
    count, width = x_ref.shape
    batch = count // length
    outer, inner = sums[0].shape[0] // CHUNK, sums[1].shape[1] // CHUNK
    quads = width // QUAD
    kinds = orders(rows)
    near = kinds["ab"]
    n = len(near)
    seq, row_place = lax.axis_index("seq"), lax.axis_index("rows")
    seqs = token_out.shape[0] // batch
    part = length // seqs
    groups = [
        ((CHUNK, width), True, g_outer, sums[0], 0),
        ((width, CHUNK), False, g_inner, sums[1], outer),
        ((CHUNK, width), True, g_attn, sums[2], outer + inner),
    ]
    chains = []
    for kind, group, *entry in plan(outer, inner, quads, batch):
        came = landing[group * (n + 1) : group * (n + 1) + n]
        piece = landing[group * (n + 1) + n]
        chains.append(
            Chain(kinds[kind], entry, *groups[group], came, piece, send, receive, keep)
        )
    before = outer + inner
    ticks = before + 2 * quads * batch
    last = max(max(chain.last for chain in chains), ticks + n)
    u = jnp.maximum(step - before, 0)

    def tick(t):
        for chain in chains:
            chain.step(t)

    def piece(i):
        to = lax.rem(seq + i, seqs)
        return remote(
            tokens.at[:, pl.ds(pl.multiple_of(to * part, part), part)],
            token_out.at[pl.ds(seq * batch, batch)],
            t_send.at[i - 1], t_receive.at[i - 1], (to, row_place),
        )

    def small_copy(i):
        source = small_out if i == 0 else small_came.at[n + i - 1]
        return remote(source, small_came.at[i], s_send.at[i], s_receive.at[i], near[i][0])

    load_dx = pltpu.make_async_copy(dr_ref, dx, other.at[0])

    @pl.when(step == 0)
    def _():
        greet([device for device, _ in near] + [(flip(flip(seq, 1), 2), row_place)])
        small_out[...] = small_ref[...]
        load_dx.start()

    tick(step + u)

    @pl.when(step < outer)
    def _():
        at = pl.ds(pl.multiple_of(step * CHUNK, CHUNK), CHUNK)
        g_outer[at] = t_dot(act_ref[...], df_ref[...]).astype(BF)

    @pl.when((step >= outer) & (step < before))
    def _():
        at = pl.ds(pl.multiple_of((step - outer) * CHUNK, CHUNK), CHUNK)
        g_inner[:, at] = t_dot(h_ref[...], du_ref[...]).astype(BF)

    @pl.when(step == before)
    def _():
        load_dx.wait()

    @pl.when(step >= before)
    def _():
        attend_back_step(
            u, lambda: tick(before + 2 * u + 1), q_ref, k_ref, v_ref, o_ref, do_ref, pt_ref, x_ref, da_ref,
            wq_ref, wk_ref, wv_ref, g_attn, g_total, go_total, dx, small_out,
        )

    @pl.when(step == pl.num_programs(0) - 1)
    def _():
        for b in range(batch):
            tokens[b] = dx[b * length : (b + 1) * length].astype(BF)
        for i in range(1, seqs):
            piece(i).start()
        own = pltpu.make_async_copy(
            tokens.at[:, pl.ds(pl.multiple_of(seq * part, part), part)],
            token_out.at[pl.ds(seq * batch, batch)], other.at[1],
        )
        own.start()

        def rest(t, carry):
            tick(t)
            for i in range(n + 1):
                @pl.when(t == ticks + i)
                def _(i=i):
                    if i > 0:
                        small_copy(i - 1).wait()
                        held = small_out if i == 1 else small_came.at[n + i - 2]
                        after = small_out if i == n else small_came.at[n + i - 1]
                        after[...] = held[...] + small_came[i - 1]
                    if i < n:
                        small_copy(i).start()
            return carry

        lax.fori_loop(ticks, last + 1, rest, 0)
        own.wait()
        for i in range(1, seqs):
            piece(i).wait()


def attend_back_step(
    u, between, q_ref, k_ref, v_ref, o_ref, do_ref, pt_ref, x_ref, da_ref, wq_ref, wk_ref, wv_ref,
    grads, g_total, go_total, dx, small_out,
):
    hd = PAIR // 2
    length = q_ref.shape[1]
    count, width = x_ref.shape
    batch = count // length
    quad, row = lax.div(u, batch), lax.rem(u, batch)
    mine = pl.ds(pl.multiple_of(row * length, length), length)
    lane = lax.broadcasted_iota(jnp.int32, (length, PAIR), 1)
    lane8 = lax.broadcasted_iota(jnp.int32, (8, PAIR), 1)
    dqs, dks, dvs = [], [], []
    for pair in range(QUAD // PAIR):
        if pair == 1:
            between()
        at = slice(pair * PAIR, (pair + 1) * PAIR)
        q, k, v, o, do = (ref[0, :, at] for ref in (q_ref, k_ref, v_ref, o_ref, do_ref))
        kt = k.T
        prod = o.astype(F32) * do.astype(F32)
        high = prod.astype(BF)
        low = (prod - high.astype(F32)).astype(BF)
        dk = dv = None
        dqt = []
        for h in range(2):
            here = (lane >= hd) if h else (lane < hd)
            ones = jnp.where((lane8 >= hd) if h else (lane8 < hd), 1.0, 0.0).astype(BF)
            do_h = jnp.where(here, do, 0)
            q_h = jnp.where(here, q, 0)
            mixed = (dot_t(ones, high) + dot_t(ones, low))[0:1]
            pt = pt_ref[0, 2 * pair + h]
            ds = (pt.astype(F32) * (dot_t(v, do_h) - mixed)).astype(BF)
            dv_h, dk_h = dot(pt, do_h), dot(ds, q_h)
            dv = dv_h if dv is None else dv + dv_h
            dk = dk_h if dk is None else dk + dk_h
            dqt.append(dot(kt[h * hd : (h + 1) * hd], ds))
        dqs.append((jnp.concatenate(dqt, axis=0).T * (hd ** (-0.5))).astype(BF))
        dks.append(dk.astype(BF))
        dvs.append(dv.astype(BF))
    d_all = jnp.concatenate(dqs + dks + dvs, axis=1)
    column = jnp.sum(d_all.astype(F32), axis=0, keepdims=True)
    for j in range(width // QUAD):
        @pl.when(quad == j)
        def _(j=j):
            at = slice(j * QUAD, (j + 1) * QUAD)
            small_out[0:1, at] += column[:, 0:QUAD]
            small_out[1:2, at] += column[:, 2 * QUAD :]
    weights = jnp.concatenate([wq_ref[...], wk_ref[...], wv_ref[...]], axis=1)
    d_x = dot_t(d_all, weights)
    g_all = t_dot(x_ref[mine], d_all)
    g_o = t_dot(o_ref[0], da_ref[mine])

    dx[mine] += d_x

    @pl.when(row == 0)
    def _():
        g_total[...] = g_all
        go_total[...] = g_o

    @pl.when((row > 0) & (row < batch - 1))
    def _():
        g_total[...] += g_all
        go_total[...] += g_o

    @pl.when(row == batch - 1)
    def _():
        base = pl.multiple_of(quad * CHUNK, CHUNK)
        grads[pl.ds(base, width)] = (g_total[...] + g_all).astype(BF)
        grads[pl.ds(pl.multiple_of(base + width, QUAD), QUAD)] = (go_total[...] + g_o).astype(BF)


def back(act, df, du, hidden, q, k, v, o, do, pt, x, da, dr, wq, wk, wv, small, devices, rows, seqs):
    batch, length, width = q.shape
    count, ff = act.shape
    quads, outer, inner = width // QUAD, ff // CHUNK, ff // CHUNK
    n = len(bin(devices)) - 3
    before = outer + inner
    of = lambda g: jnp.maximum(g - before, 0)
    quad = pl.BlockSpec((1, length, QUAD), lambda g: (of(g) % batch, 0, of(g) // batch))
    cols = pl.BlockSpec((width, QUAD), lambda g: (0, of(g) // batch))
    heads = QUAD // (width // HEADS)
    vmem = pl.BlockSpec(memory_space=pltpu.VMEM)
    hbm = pl.BlockSpec(memory_space=pl.ANY)
    chunk = lambda first: pl.BlockSpec(
        (count, CHUNK), lambda g: (0, jnp.clip(g - first, 0, ff // CHUNK - 1)), pipeline_mode=pl.Buffered(1)
    )
    landing = []
    for dims, number in (((CHUNK, width), outer), ((width, CHUNK), inner), ((CHUNK, width), quads)):
        sizes = halves(n, dims)
        landing += [pltpu.VMEM((number,) + size, BF) for size in sizes + sizes[-1:]]
    chunks = outer + inner + quads
    return pl.pallas_call(
        functools.partial(back_kernel, rows),
        grid=(before + quads * batch,),
        in_specs=[chunk(0), fixed((count, width)), chunk(outer), fixed((count, width))]
        + [quad] * 5
        + [pl.BlockSpec((1, heads, length, length), lambda g: (of(g) % batch, of(g) // batch, 0, 0)),
           fixed((count, width)), fixed((count, width)), hbm, cols, cols, cols, vmem],
        out_specs=[hbm] * 4 + [vmem],
        out_shape=[
            shape_of((ff, width), BF), shape_of((width, ff), BF), shape_of((quads * CHUNK, width), BF),
            shape_of((batch * seqs, length // seqs, width), BF),
            shape_of(small.shape, F32),
        ],
        scratch_shapes=[
            pltpu.VMEM((ff, width), BF), pltpu.VMEM((width, ff), BF), pltpu.VMEM((quads * CHUNK, width), BF),
            pltpu.VMEM((width, width), F32), pltpu.VMEM((QUAD, width), F32), pltpu.VMEM((count, width), F32),
            pltpu.VMEM((batch, length, width), BF), pltpu.VMEM((2 * n,) + small.shape, F32),
        ] + sems(2 * n, chunks) + sems(n) + sems(seqs - 1)
        + [pltpu.SemaphoreType.DMA((chunks,)), pltpu.SemaphoreType.DMA((2,))] + landing,
        cost_estimate=pl.CostEstimate(
            flops=count * width * (16 * length + 16 * width), bytes_accessed=4 * count * (4 * width + HEADS * length),
            transcendentals=0,
        ),
        compiler_params=pltpu.CompilerParams(
            vmem_limit_bytes=63 << 20, collective_id=2, has_side_effects=True
        ),
    )(act, df, du, hidden, q, k, v, o, do, pt, x, da, dr, wq, wk, wv, small)


def widen_kernel(outer_in, inner_in, attn_in, outer, inner, g_q, g_k, g_v, g_o, read, wide, r_sem, w_sem):
    width, ff = inner.shape
    jobs = []
    for i in range(ff // width):
        at = slice(i * width, (i + 1) * width)
        jobs.append((outer_in.at[at], [(slice(0, width), slice(0, width), outer.at[at])]))
    for i in range(ff // width):
        at = slice(i * width, (i + 1) * width)
        jobs.append((inner_in.at[:, at], [(slice(0, width), slice(0, width), inner.at[:, at])]))
    for j in range(width // QUAD):
        at = slice(j * QUAD, (j + 1) * QUAD)
        parts = [
            (slice(0, width), slice(m * QUAD, (m + 1) * QUAD), g.at[:, at]) for m, g in enumerate((g_q, g_k, g_v))
        ]
        parts.append((slice(width, CHUNK), slice(0, width), g_o.at[at]))
        jobs.append((attn_in.at[j * CHUNK : (j + 1) * CHUNK], parts))

    def reader(i):
        source = jobs[i][0]
        return pltpu.make_async_copy(source, read.at[i % 2, 0 : source.shape[0]], r_sem.at[i % 2])

    def writers(i):
        return [
            pltpu.make_async_copy(wide.at[i % 2, r, c], target, w_sem.at[i % 2, m])
            for m, (r, c, target) in enumerate(jobs[i][1])
        ]

    reader(0).start()
    for i in range(len(jobs)):
        reader(i).wait()
        if i + 1 < len(jobs):
            reader(i + 1).start()
        if i >= 2:
            for copy in writers(i - 2):
                copy.wait()

        def cast(k, carry, i=i):
            at = pl.ds(pl.multiple_of(k * 64, 64), 64)
            wide[i % 2, at] = read[i % 2, at].astype(F32)
            return carry

        lax.fori_loop(0, jobs[i][0].shape[0] // 64, cast, 0)
        for copy in writers(i):
            copy.start()
    for i in (len(jobs) - 2, len(jobs) - 1):
        for copy in writers(i):
            copy.wait()


def widen(outer, inner, attn):
    ff, width = outer.shape
    hbm = pl.BlockSpec(memory_space=pl.ANY)
    square = shape_of((width, width), F32)
    return pl.pallas_call(
        widen_kernel,
        in_specs=[hbm] * 3,
        out_specs=[hbm] * 6,
        out_shape=[shape_of((ff, width), F32), shape_of((width, ff), F32)] + [square] * 4,
        scratch_shapes=[
            pltpu.VMEM((2, CHUNK, width), BF), pltpu.VMEM((2, CHUNK, width), F32),
            pltpu.SemaphoreType.DMA((2,)), pltpu.SemaphoreType.DMA((2, 4)),
        ],
        compiler_params=pltpu.CompilerParams(vmem_limit_bytes=32 << 20),
    )(outer, inner, attn)


def pool_back_kernel(r2_ref, gain_ref, ids_ref, de_ref, dr_ref, df_ref, sum_ref):
    length, width = r2_ref.shape[1:]
    xhat, scale = normalize(r2_ref[0])
    lane = lax.broadcasted_iota(jnp.int32, (length, PAIR), 1)
    hot = (lane % SEG_ROW == ids_ref[0]) & (lane < 3 * SEG_ROW)
    hot = jnp.where(hot, 1.0, 0.0).astype(BF)
    pieces = list(split3(de_ref[0])) + [jnp.zeros((PAIR - 3 * SEG_ROW, width), BF)]
    d_y = dot(hot, jnp.concatenate(pieces, axis=0))
    d_r = norm_back(d_y, gain_ref[...], xhat, scale)
    dr_ref[0] = d_r
    d_f = d_r.astype(BF)
    df_ref[0] = d_f
    sum_ref[0, 0:1] = jnp.sum(d_f.astype(F32), axis=0, keepdims=True)


def pool_back(r2, gain, ids_col, de):
    batch, length, width = r2.shape
    row = pl.BlockSpec((1, length, width), lambda b: (b, 0, 0))
    eight = pl.BlockSpec((1, 8, width), lambda b: (b, 0, 0))
    return call(
        pool_back_kernel,
        (batch,),
        [row, pl.BlockSpec((1, width), lambda b: (0, 0)),
         pl.BlockSpec((1, length, 1), lambda b: (b, 0, 0)),
         pl.BlockSpec((1, SEG_ROW, width), lambda b: (b, 0, 0))],
        [row, row, eight],
        [shape_of(r2.shape, F32), shape_of(r2.shape, BF), shape_of((batch, 8, width), F32)],
        [],
        batch * length * width * 300,
        batch * length * width * 10,
    )(r2, gain, ids_col, de)


def local(
    tokens,
    query_weight,
    query_bias,
    key_weight,
    value_weight,
    value_bias,
    output_weight,
    output_bias,
    attn_gain,
    attn_shift,
    inner_weight,
    inner_bias,
    outer_weight,
    outer_bias,
    ffn_gain,
    ffn_shift,
    segment_ids,
    positives,
):
    group_rows, local_len, width = tokens.shape
    ff = inner_weight.shape[1]
    seqs = lax.axis_size("seq")
    seq, row_place = lax.axis_index("seq"), lax.axis_index("rows")
    batch, length = group_rows // seqs, local_len * seqs
    count = batch * length
    ids = lax.dynamic_slice_in_dim(segment_ids, seq * batch, batch, 0)
    own_segs = batch * SEG_ROW
    own_positives = lax.dynamic_slice_in_dim(positives, seq * own_segs, own_segs, 0)
    own_ids = row_place * positives.shape[0] + seq * own_segs + jnp.arange(own_segs, dtype=jnp.int32)
    tags = jnp.stack([own_positives, own_ids] + [jnp.zeros_like(own_ids)] * (PAIR - 2), axis=1).astype(F32)
    hot = ids[:, :, None] == jnp.arange(PAIR, dtype=jnp.int32)
    real = jnp.arange(PAIR, dtype=jnp.int32) < SEG_ROW
    apart_q = jnp.where(hot, -(2.0**30), 0.0).astype(BF)
    apart_k = jnp.where(hot | ~real, 0.0, 1.0).astype(BF)
    counts = jnp.sum(hot.astype(F32), axis=1)[:, :SEG_ROW].reshape(own_segs, 1)
    vec = lambda v: v.astype(F32).reshape(1, -1)
    flat2 = lambda a: a.reshape(count, a.shape[-1])

    x = lax.all_to_all(tokens, "seq", split_axis=0, concat_axis=1, tiled=True)
    q, k, v, o, pt, r_one = attend(
        x, query_weight, vec(query_bias), key_weight, value_weight, vec(value_bias),
        output_weight, vec(output_bias), apart_q, apart_k,
    )
    hidden, active, slope, r_two, xpool = feed(
        r_one, vec(attn_gain), vec(attn_shift), inner_weight, vec(inner_bias), outer_weight,
        vec(outer_bias), ids.reshape(batch, 1, length),
    )
    xpool = xpool.reshape(own_segs, width)
    rows = lax.axis_size("rows")
    devices = rows * seqs
    d_e, loss_vec = contrast(xpool, vec(ffn_gain), vec(ffn_shift), tags, counts, devices, rows)
    d_two, d_outer, outer_sum = pool_back(
        r_two, vec(ffn_gain), ids.reshape(batch, length, 1), d_e.reshape(batch, SEG_ROW, width)
    )
    d_inner, d_one, d_attn, d_o, row_sums, inner_sum = feed_back(
        d_outer, d_two, slope, outer_weight, inner_weight, r_one, vec(attn_gain), output_weight
    )
    small = jnp.concatenate(
        [
            jnp.zeros((2, width), F32), jnp.sum(row_sums, axis=0)[:3], jnp.sum(outer_sum, axis=0)[:1],
            loss_vec[:3], jnp.sum(inner_sum, axis=0)[0].reshape(-1, width),
        ],
        axis=0,
    )
    small = jnp.pad(small, ((0, -small.shape[0] % 8), (0, 0)))
    *sums, grad_tokens, small = back(
        flat2(active), flat2(d_outer), flat2(d_inner), flat2(hidden), q, k, v, o, d_o, pt, flat2(x),
        flat2(d_attn), flat2(d_one), query_weight, key_weight, value_weight, small, devices, rows, seqs,
    )
    g_outer, g_inner, g_query, g_key, g_value, g_output = widen(*sums)
    return (
        small[8, 0] / (own_segs * devices),
        grad_tokens.astype(F32),
        g_query,
        small[0],
        g_key,
        g_value,
        small[1],
        g_output,
        small[2],
        small[3],
        small[4],
        g_inner,
        small[9 : 9 + ff // width].reshape(-1),
        g_outer,
        small[5],
        small[6],
        small[7],
    )


def solution(mesh):
    placed = (
        (P("rows", "seq", None),) + (P(),) * 15 + (P("rows", None), P("rows"))
    )
    return jax.shard_map(
        local,
        mesh=mesh,
        in_specs=placed,
        out_specs=(P(), P("rows", "seq", None)) + (P(),) * 15,
        check_vma=False,
    )
```

```python
import functools

import jax
import jax.numpy as jnp
from jax import lax
from jax.experimental import pallas as pl
from jax.experimental.pallas import tpu as pltpu
from jax.sharding import PartitionSpec as P

HEADS = 12
SEG_ROW = 8
HIGHEST = lax.Precision.HIGHEST
NORM_EPS = 1e-12
POOL_EPS = 1e-06
INV_TEMPER = 100.0
MASKED = -1000000000.0
INV_ROOT_TWO_PI = 0.3989422804014327
INV_ROOT_TWO = 0.7071067811865476
BF = jnp.bfloat16
F32 = jnp.float32
MESH = pl.DeviceIdType.MESH


def dot(a, b):
    return jnp.dot(a, b, preferred_element_type=F32)


def dot_t(a, b, precision=None):
    return lax.dot_general(
        a, b, (((1,), (1,)), ((), ())), preferred_element_type=F32, precision=precision
    )


def t_dot(a, b):
    return lax.dot_general(a, b, (((0,), (0,)), ((), ())), preferred_element_type=F32)


def normalize(resid):
    center = resid - jnp.mean(resid, axis=-1, keepdims=True)
    spread = jnp.mean(center * center, axis=-1, keepdims=True)
    scale = lax.rsqrt(spread + NORM_EPS)
    return center * scale, scale


def norm_back(grad, gain, xhat, scale):
    q = grad * gain
    return scale * (
        q - jnp.mean(q, axis=-1, keepdims=True) - xhat * jnp.mean(q * xhat, axis=-1, keepdims=True)
    )


def split3(a):
    hi = a.astype(BF)
    rest = a - hi.astype(F32)
    mid = rest.astype(BF)
    return hi, mid, (rest - mid.astype(F32)).astype(BF)


def call(kernel, grid, in_specs, out_specs, out_shape, scratch, flops, moved, vmem=62):
    return pl.pallas_call(
        kernel,
        grid=grid,
        in_specs=in_specs,
        out_specs=out_specs,
        out_shape=out_shape,
        scratch_shapes=scratch,
        cost_estimate=pl.CostEstimate(flops=flops, bytes_accessed=moved, transcendentals=0),
        compiler_params=pltpu.CompilerParams(vmem_limit_bytes=vmem << 20),
    )


def shape_of(dims, dtype):
    return jax.ShapeDtypeStruct(dims, dtype)


PAIR = 128
QUAD = 256


def attend_kernel(
    tokens_ref, wq_ref, wk_ref, wv_ref, wo_ref, bias_ref, row_ref, ids_ref,
    q_ref, k_ref, v_ref, o_ref, pt_ref, r_ref, x_out, x_ref, apart_q, apart_k, send, receive, own_sem,
):
    row, quad = pl.program_id(0), pl.program_id(1)
    batch, length = x_ref.shape[0], x_ref.shape[1]
    part = tokens_ref.shape[1]
    seqs = length // part
    hd = PAIR // 2
    seq, place = lax.axis_index("seq"), lax.axis_index("rows")

    def target(b):
        return x_ref.at[b, pl.ds(pl.multiple_of(seq * part, part), part)]

    def piece(i, b):
        to = lax.rem(seq + i, seqs)
        return remote(
            tokens_ref.at[to * batch + b], target(b), send.at[b, i - 1], receive.at[b, i - 1], (to, place)
        )

    def own(b):
        return pltpu.make_async_copy(tokens_ref.at[seq * batch + b], target(b), own_sem.at[b])

    def keep(b):
        return pltpu.make_async_copy(x_ref.at[b], x_out.at[b], own_sem.at[batch + b])

    @pl.when((row == 0) & (quad == 0))
    def _():
        greet([(lax.rem(seq + i, seqs), place) for i in range(1, seqs)])
        for b in range(batch):
            for i in range(1, seqs):
                piece(i, b).start()
            own(b).start()

    for b in range(batch):
        @pl.when((row == b) & (quad == 0))
        def _(b=b):
            hot = lax.broadcasted_iota(jnp.int32, (PAIR, length), 0) == ids_ref[pl.ds(seq * batch + b, 1), :]
            hot = jnp.where(hot, 1.0, 0.0).T
            real = lax.broadcasted_iota(jnp.int32, (length, PAIR), 1) < SEG_ROW
            apart_q[...] = (hot * -(2.0**30)).astype(BF)
            apart_k[...] = jnp.where(real, 1.0 - hot, 0.0).astype(BF)
            own(b).wait()
            for i in range(1, seqs):
                piece(i, b).wait()
            keep(b).start()

    x = x_ref[row]
    q = (dot(x, wq_ref[...]) + bias_ref[0:1]).astype(BF) * jnp.asarray(hd ** (-0.5), BF)
    k = dot(x, wk_ref[...]).astype(BF)
    v = (dot(x, wv_ref[...]) + bias_ref[1:2]).astype(BF)
    q_ref[0], k_ref[0], v_ref[0] = q, k, v
    lane = lax.broadcasted_iota(jnp.int32, (length, PAIR), 1)
    outs = []
    for pair in range(QUAD // PAIR):
        at = slice(pair * PAIR, (pair + 1) * PAIR)
        keys = jnp.concatenate([k[:, at], apart_k[...]], axis=1)
        vt = v[:, at].T
        parts = []
        for h in range(2):
            mine = (lane >= hd) if h else (lane < hd)
            queries = jnp.concatenate([jnp.where(mine, q[:, at], 0), apart_q[...]], axis=1)
            st = dot_t(keys, queries)
            expo = jnp.exp(st - jnp.max(st, axis=0, keepdims=True))
            pt = (expo * (1.0 / jnp.sum(expo, axis=0, keepdims=True))).astype(BF)
            pt_ref[0, 2 * pair + h] = pt
            parts.append(dot(vt[h * hd : (h + 1) * hd], pt))
        outs.append(jnp.concatenate(parts, axis=0).T)
    o = jnp.concatenate(outs, axis=1).astype(BF)
    o_ref[0] = o
    part_sum = dot(o, wo_ref[...])

    @pl.when(quad == 0)
    def _():
        r_ref[0] = x.astype(F32) + row_ref[2:3] + part_sum

    @pl.when(quad > 0)
    def _():
        r_ref[0] += part_sum

    @pl.when((row == batch - 1) & (quad == pl.num_programs(1) - 1))
    def _():
        for b in range(batch):
            keep(b).wait()


def attend(tokens, wq, wk, wv, wo, vectors, ids, seqs):
    rows, part, width = tokens.shape
    batch, length = rows // seqs, part * seqs
    row = pl.BlockSpec((1, length, width), lambda b, j: (b, 0, 0))
    cols = pl.BlockSpec((width, QUAD), lambda b, j: (0, j))
    quad = pl.BlockSpec((1, length, QUAD), lambda b, j: (b, 0, j))
    heads = QUAD // (width // HEADS)
    vmem = pl.BlockSpec(memory_space=pltpu.VMEM)
    dims = (batch, length, width)
    act = shape_of(dims, BF)
    return pl.pallas_call(
        attend_kernel,
        grid=(batch, width // QUAD),
        in_specs=[pl.BlockSpec(memory_space=pl.ANY), cols, cols, cols,
                  pl.BlockSpec((QUAD, width), lambda b, j: (j, 0)),
                  pl.BlockSpec((8, QUAD), lambda b, j: (0, j)), vmem, vmem],
        out_specs=[quad, quad, quad, quad,
                   pl.BlockSpec((1, heads, length, length), lambda b, j: (b, j, 0, 0)), row,
                   pl.BlockSpec(memory_space=pl.ANY)],
        out_shape=[act, act, act, act, shape_of((batch, HEADS, length, length), BF), shape_of(dims, F32), act],
        scratch_shapes=[pltpu.VMEM(dims, BF)] + [pltpu.VMEM((length, PAIR), BF)] * 2
        + [pltpu.SemaphoreType.DMA((batch, seqs - 1))] * 2 + [pltpu.SemaphoreType.DMA((2 * batch,))],
        cost_estimate=pl.CostEstimate(
            flops=batch * length * width * (8 * width + 8 * length),
            bytes_accessed=batch * length * (14 * width + 2 * HEADS * length) + 8 * width * width,
            transcendentals=0,
        ),
        compiler_params=pltpu.CompilerParams(
            vmem_limit_bytes=62 << 20, collective_id=1, has_side_effects=True
        ),
    )(tokens, wq, wk, wv, wo, vectors, vectors, ids)


def gelu_both(u):
    cdf = 0.5 + 0.5 * lax.erf(u * INV_ROOT_TWO)
    return u * cdf, cdf + (INV_ROOT_TWO_PI * u) * jnp.exp(-0.5 * u * u)


def own_row(ids_ref, b):
    return lax.axis_index("seq") * (ids_ref.shape[0] // lax.axis_size("seq")) + b


FEED_VMEM = 62
FBACK_VMEM = 62


def feed_kernel(
    r_ref, vec_ref, wi_ref, wo_ref, ids_ref,
    h_ref, act_ref, slope_ref, r2_ref, pool_ref, hidden,
):
    step = pl.program_id(0)
    batch = r_ref.shape[0]

    @pl.when(step == 0)
    def _():
        for b in range(batch):
            xhat, _ = normalize(r_ref[b])
            h = xhat * vec_ref[3:4] + vec_ref[4:5]
            hidden[b] = h + vec_ref[5:6]
            h_ref[b] = h.astype(BF)

    bias = vec_ref[pl.ds(8 + step, 1)]
    for b in range(batch):
        act, slope = gelu_both(dot(h_ref[b], wi_ref[...]) + bias)
        act = act.astype(BF)
        act_ref[b] = act
        slope_ref[b] = slope.astype(BF)
        hidden[b] += dot(act, wo_ref[...])

    @pl.when(step == pl.num_programs(0) - 1)
    def _():
        for b in range(batch):
            r2 = hidden[b]
            r2_ref[b] = r2
            xhat, _ = normalize(r2)
            ids = ids_ref[pl.ds(own_row(ids_ref, b), 1)]
            hot = lax.broadcasted_iota(jnp.int32, (SEG_ROW, r2.shape[0]), 0) == ids
            counts = jnp.sum(jnp.where(hot, 1.0, 0.0), axis=1, keepdims=True)
            hot = jnp.where(hot, 1.0, 0.0).astype(BF)
            total = sum(dot(hot, piece) for piece in split3(xhat))
            pool_ref[b] = total / counts


def feed(r, vectors, wi, wo, ids):
    batch, length, width = r.shape
    ff = wi.shape[1]
    whole = pl.BlockSpec(r.shape, lambda c: (0, 0, 0))
    vec = pl.BlockSpec(memory_space=pltpu.VMEM)
    chunk = pl.BlockSpec((batch, length, width), lambda c: (0, 0, c))
    wide = shape_of((batch, length, ff), BF)
    return call(
        feed_kernel,
        (ff // width,),
        [whole, vec, pl.BlockSpec((width, width), lambda c: (0, c)),
         pl.BlockSpec((width, width), lambda c: (c, 0)), vec],
        [whole, chunk, chunk, whole, pl.BlockSpec((batch, SEG_ROW, width), lambda c: (0, 0, 0))],
        [shape_of(r.shape, BF), wide, wide, shape_of(r.shape, F32), shape_of((batch, SEG_ROW, width), F32)],
        [pltpu.VMEM(r.shape, F32)],
        4 * batch * length * width * ff,
        batch * length * (10 * width + 4 * ff) + 4 * width * ff,
        FEED_VMEM,
    )(r, vectors, wi, wo, ids)


def flip(v, step):
    return v + step * (1 - 2 * (v // step % 2))


def links(rows):
    seq, row = lax.axis_index("seq"), lax.axis_index("rows")
    core, y, x = seq % 2, seq // 2 % 2, row % 2
    other = 1 - core
    found = [
        ((flip(seq, 1), row), core),
        ((seq + core * 2 * (1 - 2 * y), row + other * (1 - 2 * x)), core * y + other * x),
        ((seq + other * 2 * (1 - 2 * y), row + core * (1 - 2 * x)), other * y + core * x),
    ]
    step = 2
    while step < rows:
        found.append(((seq, flip(row, step)), row // step % 2))
        step *= 2
    return found


def greet(devices):
    barrier = pltpu.get_barrier_semaphore()
    for device in devices:
        pl.semaphore_signal(barrier, inc=1, device_id=device, device_id_type=MESH)
    pl.semaphore_wait(barrier, len(devices))


def remote(source, target, send, receive, device):
    return pltpu.make_async_remote_copy(
        src_ref=source, dst_ref=target, send_sem=send, recv_sem=receive,
        device_id=device, device_id_type=MESH,
    )


def contrast_kernel(
    rows, xpool_ref, in_ref, ids_ref, positives_ref,
    de_ref, vec_ref, all_ref, lse_ref, send, receive,
):
    own, width = xpool_ref.shape
    total = all_ref.shape[0]
    near = links(rows)
    hops = near[3:][::-1] + near[1:3] + near[:1]
    greet([device for device, _ in hops])
    e_own = xpool_ref[...] * in_ref[6:7] + in_ref[7:8]
    seq = lax.axis_index("seq")
    sub = lax.broadcasted_iota(jnp.int32, (own, PAIR), 0)
    lane = lax.broadcasted_iota(jnp.int32, (own, PAIR), 1)
    first = lax.axis_index("rows") * positives_ref.shape[0] + seq * own
    tag = jnp.where(lane == 1, first + sub, 0)
    for i in range(own):
        tag = jnp.where((lane == 0) & (sub == i), positives_ref[seq * own + i], tag)
    tag = tag.astype(F32)
    all_ref[0:own, 0:width] = e_own
    all_ref[0:own, width:] = tag
    have = own
    for i, (device, _) in enumerate(hops):
        copy = remote(
            all_ref.at[0:have], all_ref.at[have : 2 * have], send.at[i], receive.at[i], device
        )
        copy.start()
        copy.wait()
        have *= 2

    def unit(e):
        rho = lax.rsqrt(jnp.sum(e * e, axis=1, keepdims=True) + POOL_EPS)
        return e * rho, rho

    n_all, _ = unit(all_ref[:, 0:width])
    pick = lax.broadcasted_iota(jnp.int32, (8, PAIR), 0) == lax.broadcasted_iota(jnp.int32, (8, PAIR), 1)
    tags = dot_t(pick.astype(F32), all_ref[:, width:], HIGHEST)
    pos_all, id_all = tags[0:1], tags[1:2]
    block = min(total, 512)
    for b in range(total // block):
        n_b, _ = unit(all_ref[b * block : (b + 1) * block, 0:width])
        c = dot_t(n_all, n_b, HIGHEST) * INV_TEMPER
        i = lax.broadcasted_iota(jnp.int32, c.shape, 0)
        j = lax.broadcasted_iota(jnp.int32, c.shape, 1) + b * block
        c = jnp.where(i == j, MASKED, c)
        top = jnp.max(c, axis=0, keepdims=True)
        lse_ref[:, b * block : (b + 1) * block] = (
            jnp.log(jnp.sum(jnp.exp(c - top), axis=0, keepdims=True)) + top
        )
    n_own, rho = unit(e_own)
    pos_own, id_own = tag[:, 0:1], tag[:, 1:2]
    c = dot_t(n_own, n_all, HIGHEST) * INV_TEMPER
    c = jnp.where(id_own == id_all, MASKED, c)
    top = jnp.max(c, axis=1, keepdims=True)
    lse_own = jnp.log(jnp.sum(jnp.exp(c - top), axis=1, keepdims=True)) + top
    chosen = id_all == pos_own
    picked = jnp.sum(jnp.where(chosen, c, 0.0), axis=1, keepdims=True)
    weight = (
        jnp.exp(c - lse_own)
        + jnp.exp(c - lse_ref[...])
        - jnp.where(chosen, 1.0, 0.0)
        - jnp.where(id_own == pos_all, 1.0, 0.0)
    )
    d_n = INV_TEMPER * jnp.dot(weight, n_all, precision=HIGHEST, preferred_element_type=F32)
    along = jnp.sum(e_own * d_n, axis=1, keepdims=True)
    d_e = rho * d_n - (rho * rho * rho) * e_own * along
    for b in range(own // SEG_ROW):
        ids = ids_ref[pl.ds(own_row(ids_ref, b), 1)]
        hot = lax.broadcasted_iota(jnp.int32, (SEG_ROW, ids.shape[1]), 0) == ids
        at = slice(b * SEG_ROW, (b + 1) * SEG_ROW)
        de_ref[at] = d_e[at] / jnp.sum(jnp.where(hot, 1.0, 0.0), axis=1, keepdims=True)
    vec_ref[0:1] = jnp.sum(d_e * xpool_ref[...], axis=0, keepdims=True)
    vec_ref[1:2] = jnp.sum(d_e, axis=0, keepdims=True)
    vec_ref[2:3] = jnp.broadcast_to(jnp.sum(lse_own - picked), (1, vec_ref.shape[1]))
    vec_ref[3:8] = jnp.zeros((5, vec_ref.shape[1]), F32)


def contrast(xpool, vectors, ids, positives, devices, rows):
    own, width = xpool.shape
    total = own * devices
    vmem = pl.BlockSpec(memory_space=pltpu.VMEM)
    stages = len(bin(devices)) - 3
    return pl.pallas_call(
        functools.partial(contrast_kernel, rows),
        in_specs=[vmem] * 3 + [pl.BlockSpec(memory_space=pltpu.SMEM)],
        out_specs=[vmem, vmem],
        out_shape=[shape_of((own, width), F32), shape_of((8, width), F32)],
        scratch_shapes=[
            pltpu.VMEM((total, width + PAIR), F32),
            pltpu.VMEM((1, total), F32),
            pltpu.SemaphoreType.DMA((stages,)),
            pltpu.SemaphoreType.DMA((stages,)),
        ],
        cost_estimate=pl.CostEstimate(
            flops=12 * total * total * width, bytes_accessed=4 * total * width, transcendentals=0
        ),
        compiler_params=pltpu.CompilerParams(
            vmem_limit_bytes=62 << 20, collective_id=0, has_side_effects=True
        ),
    )(xpool, vectors, ids, positives)


CHUNK = 1024


def halves(steps, dims):
    sizes, (height, wide) = [], dims
    for _ in range(steps):
        if height % 32 == 0:
            height //= 2
        else:
            wide //= 2
        sizes.append((height, wide))
    return sizes


def plan(outer, parts, quads, batch):
    attention = outer + 2 * parts
    return [
        ("ab", 0, 0, outer, 1, 1, (1, 3, 2, 1)),
        ("ab", 1, 0, outer, outer + 4, 2, (1, 3, 2, 1)),
        ("ab", 2, 0, quads, attention + 2 * batch, 2 * batch, (1, 2, 2, 1)),
    ]


def orders(rows):
    near = links(rows)
    seq, row = lax.axis_index("seq"), lax.axis_index("rows")
    along = [((seq, flip(row, 1)), row % 2), ((flip(seq, 2), row), seq // 2 % 2)]
    return {
        "ab": near,
        "xy": near[:1] + along + near[3:],
        "z": near[:1] + near[3:] + near[1:3],
    }


class Chain:
    def __init__(self, order, entry, dims, down, grads, sums, mark, came, piece, send, receive, keep):
        self.first, self.number, self.start, self.period, stretch = entry
        stretch = list(stretch) + [stretch[-1]] * (len(order) - len(stretch))
        self.after = [0]
        for wait in stretch + stretch[::-1]:
            self.after.append(self.after[-1] + wait)
        self.order, self.dims, self.down = order, dims, down
        self.grads, self.sums, self.mark = grads, sums, mark
        self.came, self.piece = came, piece
        self.send, self.receive, self.keep = send, receive, keep
        self.sizes = halves(len(order), dims)
        self.last = self.start + (self.number - 1) * self.period + self.after[-1]

    def places(self, chunk):
        row, column = (chunk * self.dims[0], 0) if self.down else (0, chunk * self.dims[1])
        before = self.dims[0]
        found = []
        for (height, wide), (_, bit) in zip(self.sizes, self.order):
            if height < before:
                kept = (row + bit * height, column)
                sent = (row + (1 - bit) * height, column)
            else:
                kept = (row, column + bit * wide)
                sent = (row, column + (1 - bit) * wide)
            found.append((kept, sent))
            (row, column), before = kept, height
        return found

    def at(self, ref, place, size):
        row, column = place
        return ref.at[
            pl.ds(pl.multiple_of(row, 16), size[0]), pl.ds(pl.multiple_of(column, PAIR), size[1])
        ]

    def copy(self, chunk, places, stage):
        n = len(self.order)
        i = stage if stage < n else 2 * n - 1 - stage
        kept, sent = places[i]
        size, device = self.sizes[i], self.order[i][0]
        mark = chunk + self.mark
        pair = self.send.at[stage, mark], self.receive.at[stage, mark]
        if stage < n:
            return remote(self.at(self.grads, sent, size), self.came[i].at[chunk], *pair, device)
        target = self.at(self.sums, kept, size)
        return remote(self.piece.at[chunk] if stage == n else target, target, *pair, device)

    def own(self, chunk, places):
        target = self.at(self.sums, places[-1][0], self.sizes[-1])
        return pltpu.make_async_copy(self.piece.at[chunk], target, self.keep.at[chunk + self.mark])

    def step(self, t):
        for stage in range(2 * len(self.order), -1, -1):
            since = t - self.after[stage] - self.start
            if self.number == 1:
                pl.when(since == 0)(functools.partial(self.advance, stage, self.first))
                continue
            index = since // self.period if self.period > 1 else since
            here = (since >= 0) & (index < self.number)
            if self.period > 1:
                here &= since % self.period == 0
            pl.when(here)(functools.partial(self.advance, stage, index + self.first))

    def advance(self, stage, chunk):
        n = len(self.order)
        places = self.places(chunk)
        if stage > 0:
            self.copy(chunk, places, stage - 1).wait()
        if 0 < stage <= n:
            height, wide = self.sizes[stage - 1]
            row, column = places[stage - 1][0]
            tile = 16 if height % 32 else 32

            def add(k, carry):
                at = pl.ds(pl.multiple_of(k * tile, 16), tile)
                mine = self.at(self.grads, (row + k * tile, column), (tile, wide))
                total = (mine[...].astype(F32) + self.came[stage - 1][chunk, at].astype(F32)).astype(BF)
                if stage < n:
                    mine[...] = total
                else:
                    self.piece[chunk, at] = total
                return carry

            lax.fori_loop(0, height // tile, add, 0)
        if stage == n:
            self.own(chunk, places).start()
        if stage == n + 1:
            self.own(chunk, places).wait()
        if stage < 2 * n:
            self.copy(chunk, places, stage).start()


def sems(*dims):
    return [pltpu.SemaphoreType.DMA(dims)] * 2


FEED_BUFFERS = 1
WEIGHT_BUFFERS = 1


def fixed(dims):
    return pl.BlockSpec(dims, lambda g: (0,) * len(dims), pipeline_mode=pl.Buffered(1))


def pool_back_step(ids, d_e, gain, resid):
    length, width = resid.shape
    xhat, scale = normalize(resid)
    sub = lax.broadcasted_iota(jnp.int32, (PAIR, length), 0)
    hot = (sub % SEG_ROW == ids) & (sub < 3 * SEG_ROW)
    hot = jnp.where(hot, 1.0, 0.0).T.astype(BF)
    pieces = list(split3(d_e)) + [jnp.zeros((PAIR - 3 * SEG_ROW, width), BF)]
    d_y = dot(hot, jnp.concatenate(pieces, axis=0))
    return norm_back(d_y, gain, xhat, scale)


def back_kernel(rows, *refs):
    (r2_ref, r1_ref, de_ref, vec_ref, ids_ref, loss_ref, act_ref, slope_ref, wo_ref, wi_ref, h_ref, wa_ref,
     q_ref, k_ref, v_ref, o_ref, pt_ref, x_ref, wq_ref, wk_ref, wv_ref) = refs[:21]
    sums, (token_out, small_out) = refs[21:24], refs[24:26]
    (g_outer, g_inner, g_attn, g_total, dx, d_f, d_u, d_a, d_o, hx, small_came, send, receive, s_send,
     s_receive, t_send, t_receive, keep, other) = refs[26:45]
    landing = refs[45:]
    step = pl.program_id(0)
    length = q_ref.shape[1]
    count, width = dx.shape
    batch = count // length
    outer, parts = sums[0].shape[0] // CHUNK, sums[1].shape[1] // width
    quads = width // QUAD
    kinds = orders(rows)
    near = kinds["ab"]
    n = len(near)
    seq, row_place = lax.axis_index("seq"), lax.axis_index("rows")
    seqs = token_out.shape[0] // batch
    part = length // seqs
    groups = [
        ((CHUNK, width), True, g_outer, sums[0], 0),
        ((width, CHUNK), False, g_inner, sums[1], outer),
        ((CHUNK, width), True, g_attn, sums[2], 2 * outer),
    ]
    chains = []
    for kind, group, *entry in plan(outer, parts, quads, batch):
        came = landing[group * (n + 1) : group * (n + 1) + n]
        piece = landing[group * (n + 1) + n]
        chains.append(Chain(kinds[kind], entry, *groups[group], came, piece, send, receive, keep))
    before = outer + parts
    ticks = outer + 2 * (parts + quads * batch)
    last = max(max(chain.last for chain in chains), ticks + n)
    p = jnp.clip(step - outer, 0, parts - 1)
    u = jnp.maximum(step - before, 0)
    now = step + jnp.maximum(step - outer, 0)

    def tick(t):
        for chain in chains:
            chain.step(t)

    def piece(i, b):
        to = lax.rem(seq + i, seqs)
        return remote(
            d_u.at[pl.ds(pl.multiple_of(b * length + to * part, part), part)],
            token_out.at[seq * batch + b],
            t_send.at[b, i - 1], t_receive.at[b, i - 1], (to, row_place),
        )

    def own_piece(b):
        return pltpu.make_async_copy(
            d_u.at[pl.ds(pl.multiple_of(b * length + seq * part, part), part)],
            token_out.at[seq * batch + b], other.at[3 + b],
        )

    def small_copy(i):
        source = small_out if i == 0 else small_came.at[n + i - 1]
        return remote(source, small_came.at[i], s_send.at[i], s_receive.at[i], near[i][0])

    load_r2 = pltpu.make_async_copy(r2_ref, dx, other.at[0])
    load_r1 = pltpu.make_async_copy(r1_ref, g_total, other.at[2])
    load_h = pltpu.make_async_copy(h_ref, hx, other.at[1])
    load_x = pltpu.make_async_copy(x_ref, hx, other.at[1])

    @pl.when(step == 0)
    def _():
        load_r2.start()
        load_r1.start()
        load_h.start()
        greet([device for device, _ in near] + [(flip(flip(seq, 1), 2), row_place)])
        small_out[...] = jnp.zeros_like(small_out)
        small_out[6:9] = loss_ref[0:3]
        load_r2.wait()
        for b in range(batch):
            at = slice(b * length, (b + 1) * length)
            ids = ids_ref[pl.ds(own_row(ids_ref, b), 1)]
            d_r = pool_back_step(ids, de_ref[b], vec_ref[6:7], dx[at])
            dx[at] = d_r
            low = d_r.astype(BF)
            d_f[at] = low
            small_out[5:6] += jnp.sum(low.astype(F32), axis=0, keepdims=True)

    tick(now)

    @pl.when(step < outer)
    def _():
        at = pl.ds(pl.multiple_of(step * CHUNK, CHUNK), CHUNK)
        g_outer[at] = t_dot(act_ref[...], d_f[...]).astype(BF)

    @pl.when(step == outer)
    def _():
        load_h.wait()

    @pl.when((step >= outer) & (step < before))
    def _():
        for b in range(batch):
            at = slice(b * length, (b + 1) * length)
            low = (dot_t(d_f[at], wo_ref[...]) * slope_ref[at].astype(F32)).astype(BF)
            d_u[at] = low
            small_out[pl.ds(9 + p, 1)] += jnp.sum(low.astype(F32), axis=0, keepdims=True)
            dx[at] += dot_t(low, wi_ref[...])
        tick(now + 1)
        at = pl.ds(pl.multiple_of(p * width, width), width)
        g_inner[:, at] = t_dot(hx[...], d_u[...]).astype(BF)

    @pl.when(step == before - 1)
    def _():
        load_x.start()
        load_r1.wait()
        for b in range(batch):
            at = slice(b * length, (b + 1) * length)
            d_h = dx[at]
            xhat, scale = normalize(g_total[at])
            d_r = norm_back(d_h, vec_ref[3:4], xhat, scale)
            dx[at] = d_r
            low = d_r.astype(BF)
            d_a[at] = low
            d_o[at] = dot_t(low, wa_ref[...]).astype(BF)
            small_out[2:3] += jnp.sum(low.astype(F32), axis=0, keepdims=True)
            small_out[3:4] += jnp.sum(d_h * xhat, axis=0, keepdims=True)
            small_out[4:5] += jnp.sum(d_h, axis=0, keepdims=True)

    @pl.when(step == before)
    def _():
        load_x.wait()

    @pl.when(step >= before)
    def _():
        attend_back_step(
            u, lambda: tick(now + 1), q_ref, k_ref, v_ref, o_ref, d_o, pt_ref, hx, d_a,
            wq_ref, wk_ref, wv_ref, g_attn, g_total, dx, small_out,
        )

    @pl.when(step == pl.num_programs(0) - 1)
    def _():
        d_u[...] = dx[...].astype(BF)
        for b in range(batch):
            for i in range(1, seqs):
                piece(i, b).start()
            own_piece(b).start()

        def rest(t, carry):
            tick(t)
            for i in range(n + 1):
                @pl.when(t == ticks + i)
                def _(i=i):
                    if i > 0:
                        small_copy(i - 1).wait()
                        held = small_out if i == 1 else small_came.at[n + i - 2]
                        after = small_out if i == n else small_came.at[n + i - 1]
                        after[...] = held[...] + small_came[i - 1]
                    if i < n:
                        small_copy(i).start()
            return carry

        lax.fori_loop(ticks, last + 1, rest, 0)
        for b in range(batch):
            own_piece(b).wait()
            for i in range(1, seqs):
                piece(i, b).wait()


def attend_back_step(
    u, between, q_ref, k_ref, v_ref, o_ref, d_o, pt_ref, x_ref, da_ref, wq_ref, wk_ref, wv_ref,
    grads, g_total, dx, small_out,
):
    hd = PAIR // 2
    length = q_ref.shape[1]
    count, width = x_ref.shape
    batch = count // length
    quad, row = lax.div(u, batch), lax.rem(u, batch)
    mine = pl.ds(pl.multiple_of(row * length, length), length)
    lane = lax.broadcasted_iota(jnp.int32, (length, PAIR), 1)
    lane8 = lax.broadcasted_iota(jnp.int32, (8, PAIR), 1)
    dqs, dks, dvs = [], [], []
    for pair in range(QUAD // PAIR):
        if pair == 1:
            between()
        at = slice(pair * PAIR, (pair + 1) * PAIR)
        q, k, v, o = (ref[0, :, at] for ref in (q_ref, k_ref, v_ref, o_ref))
        do = d_o[mine, pl.ds(pl.multiple_of(quad * QUAD + pair * PAIR, PAIR), PAIR)]
        kt = k.T
        prod = o.astype(F32) * do.astype(F32)
        high = prod.astype(BF)
        low = (prod - high.astype(F32)).astype(BF)
        dk = dv = None
        dqt = []
        for h in range(2):
            here = (lane >= hd) if h else (lane < hd)
            ones = jnp.where((lane8 >= hd) if h else (lane8 < hd), 1.0, 0.0).astype(BF)
            do_h = jnp.where(here, do, 0)
            q_h = jnp.where(here, q, 0)
            mixed = (dot_t(ones, high) + dot_t(ones, low))[0:1]
            pt = pt_ref[0, 2 * pair + h]
            ds = (pt.astype(F32) * (dot_t(v, do_h) - mixed)).astype(BF)
            dv_h, dk_h = dot(pt, do_h), dot(ds, q_h)
            dv = dv_h if dv is None else dv + dv_h
            dk = dk_h if dk is None else dk + dk_h
            dqt.append(dot(kt[h * hd : (h + 1) * hd], ds))
        dqs.append((jnp.concatenate(dqt, axis=0).T * (hd ** (-0.5))).astype(BF))
        dks.append(dk.astype(BF))
        dvs.append(dv.astype(BF))
    d_all = jnp.concatenate(dqs + dks + dvs, axis=1)
    column = jnp.sum(d_all.astype(F32), axis=0, keepdims=True)
    for j in range(width // QUAD):
        @pl.when(quad == j)
        def _(j=j):
            at = slice(j * QUAD, (j + 1) * QUAD)
            small_out[0:1, at] += column[:, 0:QUAD]
            small_out[1:2, at] += column[:, 2 * QUAD :]
    weights = jnp.concatenate([wq_ref[...], wk_ref[...], wv_ref[...]], axis=1)
    d_x = dot_t(d_all, weights)
    g_all = t_dot(x_ref[mine], d_all)
    g_o = t_dot(o_ref[0], da_ref[mine])

    dx[mine] += d_x

    top, bottom = slice(0, width), slice(width, width + QUAD)

    @pl.when(row == 0)
    def _():
        g_total[top] = g_all
        g_total[bottom] = g_o

    @pl.when((row > 0) & (row < batch - 1))
    def _():
        g_total[top] += g_all
        g_total[bottom] += g_o

    @pl.when(row == batch - 1)
    def _():
        base = pl.multiple_of(quad * CHUNK, CHUNK)
        grads[pl.ds(base, width)] = (g_total[top] + g_all).astype(BF)
        grads[pl.ds(pl.multiple_of(base + width, QUAD), QUAD)] = (g_total[bottom] + g_o).astype(BF)


def back(r2, r1, de, vectors, ids, loss, act, slope, wo, wi, hidden, wa, q, k, v, o, pt, x, wq, wk, wv,
         devices, rows, seqs):
    batch, length, width = q.shape
    count, ff = act.shape
    quads, outer, parts = width // QUAD, ff // CHUNK, ff // width
    n = len(bin(devices)) - 3
    before = outer + parts
    of = lambda g: jnp.maximum(g - before, 0)
    at = lambda g: jnp.clip(g - outer, 0, parts - 1)
    quad = pl.BlockSpec((1, length, QUAD), lambda g: (of(g) % batch, 0, of(g) // batch))
    cols = pl.BlockSpec((width, QUAD), lambda g: (0, of(g) // batch), pipeline_mode=pl.Buffered(WEIGHT_BUFFERS))
    heads = QUAD // (width // HEADS)
    vmem = pl.BlockSpec(memory_space=pltpu.VMEM)
    hbm = pl.BlockSpec(memory_space=pl.ANY)
    one = pl.Buffered(1)
    landing = []
    for dims, number in (((CHUNK, width), outer), ((width, CHUNK), outer), ((CHUNK, width), quads)):
        sizes = halves(n, dims)
        landing += [pltpu.VMEM((number,) + size, BF) for size in sizes + sizes[-1:]]
    chunks = 2 * outer + quads
    small = shape_of((-(-(9 + parts) // 8) * 8, width), F32)
    return pl.pallas_call(
        functools.partial(back_kernel, rows),
        grid=(before + quads * batch,),
        in_specs=[
            hbm, hbm, vmem, vmem, vmem, vmem,
            pl.BlockSpec((count, CHUNK), lambda g: (0, jnp.clip(g, 0, outer - 1)), pipeline_mode=one),
            pl.BlockSpec((count, width), lambda g: (0, at(g)), pipeline_mode=one),
            pl.BlockSpec((width, width), lambda g: (at(g), 0), pipeline_mode=pl.Buffered(FEED_BUFFERS)),
            pl.BlockSpec((width, width), lambda g: (0, at(g)), pipeline_mode=pl.Buffered(FEED_BUFFERS)),
            hbm, fixed((width, width)),
            quad, quad, quad, quad,
            pl.BlockSpec((1, heads, length, length), lambda g: (of(g) % batch, of(g) // batch, 0, 0)),
            hbm, cols, cols, cols,
        ],
        out_specs=[hbm] * 4 + [vmem],
        out_shape=[
            shape_of((ff, width), BF), shape_of((width, ff), BF), shape_of((quads * CHUNK, width), BF),
            shape_of((batch * seqs, length // seqs, width), BF), small,
        ],
        scratch_shapes=[
            pltpu.VMEM((ff, width), BF), pltpu.VMEM((width, ff), BF), pltpu.VMEM((quads * CHUNK, width), BF),
            pltpu.VMEM((count, width), F32), pltpu.VMEM((count, width), F32),
        ] + [pltpu.VMEM((count, width), BF)] * 4 + [
            pltpu.VMEM((count, width), BF), pltpu.VMEM((2 * n,) + small.shape, F32),
        ] + sems(2 * n, chunks) + sems(n) + sems(batch, seqs - 1)
        + [pltpu.SemaphoreType.DMA((chunks,)), pltpu.SemaphoreType.DMA((3 + batch,))] + landing,
        cost_estimate=pl.CostEstimate(
            flops=count * width * (16 * length + 16 * width), bytes_accessed=4 * count * (4 * width + HEADS * length),
            transcendentals=0,
        ),
        compiler_params=pltpu.CompilerParams(
            vmem_limit_bytes=63 << 20, collective_id=2, has_side_effects=True
        ),
    )(r2, r1, de, vectors, ids, loss, act, slope, wo, wi, hidden, wa, q, k, v, o, pt, x, wq, wk, wv)


RING = 4


def widen_kernel(outer_in, inner_in, attn_in, token_in, outer, inner, g_q, g_k, g_v, g_o, g_tok, read, wide, r_sem, w_sem):
    width, ff = inner.shape
    jobs = []
    for i in range(ff // width):
        at = slice(i * width, (i + 1) * width)
        jobs.append((outer_in.at[at], [(slice(0, width), slice(0, width), outer.at[at])]))
    for i in range(ff // width):
        at = slice(i * width, (i + 1) * width)
        jobs.append((inner_in.at[:, at], [(slice(0, width), slice(0, width), inner.at[:, at])]))
    for j in range(width // QUAD):
        at = slice(j * QUAD, (j + 1) * QUAD)
        parts = [
            (slice(0, width), slice(m * QUAD, (m + 1) * QUAD), g.at[:, at]) for m, g in enumerate((g_q, g_k, g_v))
        ]
        parts.append((slice(width, CHUNK), slice(0, width), g_o.at[at]))
        jobs.append((attn_in.at[j * CHUNK : (j + 1) * CHUNK], parts))

    for at in range(0, g_tok.shape[0], CHUNK):
        at = slice(at, at + CHUNK)
        jobs.append((token_in.at[at], [(slice(0, CHUNK), slice(0, width), g_tok.at[at])]))

    def reader(i):
        source = jobs[i][0]
        return pltpu.make_async_copy(source, read.at[i % RING, 0 : source.shape[0]], r_sem.at[i % RING])

    def writers(i):
        return [
            pltpu.make_async_copy(wide.at[i % RING, r, c], target, w_sem.at[i % RING, m])
            for m, (r, c, target) in enumerate(jobs[i][1])
        ]

    for i in range(RING - 1):
        reader(i).start()
    for i in range(len(jobs)):
        reader(i).wait()
        if i + RING - 1 < len(jobs):
            reader(i + RING - 1).start()
        if i >= RING:
            for copy in writers(i - RING):
                copy.wait()

        def cast(k, carry, i=i):
            at = pl.ds(pl.multiple_of(k * 64, 64), 64)
            wide[i % RING, at] = read[i % RING, at].astype(F32)
            return carry

        lax.fori_loop(0, jobs[i][0].shape[0] // 64, cast, 0)
        for copy in writers(i):
            copy.start()
    for i in range(len(jobs) - RING, len(jobs)):
        for copy in writers(i):
            copy.wait()


def widen(outer, inner, attn, tokens):
    ff, width = outer.shape
    hbm = pl.BlockSpec(memory_space=pl.ANY)
    square = shape_of((width, width), F32)
    return pl.pallas_call(
        widen_kernel,
        in_specs=[hbm] * 4,
        out_specs=[hbm] * 7,
        out_shape=[shape_of((ff, width), F32), shape_of((width, ff), F32)] + [square] * 4
        + [shape_of(tokens.shape, F32)],
        scratch_shapes=[
            pltpu.VMEM((RING, CHUNK, width), BF), pltpu.VMEM((RING, CHUNK, width), F32),
            pltpu.SemaphoreType.DMA((RING,)), pltpu.SemaphoreType.DMA((RING, 4)),
        ],
        compiler_params=pltpu.CompilerParams(vmem_limit_bytes=62 << 20),
    )(outer, inner, attn, tokens)


def local(
    tokens,
    query_weight,
    query_bias,
    key_weight,
    value_weight,
    value_bias,
    output_weight,
    output_bias,
    attn_gain,
    attn_shift,
    inner_weight,
    inner_bias,
    outer_weight,
    outer_bias,
    ffn_gain,
    ffn_shift,
    segment_ids,
    positives,
):
    group_rows, local_len, width = tokens.shape
    ff = inner_weight.shape[1]
    seqs = lax.axis_size("seq")
    batch, length = group_rows // seqs, local_len * seqs
    count = batch * length
    own_segs = batch * SEG_ROW
    rows = lax.axis_size("rows")
    devices = rows * seqs
    flat2 = lambda a: a.reshape(count, a.shape[-1])
    lines = [query_bias, value_bias, output_bias, attn_gain, attn_shift, outer_bias, ffn_gain, ffn_shift]
    lines += [inner_bias[i * width : (i + 1) * width] for i in range(ff // width)]
    place = lax.broadcasted_iota(jnp.int32, (-(-len(lines) // 8) * 8, width), 0)
    vectors = jnp.zeros(place.shape, F32)
    for i, line in enumerate(lines):
        vectors = jnp.where(place == i, line.astype(F32)[None, :], vectors)

    q, k, v, o, pt, r_one, x = attend(
        tokens, query_weight, key_weight, value_weight, output_weight, vectors, segment_ids, seqs
    )
    hidden, active, slope, r_two, xpool = feed(r_one, vectors, inner_weight, outer_weight, segment_ids)
    d_e, loss_vec = contrast(
        xpool.reshape(own_segs, width), vectors, segment_ids, positives, devices, rows
    )
    *sums, grad_tokens, small = back(
        flat2(r_two), flat2(r_one), d_e.reshape(batch, SEG_ROW, width), vectors, segment_ids, loss_vec,
        flat2(active), flat2(slope), outer_weight, inner_weight, flat2(hidden), output_weight,
        q, k, v, o, pt, flat2(x), query_weight, key_weight, value_weight, devices, rows, seqs,
    )
    g_outer, g_inner, g_query, g_key, g_value, g_output, g_tokens = widen(
        *sums, grad_tokens.reshape(count, width)
    )
    return (
        small[8, 0] / (own_segs * devices),
        g_tokens.reshape(tokens.shape),
        g_query,
        small[0],
        g_key,
        g_value,
        small[1],
        g_output,
        small[2],
        small[3],
        small[4],
        g_inner,
        small[9 : 9 + ff // width].reshape(-1),
        g_outer,
        small[5],
        small[6],
        small[7],
    )


def solution(mesh):
    placed = (
        (P("rows", "seq", None),) + (P(),) * 15 + (P("rows", None), P("rows"))
    )
    return jax.shard_map(
        local,
        mesh=mesh,
        in_specs=placed,
        out_specs=(P(), P("rows", "seq", None)) + (P(),) * 15,
        check_vma=False,
    )
```

```python
import functools

import jax
import jax.numpy as jnp
from jax import lax
from jax.experimental import pallas as pl
from jax.experimental.pallas import tpu as pltpu
from jax.sharding import PartitionSpec as P

HEADS = 12
SEG_ROW = 8
HIGHEST = lax.Precision.HIGHEST
NORM_EPS = 1e-12
POOL_EPS = 1e-06
INV_TEMPER = 100.0
MASKED = -1000000000.0
INV_ROOT_TWO_PI = 0.3989422804014327
INV_ROOT_TWO = 0.7071067811865476
BF = jnp.bfloat16
F32 = jnp.float32
MESH = pl.DeviceIdType.MESH


def dot(a, b):
    return jnp.dot(a, b, preferred_element_type=F32)


def dot_t(a, b, precision=None):
    return lax.dot_general(
        a, b, (((1,), (1,)), ((), ())), preferred_element_type=F32, precision=precision
    )


def t_dot(a, b):
    return lax.dot_general(a, b, (((0,), (0,)), ((), ())), preferred_element_type=F32)


def normalize(resid):
    center = resid - jnp.mean(resid, axis=-1, keepdims=True)
    spread = jnp.mean(center * center, axis=-1, keepdims=True)
    scale = lax.rsqrt(spread + NORM_EPS)
    return center * scale, scale


def norm_back(grad, gain, xhat, scale):
    q = grad * gain
    return scale * (
        q - jnp.mean(q, axis=-1, keepdims=True) - xhat * jnp.mean(q * xhat, axis=-1, keepdims=True)
    )


def split3(a):
    hi = a.astype(BF)
    rest = a - hi.astype(F32)
    mid = rest.astype(BF)
    return hi, mid, (rest - mid.astype(F32)).astype(BF)


def call(kernel, grid, in_specs, out_specs, out_shape, scratch, flops, moved, vmem=62):
    return pl.pallas_call(
        kernel,
        grid=grid,
        in_specs=in_specs,
        out_specs=out_specs,
        out_shape=out_shape,
        scratch_shapes=scratch,
        cost_estimate=pl.CostEstimate(flops=flops, bytes_accessed=moved, transcendentals=0),
        compiler_params=pltpu.CompilerParams(vmem_limit_bytes=vmem << 20),
    )


def shape_of(dims, dtype):
    return jax.ShapeDtypeStruct(dims, dtype)


PAIR = 128
QUAD = 256


def attend_kernel(
    tokens_ref, wq_ref, wk_ref, wv_ref, wo_ref, bias_ref, row_ref, ids_ref,
    q_ref, k_ref, v_ref, o_ref, pt_ref, r_ref, x_out, x_ref, apart_q, apart_k, send, receive, own_sem,
):
    row, quad = pl.program_id(0), pl.program_id(1)
    batch, length = x_ref.shape[0], x_ref.shape[1]
    part = tokens_ref.shape[1]
    seqs = length // part
    hd = PAIR // 2
    seq, place = lax.axis_index("seq"), lax.axis_index("rows")

    def target(b):
        return x_ref.at[b, pl.ds(pl.multiple_of(seq * part, part), part)]

    def piece(i, b):
        to = lax.rem(seq + i, seqs)
        return remote(
            tokens_ref.at[to * batch + b], target(b), send.at[b, i - 1], receive.at[b, i - 1], (to, place)
        )

    def own(b):
        return pltpu.make_async_copy(tokens_ref.at[seq * batch + b], target(b), own_sem.at[b])

    def keep(b):
        return pltpu.make_async_copy(x_ref.at[b], x_out.at[b], own_sem.at[batch + b])

    @pl.when((row == 0) & (quad == 0))
    def _():
        greet([(lax.rem(seq + i, seqs), place) for i in range(1, seqs)])
        for b in range(batch):
            for i in range(1, seqs):
                piece(i, b).start()
            own(b).start()

    for b in range(batch):
        @pl.when((row == b) & (quad == 0))
        def _(b=b):
            hot = lax.broadcasted_iota(jnp.int32, (PAIR, length), 0) == ids_ref[pl.ds(seq * batch + b, 1), :]
            hot = jnp.where(hot, 1.0, 0.0).T
            real = lax.broadcasted_iota(jnp.int32, (length, PAIR), 1) < SEG_ROW
            apart_q[...] = (hot * -(2.0**30)).astype(BF)
            apart_k[...] = jnp.where(real, 1.0 - hot, 0.0).astype(BF)
            own(b).wait()
            for i in range(1, seqs):
                piece(i, b).wait()
            keep(b).start()

    x = x_ref[row]
    q = (dot(x, wq_ref[...]) + bias_ref[0:1]).astype(BF) * jnp.asarray(hd ** (-0.5), BF)
    k = dot(x, wk_ref[...]).astype(BF)
    v = (dot(x, wv_ref[...]) + bias_ref[1:2]).astype(BF)
    q_ref[0], k_ref[0], v_ref[0] = q, k, v
    lane = lax.broadcasted_iota(jnp.int32, (length, PAIR), 1)
    outs = []
    for pair in range(QUAD // PAIR):
        at = slice(pair * PAIR, (pair + 1) * PAIR)
        keys = jnp.concatenate([k[:, at], apart_k[...]], axis=1)
        vt = v[:, at].T
        parts = []
        for h in range(2):
            mine = (lane >= hd) if h else (lane < hd)
            queries = jnp.concatenate([jnp.where(mine, q[:, at], 0), apart_q[...]], axis=1)
            st = dot_t(keys, queries)
            expo = jnp.exp(st - jnp.max(st, axis=0, keepdims=True))
            pt = (expo * (1.0 / jnp.sum(expo, axis=0, keepdims=True))).astype(BF)
            pt_ref[0, 2 * pair + h] = pt
            parts.append(dot(vt[h * hd : (h + 1) * hd], pt))
        outs.append(jnp.concatenate(parts, axis=0).T)
    o = jnp.concatenate(outs, axis=1).astype(BF)
    o_ref[0] = o
    part_sum = dot(o, wo_ref[...])

    @pl.when(quad == 0)
    def _():
        r_ref[0] = x.astype(F32) + row_ref[2:3] + part_sum

    @pl.when(quad > 0)
    def _():
        r_ref[0] += part_sum

    @pl.when((row == batch - 1) & (quad == pl.num_programs(1) - 1))
    def _():
        for b in range(batch):
            keep(b).wait()


def attend(tokens, wq, wk, wv, wo, vectors, ids, seqs):
    rows, part, width = tokens.shape
    batch, length = rows // seqs, part * seqs
    row = pl.BlockSpec((1, length, width), lambda b, j: (b, 0, 0))
    cols = pl.BlockSpec((width, QUAD), lambda b, j: (0, j))
    quad = pl.BlockSpec((1, length, QUAD), lambda b, j: (b, 0, j))
    heads = QUAD // (width // HEADS)
    vmem = pl.BlockSpec(memory_space=pltpu.VMEM)
    dims = (batch, length, width)
    act = shape_of(dims, BF)
    return pl.pallas_call(
        attend_kernel,
        grid=(batch, width // QUAD),
        in_specs=[pl.BlockSpec(memory_space=pl.ANY), cols, cols, cols,
                  pl.BlockSpec((QUAD, width), lambda b, j: (j, 0)),
                  pl.BlockSpec((8, QUAD), lambda b, j: (0, j)), vmem, vmem],
        out_specs=[quad, quad, quad, quad,
                   pl.BlockSpec((1, heads, length, length), lambda b, j: (b, j, 0, 0)), row,
                   pl.BlockSpec(memory_space=pl.ANY)],
        out_shape=[act, act, act, act, shape_of((batch, HEADS, length, length), BF), shape_of(dims, F32), act],
        scratch_shapes=[pltpu.VMEM(dims, BF)] + [pltpu.VMEM((length, PAIR), BF)] * 2
        + [pltpu.SemaphoreType.DMA((batch, seqs - 1))] * 2 + [pltpu.SemaphoreType.DMA((2 * batch,))],
        cost_estimate=pl.CostEstimate(
            flops=batch * length * width * (8 * width + 8 * length),
            bytes_accessed=batch * length * (14 * width + 2 * HEADS * length) + 8 * width * width,
            transcendentals=0,
        ),
        compiler_params=pltpu.CompilerParams(
            vmem_limit_bytes=62 << 20, collective_id=1, has_side_effects=True
        ),
    )(tokens, wq, wk, wv, wo, vectors, vectors, ids)


def gelu_both(u):
    cdf = 0.5 + 0.5 * lax.erf(u * INV_ROOT_TWO)
    return u * cdf, cdf + (INV_ROOT_TWO_PI * u) * jnp.exp(-0.5 * u * u)


def own_row(ids_ref, b):
    return lax.axis_index("seq") * (ids_ref.shape[0] // lax.axis_size("seq")) + b


FEED_VMEM = 62
FBACK_VMEM = 62


def feed_kernel(
    r_ref, vec_ref, wi_ref, wo_ref, ids_ref,
    h_ref, act_ref, slope_ref, r2_ref, pool_ref, hidden,
):
    step = pl.program_id(0)
    batch = r_ref.shape[0]

    @pl.when(step == 0)
    def _():
        for b in range(batch):
            xhat, _ = normalize(r_ref[b])
            h = xhat * vec_ref[3:4] + vec_ref[4:5]
            hidden[b] = h + vec_ref[5:6]
            h_ref[b] = h.astype(BF)

    bias = vec_ref[pl.ds(8 + step, 1)]
    for b in range(batch):
        act, slope = gelu_both(dot(h_ref[b], wi_ref[...]) + bias)
        act = act.astype(BF)
        act_ref[b] = act
        slope_ref[b] = slope.astype(BF)
        hidden[b] += dot(act, wo_ref[...])

    @pl.when(step == pl.num_programs(0) - 1)
    def _():
        for b in range(batch):
            r2 = hidden[b]
            r2_ref[b] = r2
            xhat, _ = normalize(r2)
            ids = ids_ref[pl.ds(own_row(ids_ref, b), 1)]
            hot = lax.broadcasted_iota(jnp.int32, (SEG_ROW, r2.shape[0]), 0) == ids
            counts = jnp.sum(jnp.where(hot, 1.0, 0.0), axis=1, keepdims=True)
            hot = jnp.where(hot, 1.0, 0.0).astype(BF)
            total = sum(dot(hot, piece) for piece in split3(xhat))
            pool_ref[b] = total / counts


def feed(r, vectors, wi, wo, ids):
    batch, length, width = r.shape
    ff = wi.shape[1]
    whole = pl.BlockSpec(r.shape, lambda c: (0, 0, 0))
    vec = pl.BlockSpec(memory_space=pltpu.VMEM)
    chunk = pl.BlockSpec((batch, length, width), lambda c: (0, 0, c))
    wide = shape_of((batch, length, ff), BF)
    return call(
        feed_kernel,
        (ff // width,),
        [whole, vec, pl.BlockSpec((width, width), lambda c: (0, c)),
         pl.BlockSpec((width, width), lambda c: (c, 0)), vec],
        [whole, chunk, chunk, whole, pl.BlockSpec((batch, SEG_ROW, width), lambda c: (0, 0, 0))],
        [shape_of(r.shape, BF), wide, wide, shape_of(r.shape, F32), shape_of((batch, SEG_ROW, width), F32)],
        [pltpu.VMEM(r.shape, F32)],
        4 * batch * length * width * ff,
        batch * length * (10 * width + 4 * ff) + 4 * width * ff,
        FEED_VMEM,
    )(r, vectors, wi, wo, ids)


def flip(v, step):
    return v + step * (1 - 2 * (v // step % 2))


def links(rows):
    seq, row = lax.axis_index("seq"), lax.axis_index("rows")
    core, y, x = seq % 2, seq // 2 % 2, row % 2
    other = 1 - core
    found = [
        ((flip(seq, 1), row), core),
        ((seq + core * 2 * (1 - 2 * y), row + other * (1 - 2 * x)), core * y + other * x),
        ((seq + other * 2 * (1 - 2 * y), row + core * (1 - 2 * x)), other * y + core * x),
    ]
    step = 2
    while step < rows:
        found.append(((seq, flip(row, step)), row // step % 2))
        step *= 2
    return found


def greet(devices):
    barrier = pltpu.get_barrier_semaphore()
    for device in devices:
        pl.semaphore_signal(barrier, inc=1, device_id=device, device_id_type=MESH)
    pl.semaphore_wait(barrier, len(devices))


def remote(source, target, send, receive, device):
    return pltpu.make_async_remote_copy(
        src_ref=source, dst_ref=target, send_sem=send, recv_sem=receive,
        device_id=device, device_id_type=MESH,
    )


def contrast_kernel(
    rows, xpool_ref, in_ref, ids_ref, positives_ref,
    de_ref, vec_ref, all_ref, lse_ref, send, receive,
):
    own, width = xpool_ref.shape
    total = all_ref.shape[0]
    near = links(rows)
    hops = near[3:][::-1] + near[1:3] + near[:1]
    greet([device for device, _ in hops])
    e_own = xpool_ref[...] * in_ref[6:7] + in_ref[7:8]
    seq = lax.axis_index("seq")
    sub = lax.broadcasted_iota(jnp.int32, (own, PAIR), 0)
    lane = lax.broadcasted_iota(jnp.int32, (own, PAIR), 1)
    first = lax.axis_index("rows") * positives_ref.shape[0] + seq * own
    tag = jnp.where(lane == 1, first + sub, 0)
    for i in range(own):
        tag = jnp.where((lane == 0) & (sub == i), positives_ref[seq * own + i], tag)
    tag = tag.astype(F32)
    all_ref[0:own, 0:width] = e_own
    all_ref[0:own, width:] = tag
    have = own
    for i, (device, _) in enumerate(hops):
        copy = remote(
            all_ref.at[0:have], all_ref.at[have : 2 * have], send.at[i], receive.at[i], device
        )
        copy.start()
        copy.wait()
        have *= 2

    def unit(e):
        rho = lax.rsqrt(jnp.sum(e * e, axis=1, keepdims=True) + POOL_EPS)
        return e * rho, rho

    n_all, _ = unit(all_ref[:, 0:width])
    pick = lax.broadcasted_iota(jnp.int32, (8, PAIR), 0) == lax.broadcasted_iota(jnp.int32, (8, PAIR), 1)
    tags = dot_t(pick.astype(F32), all_ref[:, width:], HIGHEST)
    pos_all, id_all = tags[0:1], tags[1:2]
    block = min(total, 512)
    for b in range(total // block):
        n_b, _ = unit(all_ref[b * block : (b + 1) * block, 0:width])
        c = dot_t(n_all, n_b, HIGHEST) * INV_TEMPER
        i = lax.broadcasted_iota(jnp.int32, c.shape, 0)
        j = lax.broadcasted_iota(jnp.int32, c.shape, 1) + b * block
        c = jnp.where(i == j, MASKED, c)
        top = jnp.max(c, axis=0, keepdims=True)
        lse_ref[:, b * block : (b + 1) * block] = (
            jnp.log(jnp.sum(jnp.exp(c - top), axis=0, keepdims=True)) + top
        )
    n_own, rho = unit(e_own)
    pos_own, id_own = tag[:, 0:1], tag[:, 1:2]
    c = dot_t(n_own, n_all, HIGHEST) * INV_TEMPER
    c = jnp.where(id_own == id_all, MASKED, c)
    top = jnp.max(c, axis=1, keepdims=True)
    lse_own = jnp.log(jnp.sum(jnp.exp(c - top), axis=1, keepdims=True)) + top
    chosen = id_all == pos_own
    picked = jnp.sum(jnp.where(chosen, c, 0.0), axis=1, keepdims=True)
    weight = (
        jnp.exp(c - lse_own)
        + jnp.exp(c - lse_ref[...])
        - jnp.where(chosen, 1.0, 0.0)
        - jnp.where(id_own == pos_all, 1.0, 0.0)
    )
    d_n = INV_TEMPER * jnp.dot(weight, n_all, precision=HIGHEST, preferred_element_type=F32)
    along = jnp.sum(e_own * d_n, axis=1, keepdims=True)
    d_e = rho * d_n - (rho * rho * rho) * e_own * along
    for b in range(own // SEG_ROW):
        ids = ids_ref[pl.ds(own_row(ids_ref, b), 1)]
        hot = lax.broadcasted_iota(jnp.int32, (SEG_ROW, ids.shape[1]), 0) == ids
        at = slice(b * SEG_ROW, (b + 1) * SEG_ROW)
        de_ref[at] = d_e[at] / jnp.sum(jnp.where(hot, 1.0, 0.0), axis=1, keepdims=True)
    vec_ref[0:1] = jnp.sum(d_e * xpool_ref[...], axis=0, keepdims=True)
    vec_ref[1:2] = jnp.sum(d_e, axis=0, keepdims=True)
    vec_ref[2:3] = jnp.broadcast_to(jnp.sum(lse_own - picked), (1, vec_ref.shape[1]))
    vec_ref[3:8] = jnp.zeros((5, vec_ref.shape[1]), F32)


def contrast(xpool, vectors, ids, positives, devices, rows):
    own, width = xpool.shape
    total = own * devices
    vmem = pl.BlockSpec(memory_space=pltpu.VMEM)
    stages = len(bin(devices)) - 3
    return pl.pallas_call(
        functools.partial(contrast_kernel, rows),
        in_specs=[vmem] * 3 + [pl.BlockSpec(memory_space=pltpu.SMEM)],
        out_specs=[vmem, vmem],
        out_shape=[shape_of((own, width), F32), shape_of((8, width), F32)],
        scratch_shapes=[
            pltpu.VMEM((total, width + PAIR), F32),
            pltpu.VMEM((1, total), F32),
            pltpu.SemaphoreType.DMA((stages,)),
            pltpu.SemaphoreType.DMA((stages,)),
        ],
        cost_estimate=pl.CostEstimate(
            flops=12 * total * total * width, bytes_accessed=4 * total * width, transcendentals=0
        ),
        compiler_params=pltpu.CompilerParams(
            vmem_limit_bytes=62 << 20, collective_id=0, has_side_effects=True
        ),
    )(xpool, vectors, ids, positives)


CHUNK = 1024


def halves(steps, dims):
    sizes, (height, wide) = [], dims
    for _ in range(steps):
        if height % 32 == 0:
            height //= 2
        else:
            wide //= 2
        sizes.append((height, wide))
    return sizes


def plan(outer, parts, quads, batch):
    attention = outer + 2 * parts
    return [
        ("ab", 0, 0, outer, 1, 1, (1, 3, 2, 1)),
        ("ab", 1, 0, outer, outer + 4, 2, (1, 2, 2, 1)),
        ("ab", 2, 0, quads, attention + 2 * batch, 2 * batch, (1, 2, 1, 1)),
    ]


def orders(rows):
    near = links(rows)
    seq, row = lax.axis_index("seq"), lax.axis_index("rows")
    along = [((seq, flip(row, 1)), row % 2), ((flip(seq, 2), row), seq // 2 % 2)]
    return {
        "ab": near,
        "xy": near[:1] + along + near[3:],
        "z": near[:1] + near[3:] + near[1:3],
    }


class Chain:
    def __init__(self, order, entry, dims, down, grads, sums, mark, came, piece, send, receive, keep):
        self.first, self.number, self.start, self.period, stretch = entry
        stretch = list(stretch) + [stretch[-1]] * (len(order) - len(stretch))
        self.after = [0]
        for wait in stretch + stretch[::-1]:
            self.after.append(self.after[-1] + wait)
        self.order, self.dims, self.down = order, dims, down
        self.grads, self.sums, self.mark = grads, sums, mark
        self.came, self.piece = came, piece
        self.send, self.receive, self.keep = send, receive, keep
        self.sizes = halves(len(order), dims)
        self.last = self.start + (self.number - 1) * self.period + self.after[-1]

    def places(self, chunk):
        row, column = (chunk * self.dims[0], 0) if self.down else (0, chunk * self.dims[1])
        before = self.dims[0]
        found = []
        for (height, wide), (_, bit) in zip(self.sizes, self.order):
            if height < before:
                kept = (row + bit * height, column)
                sent = (row + (1 - bit) * height, column)
            else:
                kept = (row, column + bit * wide)
                sent = (row, column + (1 - bit) * wide)
            found.append((kept, sent))
            (row, column), before = kept, height
        return found

    def at(self, ref, place, size):
        row, column = place
        return ref.at[
            pl.ds(pl.multiple_of(row, 16), size[0]), pl.ds(pl.multiple_of(column, PAIR), size[1])
        ]

    def copy(self, chunk, places, stage):
        n = len(self.order)
        i = stage if stage < n else 2 * n - 1 - stage
        kept, sent = places[i]
        size, device = self.sizes[i], self.order[i][0]
        mark = chunk + self.mark
        pair = self.send.at[stage, mark], self.receive.at[stage, mark]
        if stage < n:
            return remote(self.at(self.grads, sent, size), self.came[i].at[chunk], *pair, device)
        target = self.at(self.sums, kept, size)
        return remote(self.piece.at[chunk] if stage == n else target, target, *pair, device)

    def own(self, chunk, places):
        target = self.at(self.sums, places[-1][0], self.sizes[-1])
        return pltpu.make_async_copy(self.piece.at[chunk], target, self.keep.at[chunk + self.mark])

    def step(self, t):
        for stage in range(2 * len(self.order), -1, -1):
            since = t - self.after[stage] - self.start
            if self.number == 1:
                pl.when(since == 0)(functools.partial(self.advance, stage, self.first))
                continue
            index = since // self.period if self.period > 1 else since
            here = (since >= 0) & (index < self.number)
            if self.period > 1:
                here &= since % self.period == 0
            pl.when(here)(functools.partial(self.advance, stage, index + self.first))

    def advance(self, stage, chunk):
        n = len(self.order)
        places = self.places(chunk)
        if stage > 0:
            self.copy(chunk, places, stage - 1).wait()
        if 0 < stage <= n:
            height, wide = self.sizes[stage - 1]
            row, column = places[stage - 1][0]
            tile = 16 if height % 32 else 32

            def add(k, carry):
                at = pl.ds(pl.multiple_of(k * tile, 16), tile)
                mine = self.at(self.grads, (row + k * tile, column), (tile, wide))
                total = (mine[...].astype(F32) + self.came[stage - 1][chunk, at].astype(F32)).astype(BF)
                if stage < n:
                    mine[...] = total
                else:
                    self.piece[chunk, at] = total
                return carry

            lax.fori_loop(0, height // tile, add, 0)
        if stage == n:
            self.own(chunk, places).start()
        if stage == n + 1:
            self.own(chunk, places).wait()
        if stage < 2 * n:
            self.copy(chunk, places, stage).start()


def sems(*dims):
    return [pltpu.SemaphoreType.DMA(dims)] * 2


FEED_BUFFERS = 1
TOKENS_AT = 2
TOKENS_STEP = 3
SMALL_AT = 6
WEIGHT_BUFFERS = 1


def fixed(dims):
    return pl.BlockSpec(dims, lambda g: (0,) * len(dims), pipeline_mode=pl.Buffered(1))


def pool_back_step(ids, d_e, gain, resid):
    length, width = resid.shape
    xhat, scale = normalize(resid)
    sub = lax.broadcasted_iota(jnp.int32, (PAIR, length), 0)
    hot = (sub % SEG_ROW == ids) & (sub < 3 * SEG_ROW)
    hot = jnp.where(hot, 1.0, 0.0).T.astype(BF)
    pieces = list(split3(d_e)) + [jnp.zeros((PAIR - 3 * SEG_ROW, width), BF)]
    d_y = dot(hot, jnp.concatenate(pieces, axis=0))
    return norm_back(d_y, gain, xhat, scale)


def back_kernel(rows, *refs):
    (r2_ref, r1_ref, de_ref, vec_ref, ids_ref, loss_ref, act_ref, slope_ref, wo_ref, wi_ref, h_ref, wa_ref,
     q_ref, k_ref, v_ref, o_ref, pt_ref, x_ref, wq_ref, wk_ref, wv_ref) = refs[:21]
    sums, (token_out, small_out) = refs[21:24], refs[24:26]
    (g_outer, g_inner, g_attn, g_total, dx, d_f, d_u, d_a, d_o, hx, small_came, send, receive, s_send,
     s_receive, t_send, t_receive, keep, other) = refs[26:45]
    landing = refs[45:]
    step = pl.program_id(0)
    length = q_ref.shape[1]
    count, width = dx.shape
    batch = count // length
    outer, parts = sums[0].shape[0] // CHUNK, sums[1].shape[1] // width
    quads = width // QUAD
    kinds = orders(rows)
    near = kinds["ab"]
    n = len(near)
    seq, row_place = lax.axis_index("seq"), lax.axis_index("rows")
    seqs = token_out.shape[0] // batch
    part = length // seqs
    groups = [
        ((CHUNK, width), True, g_outer, sums[0], 0),
        ((width, CHUNK), False, g_inner, sums[1], outer),
        ((CHUNK, width), True, g_attn, sums[2], 2 * outer),
    ]
    chains = []
    for kind, group, *entry in plan(outer, parts, quads, batch):
        came = landing[group * (n + 1) : group * (n + 1) + n]
        piece = landing[group * (n + 1) + n]
        chains.append(Chain(kinds[kind], entry, *groups[group], came, piece, send, receive, keep))
    before = outer + parts
    ticks = outer + 2 * (parts + quads * batch)
    last = max(max(chain.last for chain in chains), ticks + SMALL_AT + n, ticks + TOKENS_AT + batch * TOKENS_STEP)
    p = jnp.clip(step - outer, 0, parts - 1)
    u = jnp.maximum(step - before, 0)
    now = step + jnp.maximum(step - outer, 0)

    def tick(t):
        for chain in chains:
            chain.step(t)

    def piece(i, b):
        to = lax.rem(seq + i, seqs)
        return remote(
            d_u.at[pl.ds(pl.multiple_of(b * length + to * part, part), part)],
            token_out.at[seq * batch + b],
            t_send.at[b, i - 1], t_receive.at[b, i - 1], (to, row_place),
        )

    def own_piece(b):
        return pltpu.make_async_copy(
            d_u.at[pl.ds(pl.multiple_of(b * length + seq * part, part), part)],
            token_out.at[seq * batch + b], other.at[3 + b],
        )

    def small_copy(i):
        source = small_out if i == 0 else small_came.at[n + i - 1]
        return remote(source, small_came.at[i], s_send.at[i], s_receive.at[i], near[i][0])

    load_r2 = pltpu.make_async_copy(r2_ref, dx, other.at[0])
    load_r1 = pltpu.make_async_copy(r1_ref, g_total, other.at[2])
    load_h = pltpu.make_async_copy(h_ref, hx, other.at[1])
    load_x = pltpu.make_async_copy(x_ref, hx, other.at[1])

    @pl.when(step == 0)
    def _():
        load_r2.start()
        load_r1.start()
        load_h.start()
        greet([device for device, _ in near] + [(flip(flip(seq, 1), 2), row_place)])
        small_out[...] = jnp.zeros_like(small_out)
        small_out[6:9] = loss_ref[0:3]
        load_r2.wait()
        for b in range(batch):
            at = slice(b * length, (b + 1) * length)
            ids = ids_ref[pl.ds(own_row(ids_ref, b), 1)]
            d_r = pool_back_step(ids, de_ref[b], vec_ref[6:7], dx[at])
            dx[at] = d_r
            low = d_r.astype(BF)
            d_f[at] = low
            small_out[5:6] += jnp.sum(low.astype(F32), axis=0, keepdims=True)

    tick(now)

    @pl.when(step < outer)
    def _():
        at = pl.ds(pl.multiple_of(step * CHUNK, CHUNK), CHUNK)
        g_outer[at] = t_dot(act_ref[...], d_f[...]).astype(BF)

    @pl.when(step == outer)
    def _():
        load_h.wait()

    @pl.when((step >= outer) & (step < before))
    def _():
        for b in range(batch):
            at = slice(b * length, (b + 1) * length)
            low = (dot_t(d_f[at], wo_ref[...]) * slope_ref[at].astype(F32)).astype(BF)
            d_u[at] = low
            small_out[pl.ds(9 + p, 1)] += jnp.sum(low.astype(F32), axis=0, keepdims=True)
            dx[at] += dot_t(low, wi_ref[...])
        tick(now + 1)
        at = pl.ds(pl.multiple_of(p * width, width), width)
        g_inner[:, at] = t_dot(hx[...], d_u[...]).astype(BF)

    @pl.when(step == before - 1)
    def _():
        load_x.start()
        load_r1.wait()
        for b in range(batch):
            at = slice(b * length, (b + 1) * length)
            d_h = dx[at]
            xhat, scale = normalize(g_total[at])
            d_r = norm_back(d_h, vec_ref[3:4], xhat, scale)
            dx[at] = d_r
            low = d_r.astype(BF)
            d_a[at] = low
            d_o[at] = dot_t(low, wa_ref[...]).astype(BF)
            small_out[2:3] += jnp.sum(low.astype(F32), axis=0, keepdims=True)
            small_out[3:4] += jnp.sum(d_h * xhat, axis=0, keepdims=True)
            small_out[4:5] += jnp.sum(d_h, axis=0, keepdims=True)

    @pl.when(step == before)
    def _():
        load_x.wait()

    @pl.when(step >= before)
    def _():
        attend_back_step(
            u, lambda: tick(now + 1), q_ref, k_ref, v_ref, o_ref, d_o, pt_ref, hx, d_a,
            wq_ref, wk_ref, wv_ref, g_attn, g_total, dx, small_out,
        )

    @pl.when(step == pl.num_programs(0) - 1)
    def _():
        d_u[...] = dx[...].astype(BF)
        for b in range(batch):
            own_piece(b).start()

        def rest(t, carry):
            tick(t)
            for b in range(batch):
                @pl.when(t == ticks + TOKENS_AT + b * TOKENS_STEP)
                def _(b=b):
                    for i in range(1, seqs):
                        piece(i, b).start()
            for i in range(n + 1):
                @pl.when(t == ticks + SMALL_AT + i)
                def _(i=i):
                    if i > 0:
                        small_copy(i - 1).wait()
                        held = small_out if i == 1 else small_came.at[n + i - 2]
                        after = small_out if i == n else small_came.at[n + i - 1]
                        after[...] = held[...] + small_came[i - 1]
                    if i < n:
                        small_copy(i).start()
            return carry

        lax.fori_loop(ticks, last + 1, rest, 0)
        for b in range(batch):
            own_piece(b).wait()
            for i in range(1, seqs):
                piece(i, b).wait()


def attend_back_step(
    u, between, q_ref, k_ref, v_ref, o_ref, d_o, pt_ref, x_ref, da_ref, wq_ref, wk_ref, wv_ref,
    grads, g_total, dx, small_out,
):
    hd = PAIR // 2
    length = q_ref.shape[1]
    count, width = x_ref.shape
    batch = count // length
    quad, row = lax.div(u, batch), lax.rem(u, batch)
    mine = pl.ds(pl.multiple_of(row * length, length), length)
    lane = lax.broadcasted_iota(jnp.int32, (length, PAIR), 1)
    lane8 = lax.broadcasted_iota(jnp.int32, (8, PAIR), 1)
    dqs, dks, dvs = [], [], []
    for pair in range(QUAD // PAIR):
        if pair == 1:
            between()
        at = slice(pair * PAIR, (pair + 1) * PAIR)
        q, k, v, o = (ref[0, :, at] for ref in (q_ref, k_ref, v_ref, o_ref))
        do = d_o[mine, pl.ds(pl.multiple_of(quad * QUAD + pair * PAIR, PAIR), PAIR)]
        kt = k.T
        prod = o.astype(F32) * do.astype(F32)
        high = prod.astype(BF)
        low = (prod - high.astype(F32)).astype(BF)
        dk = dv = None
        dqt = []
        for h in range(2):
            here = (lane >= hd) if h else (lane < hd)
            ones = jnp.where((lane8 >= hd) if h else (lane8 < hd), 1.0, 0.0).astype(BF)
            do_h = jnp.where(here, do, 0)
            q_h = jnp.where(here, q, 0)
            mixed = (dot_t(ones, high) + dot_t(ones, low))[0:1]
            pt = pt_ref[0, 2 * pair + h]
            ds = (pt.astype(F32) * (dot_t(v, do_h) - mixed)).astype(BF)
            dv_h, dk_h = dot(pt, do_h), dot(ds, q_h)
            dv = dv_h if dv is None else dv + dv_h
            dk = dk_h if dk is None else dk + dk_h
            dqt.append(dot(kt[h * hd : (h + 1) * hd], ds))
        dqs.append((jnp.concatenate(dqt, axis=0).T * (hd ** (-0.5))).astype(BF))
        dks.append(dk.astype(BF))
        dvs.append(dv.astype(BF))
    d_all = jnp.concatenate(dqs + dks + dvs, axis=1)
    column = jnp.sum(d_all.astype(F32), axis=0, keepdims=True)
    for j in range(width // QUAD):
        @pl.when(quad == j)
        def _(j=j):
            at = slice(j * QUAD, (j + 1) * QUAD)
            small_out[0:1, at] += column[:, 0:QUAD]
            small_out[1:2, at] += column[:, 2 * QUAD :]
    weights = jnp.concatenate([wq_ref[...], wk_ref[...], wv_ref[...]], axis=1)
    d_x = dot_t(d_all, weights)
    g_all = t_dot(x_ref[mine], d_all)
    g_o = t_dot(o_ref[0], da_ref[mine])

    dx[mine] += d_x

    top, bottom = slice(0, width), slice(width, width + QUAD)

    @pl.when(row == 0)
    def _():
        g_total[top] = g_all
        g_total[bottom] = g_o

    @pl.when((row > 0) & (row < batch - 1))
    def _():
        g_total[top] += g_all
        g_total[bottom] += g_o

    @pl.when(row == batch - 1)
    def _():
        base = pl.multiple_of(quad * CHUNK, CHUNK)
        grads[pl.ds(base, width)] = (g_total[top] + g_all).astype(BF)
        grads[pl.ds(pl.multiple_of(base + width, QUAD), QUAD)] = (g_total[bottom] + g_o).astype(BF)


def back(r2, r1, de, vectors, ids, loss, act, slope, wo, wi, hidden, wa, q, k, v, o, pt, x, wq, wk, wv,
         devices, rows, seqs):
    batch, length, width = q.shape
    count, ff = act.shape
    quads, outer, parts = width // QUAD, ff // CHUNK, ff // width
    n = len(bin(devices)) - 3
    before = outer + parts
    of = lambda g: jnp.maximum(g - before, 0)
    at = lambda g: jnp.clip(g - outer, 0, parts - 1)
    quad = pl.BlockSpec((1, length, QUAD), lambda g: (of(g) % batch, 0, of(g) // batch))
    cols = pl.BlockSpec((width, QUAD), lambda g: (0, of(g) // batch), pipeline_mode=pl.Buffered(WEIGHT_BUFFERS))
    heads = QUAD // (width // HEADS)
    vmem = pl.BlockSpec(memory_space=pltpu.VMEM)
    hbm = pl.BlockSpec(memory_space=pl.ANY)
    one = pl.Buffered(1)
    landing = []
    for dims, number in (((CHUNK, width), outer), ((width, CHUNK), outer), ((CHUNK, width), quads)):
        sizes = halves(n, dims)
        landing += [pltpu.VMEM((number,) + size, BF) for size in sizes + sizes[-1:]]
    chunks = 2 * outer + quads
    small = shape_of((-(-(9 + parts) // 8) * 8, width), F32)
    return pl.pallas_call(
        functools.partial(back_kernel, rows),
        grid=(before + quads * batch,),
        in_specs=[
            hbm, hbm, vmem, vmem, vmem, vmem,
            pl.BlockSpec((count, CHUNK), lambda g: (0, jnp.clip(g, 0, outer - 1)), pipeline_mode=one),
            pl.BlockSpec((count, width), lambda g: (0, at(g)), pipeline_mode=one),
            pl.BlockSpec((width, width), lambda g: (at(g), 0), pipeline_mode=pl.Buffered(FEED_BUFFERS)),
            pl.BlockSpec((width, width), lambda g: (0, at(g)), pipeline_mode=pl.Buffered(FEED_BUFFERS)),
            hbm, fixed((width, width)),
            quad, quad, quad, quad,
            pl.BlockSpec((1, heads, length, length), lambda g: (of(g) % batch, of(g) // batch, 0, 0)),
            hbm, cols, cols, cols,
        ],
        out_specs=[hbm] * 4 + [vmem],
        out_shape=[
            shape_of((ff, width), BF), shape_of((width, ff), BF), shape_of((quads * CHUNK, width), BF),
            shape_of((batch * seqs, length // seqs, width), BF), small,
        ],
        scratch_shapes=[
            pltpu.VMEM((ff, width), BF), pltpu.VMEM((width, ff), BF), pltpu.VMEM((quads * CHUNK, width), BF),
            pltpu.VMEM((count, width), F32), pltpu.VMEM((count, width), F32),
        ] + [pltpu.VMEM((count, width), BF)] * 4 + [
            pltpu.VMEM((count, width), BF), pltpu.VMEM((2 * n,) + small.shape, F32),
        ] + sems(2 * n, chunks) + sems(n) + sems(batch, seqs - 1)
        + [pltpu.SemaphoreType.DMA((chunks,)), pltpu.SemaphoreType.DMA((3 + batch,))] + landing,
        cost_estimate=pl.CostEstimate(
            flops=count * width * (16 * length + 16 * width), bytes_accessed=4 * count * (4 * width + HEADS * length),
            transcendentals=0,
        ),
        compiler_params=pltpu.CompilerParams(
            vmem_limit_bytes=63 << 20, collective_id=2, has_side_effects=True
        ),
    )(r2, r1, de, vectors, ids, loss, act, slope, wo, wi, hidden, wa, q, k, v, o, pt, x, wq, wk, wv)


RING = 4


def widen_kernel(outer_in, inner_in, attn_in, token_in, outer, inner, g_q, g_k, g_v, g_o, g_tok, read, wide, r_sem, w_sem):
    width, ff = inner.shape
    jobs = []
    for i in range(ff // width):
        at = slice(i * width, (i + 1) * width)
        jobs.append((outer_in.at[at], [(slice(0, width), slice(0, width), outer.at[at])]))
    for i in range(ff // width):
        at = slice(i * width, (i + 1) * width)
        jobs.append((inner_in.at[:, at], [(slice(0, width), slice(0, width), inner.at[:, at])]))
    for j in range(width // QUAD):
        at = slice(j * QUAD, (j + 1) * QUAD)
        parts = [
            (slice(0, width), slice(m * QUAD, (m + 1) * QUAD), g.at[:, at]) for m, g in enumerate((g_q, g_k, g_v))
        ]
        parts.append((slice(width, CHUNK), slice(0, width), g_o.at[at]))
        jobs.append((attn_in.at[j * CHUNK : (j + 1) * CHUNK], parts))

    for at in range(0, g_tok.shape[0], CHUNK):
        at = slice(at, at + CHUNK)
        jobs.append((token_in.at[at], [(slice(0, CHUNK), slice(0, width), g_tok.at[at])]))

    def reader(i):
        source = jobs[i][0]
        return pltpu.make_async_copy(source, read.at[i % RING, 0 : source.shape[0]], r_sem.at[i % RING])

    def writers(i):
        return [
            pltpu.make_async_copy(wide.at[i % RING, r, c], target, w_sem.at[i % RING, m])
            for m, (r, c, target) in enumerate(jobs[i][1])
        ]

    for i in range(RING - 1):
        reader(i).start()
    for i in range(len(jobs)):
        reader(i).wait()
        if i + RING - 1 < len(jobs):
            reader(i + RING - 1).start()
        if i >= RING:
            for copy in writers(i - RING):
                copy.wait()

        def cast(k, carry, i=i):
            at = pl.ds(pl.multiple_of(k * 64, 64), 64)
            wide[i % RING, at] = read[i % RING, at].astype(F32)
            return carry

        lax.fori_loop(0, jobs[i][0].shape[0] // 64, cast, 0)
        for copy in writers(i):
            copy.start()
    for i in range(len(jobs) - RING, len(jobs)):
        for copy in writers(i):
            copy.wait()


def widen(outer, inner, attn, tokens):
    ff, width = outer.shape
    hbm = pl.BlockSpec(memory_space=pl.ANY)
    square = shape_of((width, width), F32)
    return pl.pallas_call(
        widen_kernel,
        in_specs=[hbm] * 4,
        out_specs=[hbm] * 7,
        out_shape=[shape_of((ff, width), F32), shape_of((width, ff), F32)] + [square] * 4
        + [shape_of(tokens.shape, F32)],
        scratch_shapes=[
            pltpu.VMEM((RING, CHUNK, width), BF), pltpu.VMEM((RING, CHUNK, width), F32),
            pltpu.SemaphoreType.DMA((RING,)), pltpu.SemaphoreType.DMA((RING, 4)),
        ],
        compiler_params=pltpu.CompilerParams(vmem_limit_bytes=62 << 20),
    )(outer, inner, attn, tokens)


def local(
    tokens,
    query_weight,
    query_bias,
    key_weight,
    value_weight,
    value_bias,
    output_weight,
    output_bias,
    attn_gain,
    attn_shift,
    inner_weight,
    inner_bias,
    outer_weight,
    outer_bias,
    ffn_gain,
    ffn_shift,
    segment_ids,
    positives,
):
    group_rows, local_len, width = tokens.shape
    ff = inner_weight.shape[1]
    seqs = lax.axis_size("seq")
    batch, length = group_rows // seqs, local_len * seqs
    count = batch * length
    own_segs = batch * SEG_ROW
    rows = lax.axis_size("rows")
    devices = rows * seqs
    flat2 = lambda a: a.reshape(count, a.shape[-1])
    lines = [query_bias, value_bias, output_bias, attn_gain, attn_shift, outer_bias, ffn_gain, ffn_shift]
    lines += [inner_bias[i * width : (i + 1) * width] for i in range(ff // width)]
    place = lax.broadcasted_iota(jnp.int32, (-(-len(lines) // 8) * 8, width), 0)
    vectors = jnp.zeros(place.shape, BF)
    for i, line in enumerate(lines):
        vectors = jnp.where(place == i, line[None, :], vectors)
    vectors = vectors.astype(F32)

    q, k, v, o, pt, r_one, x = attend(
        tokens, query_weight, key_weight, value_weight, output_weight, vectors, segment_ids, seqs
    )
    hidden, active, slope, r_two, xpool = feed(r_one, vectors, inner_weight, outer_weight, segment_ids)
    d_e, loss_vec = contrast(
        xpool.reshape(own_segs, width), vectors, segment_ids, positives, devices, rows
    )
    *sums, grad_tokens, small = back(
        flat2(r_two), flat2(r_one), d_e.reshape(batch, SEG_ROW, width), vectors, segment_ids, loss_vec,
        flat2(active), flat2(slope), outer_weight, inner_weight, flat2(hidden), output_weight,
        q, k, v, o, pt, flat2(x), query_weight, key_weight, value_weight, devices, rows, seqs,
    )
    g_outer, g_inner, g_query, g_key, g_value, g_output, g_tokens = widen(
        *sums, grad_tokens.reshape(count, width)
    )
    return (
        small[8, 0] / (own_segs * devices),
        g_tokens.reshape(tokens.shape),
        g_query,
        small[0],
        g_key,
        g_value,
        small[1],
        g_output,
        small[2],
        small[3],
        small[4],
        g_inner,
        small[9 : 9 + ff // width].reshape(-1),
        g_outer,
        small[5],
        small[6],
        small[7],
    )


def solution(mesh):
    placed = (
        (P("rows", "seq", None),) + (P(),) * 15 + (P("rows", None), P("rows"))
    )
    return jax.shard_map(
        local,
        mesh=mesh,
        in_specs=placed,
        out_specs=(P(), P("rows", "seq", None)) + (P(),) * 15,
        check_vma=False,
    )
```

```python
import functools

import jax
import jax.numpy as jnp
from jax import lax
from jax.experimental import pallas as pl
from jax.experimental.pallas import tpu as pltpu
from jax.sharding import PartitionSpec as P

HEADS = 12
SEG_ROW = 8
HIGHEST = lax.Precision.HIGHEST
NORM_EPS = 1e-12
POOL_EPS = 1e-06
INV_TEMPER = 100.0
MASKED = -1000000000.0
INV_ROOT_TWO_PI = 0.3989422804014327
INV_ROOT_TWO = 0.7071067811865476
BF = jnp.bfloat16
F32 = jnp.float32
MESH = pl.DeviceIdType.MESH


def dot(a, b):
    return jnp.dot(a, b, preferred_element_type=F32)


def dot_t(a, b, precision=None):
    return lax.dot_general(
        a, b, (((1,), (1,)), ((), ())), preferred_element_type=F32, precision=precision
    )


def t_dot(a, b):
    return lax.dot_general(a, b, (((0,), (0,)), ((), ())), preferred_element_type=F32)


def normalize(resid):
    center = resid - jnp.mean(resid, axis=-1, keepdims=True)
    spread = jnp.mean(center * center, axis=-1, keepdims=True)
    scale = lax.rsqrt(spread + NORM_EPS)
    return center * scale, scale


def norm_back(grad, gain, xhat, scale):
    q = grad * gain
    return scale * (
        q - jnp.mean(q, axis=-1, keepdims=True) - xhat * jnp.mean(q * xhat, axis=-1, keepdims=True)
    )


def dot_split(a, b):
    a_high, b_high = a.astype(BF), b.astype(BF)
    a_low, b_low = (a - a_high.astype(F32)).astype(BF), (b - b_high.astype(F32)).astype(BF)
    return dot_t(a_high, b_high) + (dot_t(a_high, b_low) + dot_t(a_low, b_high))


def split3(a):
    hi = a.astype(BF)
    rest = a - hi.astype(F32)
    mid = rest.astype(BF)
    return hi, mid, (rest - mid.astype(F32)).astype(BF)


def call(kernel, grid, in_specs, out_specs, out_shape, scratch, flops, moved, vmem=62):
    return pl.pallas_call(
        kernel,
        grid=grid,
        in_specs=in_specs,
        out_specs=out_specs,
        out_shape=out_shape,
        scratch_shapes=scratch,
        cost_estimate=pl.CostEstimate(flops=flops, bytes_accessed=moved, transcendentals=0),
        compiler_params=pltpu.CompilerParams(vmem_limit_bytes=vmem << 20),
    )


def shape_of(dims, dtype):
    return jax.ShapeDtypeStruct(dims, dtype)


PAIR = 128
QUAD = 256


def attend_kernel(
    tokens_ref, wq_ref, wk_ref, wv_ref, wo_ref, bias_ref, row_ref, ids_ref,
    q_ref, k_ref, v_ref, o_ref, pt_ref, r_ref, x_out, x_ref, apart_q, apart_k, send, receive, own_sem,
):
    row, quad = pl.program_id(0), pl.program_id(1)
    batch, length = x_ref.shape[0], x_ref.shape[1]
    part = tokens_ref.shape[1]
    seqs = length // part
    hd = PAIR // 2
    seq, place = lax.axis_index("seq"), lax.axis_index("rows")

    def target(b):
        return x_ref.at[b, pl.ds(pl.multiple_of(seq * part, part), part)]

    def piece(i, b):
        to = lax.rem(seq + i, seqs)
        return remote(
            tokens_ref.at[to * batch + b], target(b), send.at[b, i - 1], receive.at[b, i - 1], (to, place)
        )

    def own(b):
        return pltpu.make_async_copy(tokens_ref.at[seq * batch + b], target(b), own_sem.at[b])

    def keep(b):
        return pltpu.make_async_copy(x_ref.at[b], x_out.at[b], own_sem.at[batch + b])

    @pl.when((row == 0) & (quad == 0))
    def _():
        greet([(lax.rem(seq + i, seqs), place) for i in range(1, seqs)])
        for b in range(batch):
            for i in range(1, seqs):
                piece(i, b).start()
            own(b).start()

    for b in range(batch):
        @pl.when((row == b) & (quad == 0))
        def _(b=b):
            hot = lax.broadcasted_iota(jnp.int32, (PAIR, length), 0) == ids_ref[pl.ds(seq * batch + b, 1), :]
            hot = jnp.where(hot, 1.0, 0.0).T
            real = lax.broadcasted_iota(jnp.int32, (length, PAIR), 1) < SEG_ROW
            apart_q[...] = (hot * -(2.0**30)).astype(BF)
            apart_k[...] = jnp.where(real, 1.0 - hot, 0.0).astype(BF)
            own(b).wait()
            for i in range(1, seqs):
                piece(i, b).wait()
            keep(b).start()

    x = x_ref[row]
    q = (dot(x, wq_ref[...]) + bias_ref[0:1]).astype(BF) * jnp.asarray(hd ** (-0.5), BF)
    k = dot(x, wk_ref[...]).astype(BF)
    v = (dot(x, wv_ref[...]) + bias_ref[1:2]).astype(BF)
    q_ref[0], k_ref[0], v_ref[0] = q, k, v
    lane = lax.broadcasted_iota(jnp.int32, (length, PAIR), 1)
    outs = []
    for pair in range(QUAD // PAIR):
        at = slice(pair * PAIR, (pair + 1) * PAIR)
        keys = jnp.concatenate([k[:, at], apart_k[...]], axis=1)
        vt = v[:, at].T
        parts = []
        for h in range(2):
            mine = (lane >= hd) if h else (lane < hd)
            queries = jnp.concatenate([jnp.where(mine, q[:, at], 0), apart_q[...]], axis=1)
            st = dot_t(keys, queries)
            expo = jnp.exp(st - jnp.max(st, axis=0, keepdims=True))
            pt = (expo * (1.0 / jnp.sum(expo, axis=0, keepdims=True))).astype(BF)
            pt_ref[0, 2 * pair + h] = pt
            parts.append(dot(vt[h * hd : (h + 1) * hd], pt))
        outs.append(jnp.concatenate(parts, axis=0).T)
    o = jnp.concatenate(outs, axis=1).astype(BF)
    o_ref[0] = o
    part_sum = dot(o, wo_ref[...])

    @pl.when(quad == 0)
    def _():
        r_ref[0] = x.astype(F32) + row_ref[2:3] + part_sum

    @pl.when(quad > 0)
    def _():
        r_ref[0] += part_sum

    @pl.when((row == batch - 1) & (quad == pl.num_programs(1) - 1))
    def _():
        for b in range(batch):
            keep(b).wait()


def attend(tokens, wq, wk, wv, wo, vectors, ids, seqs):
    rows, part, width = tokens.shape
    batch, length = rows // seqs, part * seqs
    row = pl.BlockSpec((1, length, width), lambda b, j: (b, 0, 0))
    cols = pl.BlockSpec((width, QUAD), lambda b, j: (0, j))
    quad = pl.BlockSpec((1, length, QUAD), lambda b, j: (b, 0, j))
    heads = QUAD // (width // HEADS)
    vmem = pl.BlockSpec(memory_space=pltpu.VMEM)
    dims = (batch, length, width)
    act = shape_of(dims, BF)
    return pl.pallas_call(
        attend_kernel,
        grid=(batch, width // QUAD),
        in_specs=[pl.BlockSpec(memory_space=pl.ANY), cols, cols, cols,
                  pl.BlockSpec((QUAD, width), lambda b, j: (j, 0)),
                  pl.BlockSpec((8, QUAD), lambda b, j: (0, j)), vmem, vmem],
        out_specs=[quad, quad, quad, quad,
                   pl.BlockSpec((1, heads, length, length), lambda b, j: (b, j, 0, 0)), row,
                   pl.BlockSpec(memory_space=pl.ANY)],
        out_shape=[act, act, act, act, shape_of((batch, HEADS, length, length), BF), shape_of(dims, F32), act],
        scratch_shapes=[pltpu.VMEM(dims, BF)] + [pltpu.VMEM((length, PAIR), BF)] * 2
        + [pltpu.SemaphoreType.DMA((batch, seqs - 1))] * 2 + [pltpu.SemaphoreType.DMA((2 * batch,))],
        cost_estimate=pl.CostEstimate(
            flops=batch * length * width * (8 * width + 8 * length),
            bytes_accessed=batch * length * (14 * width + 2 * HEADS * length) + 8 * width * width,
            transcendentals=0,
        ),
        compiler_params=pltpu.CompilerParams(
            vmem_limit_bytes=62 << 20, collective_id=1, has_side_effects=True
        ),
    )(tokens, wq, wk, wv, wo, vectors, vectors, ids)


def gelu_both(u):
    cdf = 0.5 + 0.5 * lax.erf(u * INV_ROOT_TWO)
    return u * cdf, cdf + (INV_ROOT_TWO_PI * u) * jnp.exp(-0.5 * u * u)


def own_row(ids_ref, b):
    return lax.axis_index("seq") * (ids_ref.shape[0] // lax.axis_size("seq")) + b


FEED_VMEM = 62
FBACK_VMEM = 62


def feed_kernel(
    r_ref, vec_ref, wi_ref, wo_ref, ids_ref,
    h_ref, act_ref, slope_ref, r2_ref, pool_ref, hidden,
):
    step = pl.program_id(0)
    batch = r_ref.shape[0]

    @pl.when(step == 0)
    def _():
        for b in range(batch):
            xhat, _ = normalize(r_ref[b])
            h = xhat * vec_ref[3:4] + vec_ref[4:5]
            hidden[b] = h + vec_ref[5:6]
            h_ref[b] = h.astype(BF)

    bias = vec_ref[pl.ds(8 + step, 1)]
    for b in range(batch):
        act, slope = gelu_both(dot(h_ref[b], wi_ref[...]) + bias)
        act = act.astype(BF)
        act_ref[b] = act
        slope_ref[b] = slope.astype(BF)
        hidden[b] += dot(act, wo_ref[...])

    @pl.when(step == pl.num_programs(0) - 1)
    def _():
        for b in range(batch):
            r2 = hidden[b]
            r2_ref[b] = r2
            xhat, _ = normalize(r2)
            ids = ids_ref[pl.ds(own_row(ids_ref, b), 1)]
            hot = lax.broadcasted_iota(jnp.int32, (SEG_ROW, r2.shape[0]), 0) == ids
            counts = jnp.sum(jnp.where(hot, 1.0, 0.0), axis=1, keepdims=True)
            hot = jnp.where(hot, 1.0, 0.0).astype(BF)
            total = sum(dot(hot, piece) for piece in split3(xhat))
            pool_ref[b] = total / counts


def feed(r, vectors, wi, wo, ids):
    batch, length, width = r.shape
    ff = wi.shape[1]
    whole = pl.BlockSpec(r.shape, lambda c: (0, 0, 0))
    vec = pl.BlockSpec(memory_space=pltpu.VMEM)
    chunk = pl.BlockSpec((batch, length, width), lambda c: (0, 0, c))
    wide = shape_of((batch, length, ff), BF)
    return call(
        feed_kernel,
        (ff // width,),
        [whole, vec, pl.BlockSpec((width, width), lambda c: (0, c)),
         pl.BlockSpec((width, width), lambda c: (c, 0)), vec],
        [whole, chunk, chunk, whole, pl.BlockSpec((batch, SEG_ROW, width), lambda c: (0, 0, 0))],
        [shape_of(r.shape, BF), wide, wide, shape_of(r.shape, F32), shape_of((batch, SEG_ROW, width), F32)],
        [pltpu.VMEM(r.shape, F32)],
        4 * batch * length * width * ff,
        batch * length * (10 * width + 4 * ff) + 4 * width * ff,
        FEED_VMEM,
    )(r, vectors, wi, wo, ids)


def flip(v, step):
    return v + step * (1 - 2 * (v // step % 2))


def links(rows):
    seq, row = lax.axis_index("seq"), lax.axis_index("rows")
    core, y, x = seq % 2, seq // 2 % 2, row % 2
    other = 1 - core
    found = [
        ((flip(seq, 1), row), core),
        ((seq + core * 2 * (1 - 2 * y), row + other * (1 - 2 * x)), core * y + other * x),
        ((seq + other * 2 * (1 - 2 * y), row + core * (1 - 2 * x)), other * y + core * x),
    ]
    step = 2
    while step < rows:
        found.append(((seq, flip(row, step)), row // step % 2))
        step *= 2
    return found


def greet(devices):
    barrier = pltpu.get_barrier_semaphore()
    for device in devices:
        pl.semaphore_signal(barrier, inc=1, device_id=device, device_id_type=MESH)
    pl.semaphore_wait(barrier, len(devices))


def remote(source, target, send, receive, device):
    return pltpu.make_async_remote_copy(
        src_ref=source, dst_ref=target, send_sem=send, recv_sem=receive,
        device_id=device, device_id_type=MESH,
    )


def contrast_kernel(
    rows, xpool_ref, in_ref, ids_ref, positives_ref,
    de_ref, vec_ref, all_ref, lse_ref, send, receive,
):
    own, width = xpool_ref.shape
    total = all_ref.shape[0]
    near = links(rows)
    hops = near[3:][::-1] + near[1:3]
    sibling = near[0][0]
    greet([device for device, _ in near])
    e_own = xpool_ref[...] * in_ref[6:7] + in_ref[7:8]
    seq = lax.axis_index("seq")
    sub = lax.broadcasted_iota(jnp.int32, (own, PAIR), 0)
    lane = lax.broadcasted_iota(jnp.int32, (own, PAIR), 1)
    first = lax.axis_index("rows") * positives_ref.shape[0] + seq * own
    tag = jnp.where(lane == 1, first + sub, 0)
    for i in range(own):
        tag = jnp.where((lane == 0) & (sub == i), positives_ref[seq * own + i], tag)
    tag = tag.astype(F32)
    all_ref[0:own, 0:width] = e_own
    all_ref[0:own, width:] = tag
    have = own

    def across(i, low, high):
        return remote(
            all_ref.at[low:high], all_ref.at[total // 2 + low : total // 2 + high],
            send.at[len(hops) + i], receive.at[len(hops) + i], sibling,
        )

    passed = [across(0, 0, have)]
    passed[0].start()
    for i, (device, _) in enumerate(hops):
        copy = remote(
            all_ref.at[0:have], all_ref.at[have : 2 * have], send.at[i], receive.at[i], device
        )
        copy.start()
        copy.wait()
        passed.append(across(i + 1, have, 2 * have))
        passed[-1].start()
        have *= 2
    for copy in passed:
        copy.wait()

    def unit(e):
        rho = lax.rsqrt(jnp.sum(e * e, axis=1, keepdims=True) + POOL_EPS)
        return e * rho, rho

    n_all, _ = unit(all_ref[:, 0:width])
    pick = lax.broadcasted_iota(jnp.int32, (8, PAIR), 0) == lax.broadcasted_iota(jnp.int32, (8, PAIR), 1)
    tags = dot_t(pick.astype(F32), all_ref[:, width:], HIGHEST)
    pos_all, id_all = tags[0:1], tags[1:2]
    block = min(total, 512)
    for b in range(total // block):
        n_b, _ = unit(all_ref[b * block : (b + 1) * block, 0:width])
        c = dot_split(n_all, n_b) * INV_TEMPER
        i = lax.broadcasted_iota(jnp.int32, c.shape, 0)
        j = lax.broadcasted_iota(jnp.int32, c.shape, 1) + b * block
        c = jnp.where(i == j, MASKED, c)
        top = jnp.max(c, axis=0, keepdims=True)
        lse_ref[:, b * block : (b + 1) * block] = (
            jnp.log(jnp.sum(jnp.exp(c - top), axis=0, keepdims=True)) + top
        )
    n_own, rho = unit(e_own)
    pos_own, id_own = tag[:, 0:1], tag[:, 1:2]
    c = dot_t(n_own, n_all, HIGHEST) * INV_TEMPER
    c = jnp.where(id_own == id_all, MASKED, c)
    top = jnp.max(c, axis=1, keepdims=True)
    lse_own = jnp.log(jnp.sum(jnp.exp(c - top), axis=1, keepdims=True)) + top
    chosen = id_all == pos_own
    picked = jnp.sum(jnp.where(chosen, c, 0.0), axis=1, keepdims=True)
    weight = (
        jnp.exp(c - lse_own)
        + jnp.exp(c - lse_ref[...])
        - jnp.where(chosen, 1.0, 0.0)
        - jnp.where(id_own == pos_all, 1.0, 0.0)
    )
    d_n = INV_TEMPER * jnp.dot(weight, n_all, precision=HIGHEST, preferred_element_type=F32)
    along = jnp.sum(e_own * d_n, axis=1, keepdims=True)
    d_e = rho * d_n - (rho * rho * rho) * e_own * along
    for b in range(own // SEG_ROW):
        ids = ids_ref[pl.ds(own_row(ids_ref, b), 1)]
        hot = lax.broadcasted_iota(jnp.int32, (SEG_ROW, ids.shape[1]), 0) == ids
        at = slice(b * SEG_ROW, (b + 1) * SEG_ROW)
        de_ref[at] = d_e[at] / jnp.sum(jnp.where(hot, 1.0, 0.0), axis=1, keepdims=True)
    vec_ref[0:1] = jnp.sum(d_e * xpool_ref[...], axis=0, keepdims=True)
    vec_ref[1:2] = jnp.sum(d_e, axis=0, keepdims=True)
    vec_ref[2:3] = jnp.broadcast_to(jnp.sum(lse_own - picked), (1, vec_ref.shape[1]))
    vec_ref[3:8] = jnp.zeros((5, vec_ref.shape[1]), F32)


def contrast(xpool, vectors, ids, positives, devices, rows):
    own, width = xpool.shape
    total = own * devices
    vmem = pl.BlockSpec(memory_space=pltpu.VMEM)
    stages = len(bin(devices)) - 3
    return pl.pallas_call(
        functools.partial(contrast_kernel, rows),
        in_specs=[vmem] * 3 + [pl.BlockSpec(memory_space=pltpu.SMEM)],
        out_specs=[vmem, vmem],
        out_shape=[shape_of((own, width), F32), shape_of((8, width), F32)],
        scratch_shapes=[
            pltpu.VMEM((total, width + PAIR), F32),
            pltpu.VMEM((1, total), F32),
            pltpu.SemaphoreType.DMA((2 * stages,)),
            pltpu.SemaphoreType.DMA((2 * stages,)),
        ],
        cost_estimate=pl.CostEstimate(
            flops=12 * total * total * width, bytes_accessed=4 * total * width, transcendentals=0
        ),
        compiler_params=pltpu.CompilerParams(
            vmem_limit_bytes=62 << 20, collective_id=0, has_side_effects=True
        ),
    )(xpool, vectors, ids, positives)


CHUNK = 1024


def halves(steps, dims):
    sizes, (height, wide) = [], dims
    for _ in range(steps):
        if height % 32 == 0:
            height //= 2
        else:
            wide //= 2
        sizes.append((height, wide))
    return sizes


def plan(outer, parts, quads, batch):
    attention = outer + 2 * parts
    return [
        ("ab", 0, 0, outer, 1, 1, (1, 3, 2, 1)),
        ("ab", 1, 0, outer, outer + 4, 2, (1, 2, 2, 1)),
        ("ab", 2, 0, quads, attention + 2 * batch, 2 * batch, (1, 2, 1, 1)),
    ]


def orders(rows):
    near = links(rows)
    seq, row = lax.axis_index("seq"), lax.axis_index("rows")
    along = [((seq, flip(row, 1)), row % 2), ((flip(seq, 2), row), seq // 2 % 2)]
    return {
        "ab": near,
        "xy": near[:1] + along + near[3:],
        "z": near[:1] + near[3:] + near[1:3],
    }


class Chain:
    def __init__(self, order, entry, dims, down, grads, sums, mark, came, piece, send, receive, keep):
        self.first, self.number, self.start, self.period, stretch = entry
        stretch = list(stretch) + [stretch[-1]] * (len(order) - len(stretch))
        self.after = [0]
        for wait in stretch + stretch[::-1]:
            self.after.append(self.after[-1] + wait)
        self.order, self.dims, self.down = order, dims, down
        self.grads, self.sums, self.mark = grads, sums, mark
        self.came, self.piece = came, piece
        self.send, self.receive, self.keep = send, receive, keep
        self.sizes = halves(len(order), dims)
        self.last = self.start + (self.number - 1) * self.period + self.after[-1]

    def places(self, chunk):
        row, column = (chunk * self.dims[0], 0) if self.down else (0, chunk * self.dims[1])
        before = self.dims[0]
        found = []
        for (height, wide), (_, bit) in zip(self.sizes, self.order):
            if height < before:
                kept = (row + bit * height, column)
                sent = (row + (1 - bit) * height, column)
            else:
                kept = (row, column + bit * wide)
                sent = (row, column + (1 - bit) * wide)
            found.append((kept, sent))
            (row, column), before = kept, height
        return found

    def at(self, ref, place, size):
        row, column = place
        return ref.at[
            pl.ds(pl.multiple_of(row, 16), size[0]), pl.ds(pl.multiple_of(column, PAIR), size[1])
        ]

    def copy(self, chunk, places, stage):
        n = len(self.order)
        i = stage if stage < n else 2 * n - 1 - stage
        kept, sent = places[i]
        size, device = self.sizes[i], self.order[i][0]
        mark = chunk + self.mark
        pair = self.send.at[stage, mark], self.receive.at[stage, mark]
        if stage < n:
            return remote(self.at(self.grads, sent, size), self.came[i].at[chunk], *pair, device)
        target = self.at(self.sums, kept, size)
        return remote(self.piece.at[chunk] if stage == n else target, target, *pair, device)

    def own(self, chunk, places):
        target = self.at(self.sums, places[-1][0], self.sizes[-1])
        return pltpu.make_async_copy(self.piece.at[chunk], target, self.keep.at[chunk + self.mark])

    def step(self, t):
        for stage in range(2 * len(self.order), -1, -1):
            since = t - self.after[stage] - self.start
            if self.number == 1:
                pl.when(since == 0)(functools.partial(self.advance, stage, self.first))
                continue
            index = since // self.period if self.period > 1 else since
            here = (since >= 0) & (index < self.number)
            if self.period > 1:
                here &= since % self.period == 0
            pl.when(here)(functools.partial(self.advance, stage, index + self.first))

    def advance(self, stage, chunk):
        n = len(self.order)
        places = self.places(chunk)
        if stage > 0:
            self.copy(chunk, places, stage - 1).wait()
        if 0 < stage <= n:
            height, wide = self.sizes[stage - 1]
            row, column = places[stage - 1][0]
            tile = 16 if height % 32 else 32

            def add(k, carry):
                at = pl.ds(pl.multiple_of(k * tile, 16), tile)
                mine = self.at(self.grads, (row + k * tile, column), (tile, wide))
                total = (mine[...].astype(F32) + self.came[stage - 1][chunk, at].astype(F32)).astype(BF)
                if stage < n:
                    mine[...] = total
                else:
                    self.piece[chunk, at] = total
                return carry

            lax.fori_loop(0, height // tile, add, 0)
        if stage == n:
            self.own(chunk, places).start()
        if stage == n + 1:
            self.own(chunk, places).wait()
        if stage < 2 * n:
            self.copy(chunk, places, stage).start()


def sems(*dims):
    return [pltpu.SemaphoreType.DMA(dims)] * 2


FEED_BUFFERS = 1
TOKENS_AT = 2
TOKENS_STEP = 3
SMALL_AT = 6
WEIGHT_BUFFERS = 1


def fixed(dims):
    return pl.BlockSpec(dims, lambda g: (0,) * len(dims), pipeline_mode=pl.Buffered(1))


def pool_back_step(ids, d_e, gain, resid):
    length, width = resid.shape
    xhat, scale = normalize(resid)
    sub = lax.broadcasted_iota(jnp.int32, (PAIR, length), 0)
    hot = (sub % SEG_ROW == ids) & (sub < 3 * SEG_ROW)
    hot = jnp.where(hot, 1.0, 0.0).T.astype(BF)
    pieces = list(split3(d_e)) + [jnp.zeros((PAIR - 3 * SEG_ROW, width), BF)]
    d_y = dot(hot, jnp.concatenate(pieces, axis=0))
    return norm_back(d_y, gain, xhat, scale)


def back_kernel(rows, *refs):
    (r2_ref, r1_ref, de_ref, vec_ref, ids_ref, loss_ref, act_ref, slope_ref, wo_ref, wi_ref, h_ref, wa_ref,
     q_ref, k_ref, v_ref, o_ref, pt_ref, x_ref, wq_ref, wk_ref, wv_ref) = refs[:21]
    sums, (token_out, small_out) = refs[21:24], refs[24:26]
    (g_outer, g_inner, g_attn, g_total, dx, d_f, d_u, d_a, d_o, hx, small_came, send, receive, s_send,
     s_receive, t_send, t_receive, keep, other) = refs[26:45]
    landing = refs[45:]
    step = pl.program_id(0)
    length = q_ref.shape[1]
    count, width = dx.shape
    batch = count // length
    outer, parts = sums[0].shape[0] // CHUNK, sums[1].shape[1] // width
    quads = width // QUAD
    kinds = orders(rows)
    near = kinds["ab"]
    n = len(near)
    seq, row_place = lax.axis_index("seq"), lax.axis_index("rows")
    seqs = token_out.shape[0] // batch
    part = length // seqs
    groups = [
        ((CHUNK, width), True, g_outer, sums[0], 0),
        ((width, CHUNK), False, g_inner, sums[1], outer),
        ((CHUNK, width), True, g_attn, sums[2], 2 * outer),
    ]
    chains = []
    for kind, group, *entry in plan(outer, parts, quads, batch):
        came = landing[group * (n + 1) : group * (n + 1) + n]
        piece = landing[group * (n + 1) + n]
        chains.append(Chain(kinds[kind], entry, *groups[group], came, piece, send, receive, keep))
    before = outer + parts
    ticks = outer + 2 * (parts + quads * batch)
    last = max(max(chain.last for chain in chains), ticks + SMALL_AT + n, ticks + TOKENS_AT + batch * TOKENS_STEP)
    p = jnp.clip(step - outer, 0, parts - 1)
    u = jnp.maximum(step - before, 0)
    now = step + jnp.maximum(step - outer, 0)

    def tick(t):
        for chain in chains:
            chain.step(t)

    def piece(i, b):
        to = lax.rem(seq + i, seqs)
        return remote(
            d_u.at[pl.ds(pl.multiple_of(b * length + to * part, part), part)],
            token_out.at[seq * batch + b],
            t_send.at[b, i - 1], t_receive.at[b, i - 1], (to, row_place),
        )

    def own_piece(b):
        return pltpu.make_async_copy(
            d_u.at[pl.ds(pl.multiple_of(b * length + seq * part, part), part)],
            token_out.at[seq * batch + b], other.at[3 + b],
        )

    def small_copy(i):
        source = small_out if i == 0 else small_came.at[n + i - 1]
        return remote(source, small_came.at[i], s_send.at[i], s_receive.at[i], near[i][0])

    load_r2 = pltpu.make_async_copy(r2_ref, dx, other.at[0])
    load_r1 = pltpu.make_async_copy(r1_ref, g_total, other.at[2])
    load_h = pltpu.make_async_copy(h_ref, hx, other.at[1])
    load_x = pltpu.make_async_copy(x_ref, hx, other.at[1])

    @pl.when(step == 0)
    def _():
        load_r2.start()
        load_r1.start()
        load_h.start()
        greet([device for device, _ in near] + [(flip(flip(seq, 1), 2), row_place)])
        small_out[...] = jnp.zeros_like(small_out)
        small_out[6:9] = loss_ref[0:3]
        load_r2.wait()
        for b in range(batch):
            at = slice(b * length, (b + 1) * length)
            ids = ids_ref[pl.ds(own_row(ids_ref, b), 1)]
            d_r = pool_back_step(ids, de_ref[b], vec_ref[6:7], dx[at])
            dx[at] = d_r
            low = d_r.astype(BF)
            d_f[at] = low
            small_out[5:6] += jnp.sum(low.astype(F32), axis=0, keepdims=True)

    tick(now)

    @pl.when(step < outer)
    def _():
        at = pl.ds(pl.multiple_of(step * CHUNK, CHUNK), CHUNK)
        g_outer[at] = t_dot(act_ref[...], d_f[...]).astype(BF)

    @pl.when(step == outer)
    def _():
        load_h.wait()

    @pl.when((step >= outer) & (step < before))
    def _():
        for b in range(batch):
            at = slice(b * length, (b + 1) * length)
            low = (dot_t(d_f[at], wo_ref[...]) * slope_ref[at].astype(F32)).astype(BF)
            d_u[at] = low
            small_out[pl.ds(9 + p, 1)] += jnp.sum(low.astype(F32), axis=0, keepdims=True)
            dx[at] += dot_t(low, wi_ref[...])
        tick(now + 1)
        at = pl.ds(pl.multiple_of(p * width, width), width)
        g_inner[:, at] = t_dot(hx[...], d_u[...]).astype(BF)

    @pl.when(step == before - 1)
    def _():
        load_x.start()
        load_r1.wait()
        for b in range(batch):
            at = slice(b * length, (b + 1) * length)
            d_h = dx[at]
            xhat, scale = normalize(g_total[at])
            d_r = norm_back(d_h, vec_ref[3:4], xhat, scale)
            dx[at] = d_r
            low = d_r.astype(BF)
            d_a[at] = low
            d_o[at] = dot_t(low, wa_ref[...]).astype(BF)
            small_out[2:3] += jnp.sum(low.astype(F32), axis=0, keepdims=True)
            small_out[3:4] += jnp.sum(d_h * xhat, axis=0, keepdims=True)
            small_out[4:5] += jnp.sum(d_h, axis=0, keepdims=True)

    @pl.when(step == before)
    def _():
        load_x.wait()

    @pl.when(step >= before)
    def _():
        attend_back_step(
            u, lambda: tick(now + 1), q_ref, k_ref, v_ref, o_ref, d_o, pt_ref, hx, d_a,
            wq_ref, wk_ref, wv_ref, g_attn, g_total, dx, small_out,
        )

    @pl.when(step == pl.num_programs(0) - 1)
    def _():
        d_u[...] = dx[...].astype(BF)
        for b in range(batch):
            own_piece(b).start()

        def rest(t, carry):
            tick(t)
            for b in range(batch):
                @pl.when(t == ticks + TOKENS_AT + b * TOKENS_STEP)
                def _(b=b):
                    for i in range(1, seqs):
                        piece(i, b).start()
            for i in range(n + 1):
                @pl.when(t == ticks + SMALL_AT + i)
                def _(i=i):
                    if i > 0:
                        small_copy(i - 1).wait()
                        held = small_out if i == 1 else small_came.at[n + i - 2]
                        after = small_out if i == n else small_came.at[n + i - 1]
                        after[...] = held[...] + small_came[i - 1]
                    if i < n:
                        small_copy(i).start()
            return carry

        lax.fori_loop(ticks, last + 1, rest, 0)
        for b in range(batch):
            own_piece(b).wait()
            for i in range(1, seqs):
                piece(i, b).wait()


def attend_back_step(
    u, between, q_ref, k_ref, v_ref, o_ref, d_o, pt_ref, x_ref, da_ref, wq_ref, wk_ref, wv_ref,
    grads, g_total, dx, small_out,
):
    hd = PAIR // 2
    length = q_ref.shape[1]
    count, width = x_ref.shape
    batch = count // length
    quad, row = lax.div(u, batch), lax.rem(u, batch)
    mine = pl.ds(pl.multiple_of(row * length, length), length)
    lane = lax.broadcasted_iota(jnp.int32, (length, PAIR), 1)
    lane8 = lax.broadcasted_iota(jnp.int32, (8, PAIR), 1)
    dqs, dks, dvs = [], [], []
    for pair in range(QUAD // PAIR):
        if pair == 1:
            between()
        at = slice(pair * PAIR, (pair + 1) * PAIR)
        q, k, v, o = (ref[0, :, at] for ref in (q_ref, k_ref, v_ref, o_ref))
        do = d_o[mine, pl.ds(pl.multiple_of(quad * QUAD + pair * PAIR, PAIR), PAIR)]
        kt = k.T
        prod = o.astype(F32) * do.astype(F32)
        high = prod.astype(BF)
        low = (prod - high.astype(F32)).astype(BF)
        dk = dv = None
        dqt = []
        for h in range(2):
            here = (lane >= hd) if h else (lane < hd)
            ones = jnp.where((lane8 >= hd) if h else (lane8 < hd), 1.0, 0.0).astype(BF)
            do_h = jnp.where(here, do, 0)
            q_h = jnp.where(here, q, 0)
            mixed = (dot_t(ones, high) + dot_t(ones, low))[0:1]
            pt = pt_ref[0, 2 * pair + h]
            ds = (pt.astype(F32) * (dot_t(v, do_h) - mixed)).astype(BF)
            dv_h, dk_h = dot(pt, do_h), dot(ds, q_h)
            dv = dv_h if dv is None else dv + dv_h
            dk = dk_h if dk is None else dk + dk_h
            dqt.append(dot(kt[h * hd : (h + 1) * hd], ds))
        dqs.append((jnp.concatenate(dqt, axis=0).T * (hd ** (-0.5))).astype(BF))
        dks.append(dk.astype(BF))
        dvs.append(dv.astype(BF))
    d_all = jnp.concatenate(dqs + dks + dvs, axis=1)
    column = jnp.sum(d_all.astype(F32), axis=0, keepdims=True)
    for j in range(width // QUAD):
        @pl.when(quad == j)
        def _(j=j):
            at = slice(j * QUAD, (j + 1) * QUAD)
            small_out[0:1, at] += column[:, 0:QUAD]
            small_out[1:2, at] += column[:, 2 * QUAD :]
    weights = jnp.concatenate([wq_ref[...], wk_ref[...], wv_ref[...]], axis=1)
    d_x = dot_t(d_all, weights)
    g_all = t_dot(x_ref[mine], d_all)
    g_o = t_dot(o_ref[0], da_ref[mine])

    dx[mine] += d_x

    top, bottom = slice(0, width), slice(width, width + QUAD)

    @pl.when(row == 0)
    def _():
        g_total[top] = g_all
        g_total[bottom] = g_o

    @pl.when((row > 0) & (row < batch - 1))
    def _():
        g_total[top] += g_all
        g_total[bottom] += g_o

    @pl.when(row == batch - 1)
    def _():
        base = pl.multiple_of(quad * CHUNK, CHUNK)
        grads[pl.ds(base, width)] = (g_total[top] + g_all).astype(BF)
        grads[pl.ds(pl.multiple_of(base + width, QUAD), QUAD)] = (g_total[bottom] + g_o).astype(BF)


def back(r2, r1, de, vectors, ids, loss, act, slope, wo, wi, hidden, wa, q, k, v, o, pt, x, wq, wk, wv,
         devices, rows, seqs):
    batch, length, width = q.shape
    count, ff = act.shape
    quads, outer, parts = width // QUAD, ff // CHUNK, ff // width
    n = len(bin(devices)) - 3
    before = outer + parts
    of = lambda g: jnp.maximum(g - before, 0)
    at = lambda g: jnp.clip(g - outer, 0, parts - 1)
    quad = pl.BlockSpec((1, length, QUAD), lambda g: (of(g) % batch, 0, of(g) // batch))
    cols = pl.BlockSpec((width, QUAD), lambda g: (0, of(g) // batch), pipeline_mode=pl.Buffered(WEIGHT_BUFFERS))
    heads = QUAD // (width // HEADS)
    vmem = pl.BlockSpec(memory_space=pltpu.VMEM)
    hbm = pl.BlockSpec(memory_space=pl.ANY)
    one = pl.Buffered(1)
    landing = []
    for dims, number in (((CHUNK, width), outer), ((width, CHUNK), outer), ((CHUNK, width), quads)):
        sizes = halves(n, dims)
        landing += [pltpu.VMEM((number,) + size, BF) for size in sizes + sizes[-1:]]
    chunks = 2 * outer + quads
    small = shape_of((-(-(9 + parts) // 8) * 8, width), F32)
    return pl.pallas_call(
        functools.partial(back_kernel, rows),
        grid=(before + quads * batch,),
        in_specs=[
            hbm, hbm, vmem, vmem, vmem, vmem,
            pl.BlockSpec((count, CHUNK), lambda g: (0, jnp.clip(g, 0, outer - 1)), pipeline_mode=one),
            pl.BlockSpec((count, width), lambda g: (0, at(g)), pipeline_mode=one),
            pl.BlockSpec((width, width), lambda g: (at(g), 0), pipeline_mode=pl.Buffered(FEED_BUFFERS)),
            pl.BlockSpec((width, width), lambda g: (0, at(g)), pipeline_mode=pl.Buffered(FEED_BUFFERS)),
            hbm, fixed((width, width)),
            quad, quad, quad, quad,
            pl.BlockSpec((1, heads, length, length), lambda g: (of(g) % batch, of(g) // batch, 0, 0)),
            hbm, cols, cols, cols,
        ],
        out_specs=[hbm] * 4 + [vmem],
        out_shape=[
            shape_of((ff, width), BF), shape_of((width, ff), BF), shape_of((quads * CHUNK, width), BF),
            shape_of((batch * seqs, length // seqs, width), BF), small,
        ],
        scratch_shapes=[
            pltpu.VMEM((ff, width), BF), pltpu.VMEM((width, ff), BF), pltpu.VMEM((quads * CHUNK, width), BF),
            pltpu.VMEM((count, width), F32), pltpu.VMEM((count, width), F32),
        ] + [pltpu.VMEM((count, width), BF)] * 4 + [
            pltpu.VMEM((count, width), BF), pltpu.VMEM((2 * n,) + small.shape, F32),
        ] + sems(2 * n, chunks) + sems(n) + sems(batch, seqs - 1)
        + [pltpu.SemaphoreType.DMA((chunks,)), pltpu.SemaphoreType.DMA((3 + batch,))] + landing,
        cost_estimate=pl.CostEstimate(
            flops=count * width * (16 * length + 16 * width), bytes_accessed=4 * count * (4 * width + HEADS * length),
            transcendentals=0,
        ),
        compiler_params=pltpu.CompilerParams(
            vmem_limit_bytes=63 << 20, collective_id=2, has_side_effects=True
        ),
    )(r2, r1, de, vectors, ids, loss, act, slope, wo, wi, hidden, wa, q, k, v, o, pt, x, wq, wk, wv)


RING = 4


def widen_kernel(outer_in, inner_in, attn_in, token_in, outer, inner, g_q, g_k, g_v, g_o, g_tok, read, wide, r_sem, w_sem):
    width, ff = inner.shape
    jobs = []
    for i in range(ff // width):
        at = slice(i * width, (i + 1) * width)
        jobs.append((outer_in.at[at], [(slice(0, width), slice(0, width), outer.at[at])]))
    for i in range(ff // width):
        at = slice(i * width, (i + 1) * width)
        jobs.append((inner_in.at[:, at], [(slice(0, width), slice(0, width), inner.at[:, at])]))
    for j in range(width // QUAD):
        at = slice(j * QUAD, (j + 1) * QUAD)
        parts = [
            (slice(0, width), slice(m * QUAD, (m + 1) * QUAD), g.at[:, at]) for m, g in enumerate((g_q, g_k, g_v))
        ]
        parts.append((slice(width, CHUNK), slice(0, width), g_o.at[at]))
        jobs.append((attn_in.at[j * CHUNK : (j + 1) * CHUNK], parts))

    for at in range(0, g_tok.shape[0], CHUNK):
        at = slice(at, at + CHUNK)
        jobs.append((token_in.at[at], [(slice(0, CHUNK), slice(0, width), g_tok.at[at])]))

    def reader(i):
        source = jobs[i][0]
        return pltpu.make_async_copy(source, read.at[i % RING, 0 : source.shape[0]], r_sem.at[i % RING])

    def writers(i):
        return [
            pltpu.make_async_copy(wide.at[i % RING, r, c], target, w_sem.at[i % RING, m])
            for m, (r, c, target) in enumerate(jobs[i][1])
        ]

    for i in range(RING - 1):
        reader(i).start()
    for i in range(len(jobs)):
        reader(i).wait()
        if i + RING - 1 < len(jobs):
            reader(i + RING - 1).start()
        if i >= RING:
            for copy in writers(i - RING):
                copy.wait()

        def cast(k, carry, i=i):
            at = pl.ds(pl.multiple_of(k * 64, 64), 64)
            wide[i % RING, at] = read[i % RING, at].astype(F32)
            return carry

        lax.fori_loop(0, jobs[i][0].shape[0] // 64, cast, 0)
        for copy in writers(i):
            copy.start()
    for i in range(len(jobs) - RING, len(jobs)):
        for copy in writers(i):
            copy.wait()


def widen(outer, inner, attn, tokens):
    ff, width = outer.shape
    hbm = pl.BlockSpec(memory_space=pl.ANY)
    square = shape_of((width, width), F32)
    return pl.pallas_call(
        widen_kernel,
        in_specs=[hbm] * 4,
        out_specs=[hbm] * 7,
        out_shape=[shape_of((ff, width), F32), shape_of((width, ff), F32)] + [square] * 4
        + [shape_of(tokens.shape, F32)],
        scratch_shapes=[
            pltpu.VMEM((RING, CHUNK, width), BF), pltpu.VMEM((RING, CHUNK, width), F32),
            pltpu.SemaphoreType.DMA((RING,)), pltpu.SemaphoreType.DMA((RING, 4)),
        ],
        compiler_params=pltpu.CompilerParams(vmem_limit_bytes=62 << 20),
    )(outer, inner, attn, tokens)


def local(
    tokens,
    query_weight,
    query_bias,
    key_weight,
    value_weight,
    value_bias,
    output_weight,
    output_bias,
    attn_gain,
    attn_shift,
    inner_weight,
    inner_bias,
    outer_weight,
    outer_bias,
    ffn_gain,
    ffn_shift,
    segment_ids,
    positives,
):
    group_rows, local_len, width = tokens.shape
    ff = inner_weight.shape[1]
    seqs = lax.axis_size("seq")
    batch, length = group_rows // seqs, local_len * seqs
    count = batch * length
    own_segs = batch * SEG_ROW
    rows = lax.axis_size("rows")
    devices = rows * seqs
    flat2 = lambda a: a.reshape(count, a.shape[-1])
    lines = [query_bias, value_bias, output_bias, attn_gain, attn_shift, outer_bias, ffn_gain, ffn_shift]
    lines += [inner_bias[i * width : (i + 1) * width] for i in range(ff // width)]
    place = lax.broadcasted_iota(jnp.int32, (-(-len(lines) // 8) * 8, width), 0)
    vectors = jnp.zeros(place.shape, BF)
    for i, line in enumerate(lines):
        vectors = jnp.where(place == i, line[None, :], vectors)
    vectors = vectors.astype(F32)

    q, k, v, o, pt, r_one, x = attend(
        tokens, query_weight, key_weight, value_weight, output_weight, vectors, segment_ids, seqs
    )
    hidden, active, slope, r_two, xpool = feed(r_one, vectors, inner_weight, outer_weight, segment_ids)
    d_e, loss_vec = contrast(
        xpool.reshape(own_segs, width), vectors, segment_ids, positives, devices, rows
    )
    *sums, grad_tokens, small = back(
        flat2(r_two), flat2(r_one), d_e.reshape(batch, SEG_ROW, width), vectors, segment_ids, loss_vec,
        flat2(active), flat2(slope), outer_weight, inner_weight, flat2(hidden), output_weight,
        q, k, v, o, pt, flat2(x), query_weight, key_weight, value_weight, devices, rows, seqs,
    )
    g_outer, g_inner, g_query, g_key, g_value, g_output, g_tokens = widen(
        *sums, grad_tokens.reshape(count, width)
    )
    return (
        small[8, 0] / (own_segs * devices),
        g_tokens.reshape(tokens.shape),
        g_query,
        small[0],
        g_key,
        g_value,
        small[1],
        g_output,
        small[2],
        small[3],
        small[4],
        g_inner,
        small[9 : 9 + ff // width].reshape(-1),
        g_outer,
        small[5],
        small[6],
        small[7],
    )


def solution(mesh):
    placed = (
        (P("rows", "seq", None),) + (P(),) * 15 + (P("rows", None), P("rows"))
    )
    return jax.shard_map(
        local,
        mesh=mesh,
        in_specs=placed,
        out_specs=(P(), P("rows", "seq", None)) + (P(),) * 15,
        check_vma=False,
    )
```
